32 devices in a mesh: fsdp: 8 (over z, x), ctx: 4 (over y, core).
Axes of the slice: x: 2, y: 2, z: 4, core: 2. Of those that a mesh axis runs over, the one named last changes fastest.
Arguments:
- hidden_in: bfloat16 [16, 256, 1536], P('fsdp', 'ctx'), may hold values from -6 to 6
- lengths: int32 [16], P('fsdp'), may hold values from 64 to 256, as said below
- span_order: int32 [8], replicated, may hold values from 0 to 7, as said below
- attn_gain: bfloat16 [1536], P(('fsdp', 'ctx')), may hold values from 0.25 to 1.75
- w_query: bfloat16 [1536, 1536], P(('fsdp', 'ctx')), may hold values from -0.21875 to 0.21875
- w_key: bfloat16 [1536, 768], P(('fsdp', 'ctx')), may hold values from -0.21875 to 0.21875
- w_value: bfloat16 [1536, 768], P(('fsdp', 'ctx')), may hold values from -0.15625 to 0.15625
- w_out: bfloat16 [1536, 1536], P(('fsdp', 'ctx')), may hold values from -0.625 to 0.625
- mlp_gain: bfloat16 [1536], P(('fsdp', 'ctx')), may hold values from 0.25 to 1.75
- w_gate: bfloat16 [1536, 4096], P(('fsdp', 'ctx')), may hold values from -0.15625 to 0.15625
- w_up: bfloat16 [1536, 4096], P(('fsdp', 'ctx')), may hold values from -0.15625 to 0.15625
- w_down: bfloat16 [4096, 1536], P(('fsdp', 'ctx')), may hold values from -0.09375 to 0.09375
- out_grad: bfloat16 [16, 256, 1536], P('fsdp', 'ctx'), may hold values from -6 to 6
Outputs:
- block_out: bfloat16 [16, 256, 1536], P('fsdp', 'ctx')
- grad_in: bfloat16 [16, 256, 1536], P('fsdp', 'ctx')
- grad_attn_gain: float32 [1536], P(('fsdp', 'ctx'))
- grad_query: float32 [1536, 1536], P(('fsdp', 'ctx'))
- grad_key: float32 [1536, 768], P(('fsdp', 'ctx'))
- grad_value: float32 [1536, 768], P(('fsdp', 'ctx'))
- grad_out: float32 [1536, 1536], P(('fsdp', 'ctx'))
- grad_mlp_gain: float32 [1536], P(('fsdp', 'ctx'))
- grad_gate: float32 [1536, 4096], P(('fsdp', 'ctx'))
- grad_up: float32 [1536, 4096], P(('fsdp', 'ctx'))
- grad_down: float32 [4096, 1536], P(('fsdp', 'ctx'))
The draws below stay inside these ranges and needn't reach their ends.
Inputs may be any that keep to these rules, and one draw needn't show every extreme that they name: `lengths`: of the 2 sequences of each fsdp index, one chosen at random has length 256. `span_order`: paired spans: for each index d of ctx, the stored spans 2 d and 2 d + 1 hold the spans c and 7 - c of the sequence, for some c below 4, each c once; each span has 32 slots.
All inputs are finite; a program needn't handle non-finite values.
Results may differ from the reference program's by a relative error of at most 0.02.
Values may be sent and summed in bfloat16 or wider, within the bound.
No kernel may reach another device: no remote copies, remote signals or barrier semaphores. Data moves between devices by JAX's collectives and lax.ppermute only.
A program may use at most 192 MiB of HBM per device.

```python
import jax
import jax.numpy as jnp
from jax import lax

D = 1536
H = 16
KV = 8
HD = 96
FF = 4096
MICRO = 2
LENGTH = 256
SPAN = 32
SEQS = 16
N_CTX = 4


def draw_lengths(key, part):
    key = jax.random.fold_in(key, 11)
    first_key, second_key = jax.random.split(key)
    drawn_lengths = jax.random.randint(first_key, (SEQS,), LENGTH // 4, LENGTH + 1, dtype=jnp.int32)
    chosen_slot = jax.random.randint(second_key, (SEQS // MICRO,), 0, MICRO, dtype=jnp.int32)
    sequence_index = jnp.arange(SEQS, dtype=jnp.int32)
    longest = sequence_index % MICRO == jnp.repeat(chosen_slot, MICRO)
    return jnp.where(longest, LENGTH, drawn_lengths).astype(jnp.int32)


def draw_span_order(key, part):
    key = jax.random.fold_in(key, 23)
    shuffled = jax.random.permutation(key, N_CTX).astype(jnp.int32)
    mirrored = (2 * N_CTX - 1 - shuffled).astype(jnp.int32)
    return jnp.stack([shuffled, mirrored], axis=1).reshape(2 * N_CTX).astype(jnp.int32)


def raised(entries, rng, source, target, parts, factor):
    def block_of(dim):
        return (jnp.arange(entries.shape[dim]) // (entries.shape[dim] // parts)).reshape((-1,) + (1,) * (entries.ndim - 1 - dim))

    one_side = jax.random.permutation(rng, parts)[block_of(target)]
    other_side = (block_of(target) + parts // 2) % parts
    return jnp.where((block_of(source) == one_side) | (block_of(source) == other_side), factor * entries, entries)


def block_scale(stream_key, extent, cuts, low, high):
    level = 1.0
    for dim, parts in cuts:
        steps = jax.random.uniform(jax.random.fold_in(jax.random.fold_in(stream_key, 6), dim), (parts,), jnp.float32, low / len(cuts), high / len(cuts))
        level = level * jnp.repeat(jnp.exp(steps), extent[dim] // parts).reshape((-1,) + (1,) * (len(extent) - 1 - dim))
    return level


def centred(stream_key, extent, width, most, pieces=(), kind=jnp.bfloat16):
    factor_of = block_scale(stream_key, extent, pieces, -0.22, 0.18) if pieces else 1.0
    entries = jax.random.normal(stream_key, extent, jnp.float32) * width * factor_of
    return jnp.minimum(jnp.maximum(entries, -most), most).astype(kind)


def heavy_noise(key, extent, spread, limit, cuts, heavy, kind=jnp.bfloat16):
    drawn = spread * jax.random.normal(key, extent, jnp.float32)
    if cuts:
        drawn = drawn * block_scale(key, extent, cuts, -0.22, 0.18)
    return jnp.clip(raised(drawn, jax.random.fold_in(key, 3), *heavy), -limit, limit).astype(kind)


def setup_inputs(seed: int = 0) -> dict:
    splits = jax.random.split(jax.random.key(seed), 14)
    return {
        "hidden_in": centred(splits[0], (SEQS, LENGTH, D), 1.0, 6.0, ((0, 8), (1, 4))),
        "lengths": draw_lengths(jax.random.fold_in(splits[13], 71), 0),
        "span_order": draw_span_order(jax.random.fold_in(splits[13], 71), 0),
        "attn_gain": jnp.clip(1.0 + 0.15 * jax.random.normal(splits[3], (D,), jnp.float32), 0.25, 1.75).astype(jnp.bfloat16),
        "w_query": centred(splits[4], (D, H * HD), (D // 2) ** -0.5, 0.21875, ((0, 32),)),
        "w_key": centred(splits[5], (D, KV * HD), (D // 2) ** -0.5, 0.21875, ((0, 32),)),
        "w_value": centred(splits[6], (D, KV * HD), D ** -0.5, 0.15625, ((0, 32),)),
        "w_out": centred(splits[7], (H * HD, D), HD ** -0.5, 0.625, ((0, 32),)),
        "mlp_gain": jnp.clip(1.0 + 0.15 * jax.random.normal(splits[8], (D,), jnp.float32), 0.25, 1.75).astype(jnp.bfloat16),
        "w_gate": centred(splits[9], (D, FF), D ** -0.5, 0.15625, ((0, 32),)),
        "w_up": centred(splits[10], (D, FF), D ** -0.5, 0.15625, ((0, 32),)),
        "w_down": centred(splits[11], (FF, D), FF ** -0.5, 0.09375, ((0, 32),)),
        "out_grad": heavy_noise(splits[12], (SEQS, LENGTH, D), 1.0, 6.0, ((0, 8), (1, 4)), (0, 2, 8, 2.0)),
    }


@jax.custom_vjp
def low(v):
    return lax.optimization_barrier(v.astype(jnp.bfloat16)).astype(jnp.float32)

@jax.custom_vjp
def low_back(v):
    return v

def low_keep(v):
    return (low(v), None)

def low_pass(kept, grad):
    return (grad,)

def back_keep(v):
    return (v, None)

def back_low(kept, grad):
    return (low(grad),)
low.defvjp(low_keep, low_pass)
low_back.defvjp(back_keep, back_low)
epsilon = 1e-05
rope_base = 100000.0
masked_score = -1e+30

def matmul(left, right):
    return jnp.dot(left, right, precision=lax.Precision.HIGHEST)

def rms_norm(values, gain):
    return values * lax.rsqrt(lax.optimization_barrier(jnp.mean(values * values, axis=-1, keepdims=True)) + epsilon) * gain

def rotary(values, cosines, sines):
    half_dim = values.shape[-1] // 2
    former = values[..., :half_dim]
    latter = values[..., half_dim:]
    return jnp.concatenate([former * cosines - latter * sines, latter * cosines + former * sines], axis=-1)

def block_layer(inputs, usable, positions, cosines, sines, params):
    attn_gain, w_query, w_key, w_value, w_out, mlp_gain, w_gate, w_up, w_down = params
    groups = H // KV
    normed = low(rms_norm(inputs, attn_gain))
    query_pre = low_back(matmul(normed, w_query)).reshape(LENGTH, H, HD)
    key_pre = low_back(matmul(normed, w_key)).reshape(LENGTH, KV, HD)
    values = low(low_back(matmul(normed, w_value))).reshape(LENGTH, KV, HD)
    queries = low(rotary(query_pre, cosines, sines))
    keys = low(rotary(key_pre, cosines, sines))
    block_rows = min(512, LENGTH)
    blocks = LENGTH // block_rows
    score_scale = HD ** (-0.5)

    def attend_block(element):
        query_block, query_pos = element
        grouped = query_block.reshape(block_rows, KV, groups, HD)
        scores = jnp.einsum('qkgd,skd->kgqs', grouped, keys, precision=lax.Precision.HIGHEST)
        scores = low_back(scores * score_scale)
        allowed = (positions[None, :] <= query_pos[:, None]) & (usable[None, :] > 0)
        scores = jnp.where(allowed[None, None], scores, masked_score)
        weights = jax.nn.softmax(scores, axis=-1)
        mixture = jnp.einsum('kgqs,skd->qkgd', low(weights), values, precision=lax.Precision.HIGHEST)
        return mixture.reshape(block_rows, H * HD)
    attended = lax.map(jax.checkpoint(attend_block), (queries.reshape(blocks, block_rows, H, HD), positions.reshape(blocks, block_rows)))
    attended = low_back(attended.reshape(LENGTH, H * HD))
    attn_branch = low_back(matmul(low(attended), w_out))
    residual = inputs + attn_branch
    normed_mlp = low(rms_norm(residual, mlp_gain))
    gate_act = low_back(matmul(normed_mlp, w_gate))
    upward = low_back(matmul(normed_mlp, w_up))
    hidden = low(jax.nn.silu(gate_act) * upward)
    mlp_branch = low_back(matmul(hidden, w_down))
    return usable[:, None] * (residual + mlp_branch)

def reference(hidden_in, lengths, span_order, attn_gain, w_query, w_key, w_value, w_out, mlp_gain, w_gate, w_up, w_down, out_grad):
    params = tuple((weight.astype(jnp.float32) for weight in (attn_gain, w_query, w_key, w_value, w_out, mlp_gain, w_gate, w_up, w_down)))
    slot_index = jnp.arange(LENGTH, dtype=jnp.int32)
    positions = (span_order[slot_index // SPAN] * SPAN + slot_index % SPAN).astype(jnp.int32)
    frequency = rope_base ** (-2.0 * jnp.arange(HD // 2, dtype=jnp.float32) / HD)
    angles = positions.astype(jnp.float32)[:, None] * frequency[None, :]
    cosines = jnp.cos(angles)[:, None, :]
    sines = jnp.sin(angles)[:, None, :]

    def per_sequence(running, element):
        inputs, length, cotangent = element
        usable = (positions < length).astype(jnp.float32)

        def forward(values, weights):
            return block_layer(values, usable, positions, cosines, sines, weights)
        result, pullback = jax.vjp(forward, inputs.astype(jnp.float32), params)
        grad_inputs, grad_params = pullback(cotangent.astype(jnp.float32))
        running = tuple((before + summand for before, summand in zip(running, grad_params)))
        return (running, (result.astype(jnp.bfloat16), grad_inputs.astype(jnp.bfloat16)))
    initial = tuple((jnp.zeros_like(weight) for weight in params))
    running, (block_out, grad_in) = lax.scan(per_sequence, initial, (hidden_in, lengths, out_grad))
    return (block_out, grad_in, running[0], running[1], running[2], running[3], running[4], running[5], running[6], running[7], running[8])
```

```python
import jax
import jax.numpy as jnp
from jax import lax
from jax.sharding import PartitionSpec as P

H = 16
KV = 8
HD = 96
GROUP = H // KV
AXES = ("fsdp", "ctx")

epsilon = 1e-05
rope_base = 100000.0
masked_score = -1e30
BF = jnp.bfloat16
F32 = jnp.float32


def mm(left, right):
    return jnp.dot(left, right, preferred_element_type=F32)


def mm_lt(left, right):
    return lax.dot_general(left, right, (((0,), (0,)), ((), ())), preferred_element_type=F32)


def mm_rt(left, right):
    return lax.dot_general(left, right, (((1,), (1,)), ((), ())), preferred_element_type=F32)


class Plan:
    def __init__(self):
        self.ctx = lax.axis_size("ctx")
        self.fsdp = lax.axis_size("fsdp")
        self.tpf = KV // self.ctx
        self.nz = self.fsdp // self.tpf
        self.total = self.fsdp * self.ctx
        self.fast = self.ctx == 4 and self.tpf == 2 and self.nz == 4
        self.f = lax.axis_index("fsdp")
        self.c = lax.axis_index("ctx")
        self.z = self.f // self.tpf
        self.j = (self.f % self.tpf) * self.ctx + self.c

    def flip(self, bit):
        return [(d, d ^ bit) for d in range(self.total)]

    def send(self, x, pairs):
        return lax.ppermute(x, AXES, pairs)

    def planes(self, pairs):
        return [(s * KV + i, d * KV + i) for s, d in pairs for i in range(KV)]

    def scatter_columns(self, x):
        if self.tpf == 1:
            return lax.all_to_all(x, "ctx", split_axis=0, concat_axis=0, tiled=True)
        groups = [[z * KV + i for i in range(KV)] for z in range(self.nz)]
        return lax.all_to_all(
            x, AXES, split_axis=0, concat_axis=0, tiled=True, axis_index_groups=groups
        )

    def gather_tokens(self, x):
        if not self.fast:
            return lax.all_gather(x, "ctx", axis=1, tiled=True)
        a, b = x[0], x[1]
        slots, width = a.shape
        ax = jnp.stack([a, self.send(a, self.flip(4))], axis=0)
        by = jnp.stack([b, self.send(b, self.flip(2))], axis=0)
        axy = jnp.stack([ax, self.send(ax, self.flip(2))], axis=1)
        bxy = jnp.stack([by, self.send(by, self.flip(4))], axis=0)
        both = jnp.stack([axy, bxy], axis=0)
        other = self.send(both, self.flip(1))
        return jnp.stack([both, other], axis=2).reshape(4, 4 * slots, width)

    def scatter_tokens(self, x, slots):
        if not self.fast:
            return lax.psum_scatter(x, "ctx", scatter_dimension=1, tiled=True).astype(F32)
        width = x.shape[-1]
        x = x.reshape(2, 2, 2, 2, slots, width)
        got = self.send(x[:, :, 1], self.flip(1))
        x = (x[:, :, 0].astype(F32) + got.astype(F32)).astype(BF)
        a, b = x[0], x[1]
        got_a = self.send(a[:, 1], self.flip(2))
        got_b = self.send(b[1], self.flip(4))
        a = (a[:, 0].astype(F32) + got_a.astype(F32)).astype(BF)
        b = (b[0].astype(F32) + got_b.astype(F32)).astype(BF)
        got_a = self.send(a[1], self.flip(4))
        got_b = self.send(b[1], self.flip(2))
        a = a[0].astype(F32) + got_a.astype(F32)
        b = b[0].astype(F32) + got_b.astype(F32)
        return jnp.stack([a, b])

    def gather_planes(self, x):
        if not self.fast:
            full = lax.all_gather(x, "fsdp", axis=0, tiled=False)
            return [full[k] for k in range(self.nz)]
        pairs = self.planes([(0, 1), (1, 0), (2, 3), (3, 2)])
        inner = self.planes([(1, 2), (2, 1)])
        outer = self.planes([(1, 0), (2, 3)])
        p1 = self.send(x, pairs)
        p2 = self.send(x, inner)
        p3 = self.send(p2, outer)
        p4 = self.send(p1, inner)
        p5 = self.send(p4, outer)
        return [x, p1, p2 + p3, p4 + p5]

    def scatter_planes(self, pieces):
        if not self.fast:
            full = jnp.stack(pieces).astype(BF)
            return lax.psum_scatter(full, "fsdp", scatter_dimension=0, tiled=False).astype(F32)
        pairs = self.planes([(0, 1), (1, 0), (2, 3), (3, 2)])
        inner = self.planes([(1, 2), (2, 1)])
        inward = self.planes([(0, 1), (3, 2)])
        own, s1, sb, sc = pieces
        r5 = self.send(sc.astype(BF), inward)
        r3 = self.send(sb.astype(BF), inward)
        r4 = self.send((sc.astype(F32) + r5.astype(F32)).astype(BF), inner)
        r2 = self.send((sb.astype(F32) + r3.astype(F32)).astype(BF), inner)
        r1 = self.send((s1.astype(F32) + r4.astype(F32)).astype(BF), pairs)
        return own.astype(F32) + r1.astype(F32) + r2.astype(F32)

    def order(self):
        if not self.fast:
            return [jnp.int32(k) for k in range(self.nz)]
        z = self.z
        low = z < 2
        return [z, z ^ 1, jnp.where(low, 2, 1), jnp.where(low, 3, 0)]

    def slot_of(self):
        if not self.fast:
            return [jnp.int32(k) for k in range(self.nz)]
        z = self.z
        slots = []
        table = ((0, 1, 3, 3), (1, 0, 2, 2), (2, 2, 0, 1), (3, 3, 1, 0))
        for k in range(4):
            row = table[k]
            slots.append(
                jnp.where(z == 0, row[0], jnp.where(z == 1, row[1], jnp.where(z == 2, row[2], row[3])))
            )
        return slots

    def permute_columns(self, x):
        if not self.fast:
            return x
        block = x.shape[-1] // self.nz
        return jnp.concatenate(
            [lax.dynamic_slice_in_dim(x, k * block, block, axis=-1) for k in self.order()], axis=-1
        )

    def restore_columns(self, x):
        if not self.fast:
            return x
        block = x.shape[-1] // self.nz
        return jnp.concatenate(
            [lax.dynamic_slice_in_dim(x, k * block, block, axis=-1) for k in self.slot_of()], axis=-1
        )

    def restore_rows(self, pieces):
        full = jnp.stack(pieces)
        if not self.fast:
            return full.reshape((-1,) + full.shape[2:])
        return jnp.concatenate(
            [lax.dynamic_index_in_dim(full, k, axis=0, keepdims=False) for k in self.slot_of()], axis=0
        )

    def rows_to_pieces(self, x):
        rows = x.shape[0] // self.nz
        full = x.reshape((self.nz, rows) + x.shape[1:])
        return [lax.dynamic_index_in_dim(full, k, axis=0, keepdims=False) for k in self.order()]


def local(
    hidden_in,
    lengths,
    span_order,
    attn_gain,
    w_query,
    w_key,
    w_value,
    w_out,
    mlp_gain,
    w_gate,
    w_up,
    w_down,
    out_grad,
):
    plan = Plan()
    micro, slots, width = hidden_in.shape
    span_len = slots // 2
    nz = plan.nz
    qw, kw = GROUP * HD, HD
    rows = w_query.shape[0]
    hid = w_gate.shape[1] // plan.total

    def positions_of(index):
        at = jnp.arange(slots, dtype=jnp.int32)
        pair = lax.dynamic_slice_in_dim(span_order, 2 * index, 2)
        return jnp.where(at < span_len, pair[0], pair[1]) * span_len + at % span_len

    local_pos = positions_of(plan.c)
    if plan.fast:
        pos = jnp.concatenate([positions_of(plan.c ^ k) for k in (0, 2, 1, 3)])
        theirs = plan.send(lengths, plan.flip(4))
        seq_len = jnp.stack([lengths[0], theirs[0], lengths[1], theirs[1]])
    else:
        pos = jnp.concatenate([positions_of(k) for k in range(plan.ctx)])
        seq_len = lengths
    usable = (local_pos[None, :] < lengths[:, None]).astype(F32)[..., None]
    frequency = rope_base ** (-2.0 * jnp.arange(HD // 2, dtype=F32) / HD)
    angles = pos.astype(F32)[:, None] * frequency[None, :]
    cosines, sines = jnp.cos(angles), jnp.sin(angles)

    gain = attn_gain.astype(F32)[:, None]
    gain_m = mlp_gain.astype(F32)[:, None]
    qkv = jnp.concatenate(
        [
            (w_query.astype(F32) * gain).reshape(rows, KV, qw),
            (w_key.astype(F32) * gain).reshape(rows, KV, kw),
            (w_value.astype(F32) * gain).reshape(rows, KV, kw),
        ],
        axis=2,
    ).astype(BF)
    qkv = plan.scatter_columns(jnp.transpose(qkv, (1, 0, 2))).reshape(KV * rows, qw + 2 * kw)

    def columns(w):
        w = (w.astype(F32) * gain_m).astype(BF).reshape(rows, nz, KV, hid)
        w = jnp.transpose(w, (2, 0, 1, 3)).reshape(KV, rows, nz * hid)
        return plan.scatter_columns(w).reshape(KV * rows, nz * hid)

    place = [(b, (b % nz) * KV + b // nz) for b in range(plan.total)]
    out_piece = plan.send(w_out, place)

    wqkv = jnp.concatenate(plan.gather_planes(qkv), axis=0)
    wout = plan.restore_rows(plan.gather_planes(out_piece))
    wgate = jnp.concatenate(plan.gather_planes(columns(w_gate)), axis=0)
    wup = jnp.concatenate(plan.gather_planes(columns(w_up)), axis=0)
    wdown = plan.restore_rows(plan.gather_planes(w_down))

    source = hidden_in.astype(F32)
    inverse_attn = lax.rsqrt(jnp.mean(source * source, axis=-1, keepdims=True) + epsilon)
    unit = source * inverse_attn
    xs = plan.gather_tokens(plan.permute_columns(unit.astype(BF)))
    seqs, length = xs.shape[0], xs.shape[1]
    tokens = seqs * length
    xs = xs.reshape(tokens, width)
    g_res = out_grad.astype(F32) * usable
    g_mlp = plan.gather_tokens(g_res.astype(BF)).reshape(tokens, width)

    pre = mm(xs, wqkv).reshape(seqs, length, qw + 2 * kw)

    def rotate(v, s):
        half = HD // 2
        co, si = cosines[None, :, None, :], s[None, :, None, :]
        one, two = v[..., :half], v[..., half:]
        return jnp.concatenate([one * co - two * si, two * co + one * si], axis=-1)

    q = rotate(pre[..., :qw].reshape(seqs, length, GROUP, HD), sines).astype(BF)
    k = rotate(pre[..., qw : qw + kw].reshape(seqs, length, 1, HD), sines)[:, :, 0].astype(BF)
    v = pre[..., qw + kw :].astype(BF)
    scale = HD ** (-0.5)
    allowed = (pos[None, None, :] <= pos[None, :, None]) & (
        pos[None, None, :] < seq_len[:, None, None]
    )
    scores = jnp.einsum("sqgd,snd->sgqn", q, k, preferred_element_type=F32) * scale
    scores = jnp.where(allowed[:, None], scores, masked_score)
    top = jnp.max(scores, axis=-1, keepdims=True)
    expo = jnp.exp(scores - top)
    probs = expo / jnp.sum(expo, axis=-1, keepdims=True)
    low = probs.astype(BF)
    attended = jnp.einsum("sgqn,snd->sqgd", low, v, preferred_element_type=F32)
    attended = attended.astype(BF).reshape(tokens, qw)
    branch = mm(attended, wout).astype(BF).reshape(seqs, length, width)
    residual = source + plan.scatter_tokens(branch, slots)

    inverse_mlp = lax.rsqrt(jnp.mean(residual * residual, axis=-1, keepdims=True) + epsilon)
    unit_m = residual * inverse_mlp
    xm = plan.gather_tokens(plan.permute_columns(unit_m.astype(BF))).reshape(tokens, width)
    gate = mm(xm, wgate)
    up = mm(xm, wup)
    sig = jax.nn.sigmoid(gate)
    hidden = (gate * sig * up).astype(BF)
    g_down = mm_lt(hidden, g_mlp)
    g_down = plan.scatter_planes(plan.rows_to_pieces(g_down.astype(BF)))
    down = mm(hidden, wdown).astype(BF).reshape(seqs, length, width)
    block_out = (usable * (residual + plan.scatter_tokens(down, slots))).astype(BF)

    g_hidden = mm_rt(g_mlp, wdown)
    g_gate = (g_hidden * up * sig * (1.0 + gate * (1.0 - sig))).astype(BF)
    g_up = (g_hidden * gate * sig).astype(BF)
    g_nm = (mm_rt(g_gate, wgate) + mm_rt(g_up, wup)).astype(BF).reshape(seqs, length, width)

    def split_rows(x):
        return list(x.astype(BF).reshape(nz, x.shape[0] // nz, x.shape[1]))

    u_gate = plan.scatter_planes(split_rows(mm_lt(xm, g_gate)))
    u_up = plan.scatter_planes(split_rows(mm_lt(xm, g_up)))

    def norm_back(scaled, unit, inverse):
        return inverse * (scaled - unit * jnp.mean(scaled * unit, axis=-1, keepdims=True))

    scaled_m = plan.restore_columns(plan.scatter_tokens(g_nm, slots))
    g_res2 = g_res + norm_back(scaled_m, unit_m, inverse_mlp)

    g_branch = plan.gather_tokens(g_res2.astype(BF)).reshape(tokens, width)
    u_out = mm_lt(attended, g_branch)
    u_out = plan.scatter_planes(plan.rows_to_pieces(u_out.astype(BF)))
    g_att = mm_rt(g_branch, wout).astype(BF).reshape(seqs, length, GROUP, HD)
    g_probs = jnp.einsum("sqgd,snd->sgqn", g_att, v, preferred_element_type=F32)
    inner = jnp.sum(probs * g_probs, axis=-1, keepdims=True)
    g_scores = (probs * (g_probs - inner)).astype(BF)
    g_q = jnp.einsum("sgqn,snd->sqgd", g_scores, k, preferred_element_type=F32) * scale
    g_k = jnp.einsum("sgqn,sqgd->snd", g_scores, q, preferred_element_type=F32) * scale
    g_v = jnp.einsum("sgqn,sqgd->snd", low, g_att, preferred_element_type=F32)
    g_pre = jnp.concatenate(
        [
            rotate(g_q, -sines).astype(BF).reshape(seqs, length, qw),
            rotate(g_k[:, :, None], -sines).astype(BF)[:, :, 0],
            g_v.astype(BF),
        ],
        axis=-1,
    ).reshape(tokens, qw + 2 * kw)
    u_qkv = plan.scatter_planes(split_rows(mm_lt(xs, g_pre)))
    g_na = mm_rt(g_pre, wqkv).astype(BF).reshape(seqs, length, width)
    scaled = plan.restore_columns(plan.scatter_tokens(g_na, slots))
    grad_in = (g_res2 + norm_back(scaled, unit, inverse_attn)).astype(BF)

    back = [(d, s) for s, d in place]
    grad_out = plan.send(u_out.astype(BF), back).astype(F32)
    u = plan.scatter_columns(u_qkv.astype(BF).reshape(KV, rows, qw + 2 * kw))
    u = jnp.transpose(u, (1, 0, 2)).astype(F32)
    u_q = u[..., :qw].reshape(rows, KV * qw)
    u_k = u[..., qw : qw + kw].reshape(rows, KV * kw)
    u_v = u[..., qw + kw :].reshape(rows, KV * kw)

    def columns_back(x):
        x = plan.scatter_columns(x.astype(BF).reshape(KV, rows, nz * hid))
        x = jnp.transpose(x.reshape(KV, rows, nz, hid), (1, 2, 0, 3))
        return x.reshape(rows, KV * nz * hid).astype(F32)

    u_gate, u_up = columns_back(u_gate), columns_back(u_up)

    def paired(*items):
        return sum(jnp.sum(w.astype(F32) * g, axis=1) for w, g in items)

    grad_attn_gain = paired((w_query, u_q), (w_key, u_k), (w_value, u_v))
    grad_mlp_gain = paired((w_gate, u_gate), (w_up, u_up))
    return (
        block_out,
        grad_in,
        grad_attn_gain,
        u_q * gain,
        u_k * gain,
        u_v * gain,
        grad_out,
        grad_mlp_gain,
        u_gate * gain_m,
        u_up * gain_m,
        g_down,
    )


def solution(mesh):
    rows = P(AXES, None)
    tokens = P("fsdp", "ctx", None)
    return jax.shard_map(
        local,
        mesh=mesh,
        in_specs=(tokens, P("fsdp"), P(), P(AXES), rows, rows, rows, rows, P(AXES), rows, rows, rows, tokens),
        out_specs=(tokens, tokens, P(AXES), rows, rows, rows, rows, P(AXES), rows, rows, rows),
        check_vma=False,
    )
```

```python
import jax
import jax.numpy as jnp
from jax import lax
from jax.experimental import pallas as pl
from jax.experimental.pallas import tpu as pltpu
from jax.sharding import PartitionSpec as P

H = 16
KV = 8
HD = 96
GROUP = H // KV
QW = GROUP * HD
AXES = ("fsdp", "ctx")

epsilon = 1e-05
rope_base = 100000.0
masked_score = -1e30
scale = HD ** (-0.5)
BF = jnp.bfloat16
F32 = jnp.float32


def mm(left, right):
    return jnp.dot(left, right, preferred_element_type=F32)


def mm_lt(left, right):
    return lax.dot_general(left, right, (((0,), (0,)), ((), ())), preferred_element_type=F32)


def mm_rt(left, right):
    return lax.dot_general(left, right, (((1,), (1,)), ((), ())), preferred_element_type=F32)


def plus(a, b):
    return (a.astype(F32) + b.astype(F32)).astype(BF)


def send(x, pairs):
    return lax.ppermute(x, AXES, pairs)


def unit_of_work(go, body, *args):
    def idle(*args):
        return jax.tree.map(lambda leaf: jnp.zeros(leaf.shape, leaf.dtype), jax.eval_shape(body, *args))

    return lax.cond(go, body, idle, *args)


def fence(*items):
    return lax.optimization_barrier(items)


class Layout:
    def __init__(self):
        self.ctx = lax.axis_size("ctx")
        self.fsdp = lax.axis_size("fsdp")
        self.tpf = KV // self.ctx
        self.nz = self.fsdp // self.tpf
        self.total = self.fsdp * self.ctx
        self.fast = self.ctx == 4 and self.tpf == 2 and self.nz == 4
        self.f = lax.axis_index("fsdp")
        self.c = lax.axis_index("ctx")
        self.z = self.f // self.tpf
        self.place = [(b, (b % self.nz) * KV + b // self.nz) for b in range(self.total)]
        self.back = [(d, s) for s, d in self.place]

    def exchange(self, x):
        if self.tpf == 1:
            return lax.all_to_all(x, "ctx", split_axis=0, concat_axis=0, tiled=True)
        groups = [[z * KV + i for i in range(KV)] for z in range(self.nz)]
        return lax.all_to_all(
            x, AXES, split_axis=0, concat_axis=0, tiled=True, axis_index_groups=groups
        )

    def lines(self):
        return [[z * KV + i for z in range(self.nz)] for i in range(KV)]

    def spread(self, x):
        if self.tpf == 1:
            return lax.all_gather(x, "fsdp", axis=0, tiled=True)
        return lax.all_gather(x, AXES, axis=0, tiled=True, axis_index_groups=self.lines())

    def gather_sum(self, x):
        x = x.astype(BF)
        if self.tpf == 1:
            return lax.psum_scatter(x, "fsdp", scatter_dimension=0, tiled=True)
        return lax.psum_scatter(
            x, AXES, scatter_dimension=0, tiled=True, axis_index_groups=self.lines()
        )


class Line(Layout):
    def __init__(self):
        super().__init__()
        total = self.total
        self.core = [(d, d ^ 1) for d in range(total)]
        self.first = [(d, d ^ (2 if d & 1 else 4)) for d in range(total)]
        self.second = [(d, d ^ (4 if d & 1 else 2)) for d in range(total)]
        self.xflip = [(d, d ^ 4) for d in range(total)]

        def planes(pairs):
            return [(s * KV + i, d * KV + i) for s, d in pairs for i in range(KV)]

        self.pair = planes([(0, 1), (1, 0), (2, 3), (3, 2)])
        self.inner = planes([(1, 2), (2, 1)])
        self.outward = planes([(1, 0), (2, 3)])
        self.inward = planes([(0, 1), (3, 2)])
        z = self.z
        low = z < 2
        self.order = [z, z ^ 1, jnp.where(low, 2, 1), jnp.where(low, 3, 0)]
        table = ((0, 1, 3, 3), (1, 0, 2, 2), (2, 2, 0, 1), (3, 3, 1, 0))
        self.slot = [
            jnp.where(z == 0, r[0], jnp.where(z == 1, r[1], jnp.where(z == 2, r[2], r[3])))
            for r in table
        ]

    def take_columns(self, x, blocks):
        width = x.shape[-1] // self.nz
        return jnp.concatenate(
            [lax.dynamic_slice_in_dim(x, k * width, width, axis=-1) for k in blocks], axis=-1
        )

    def take_rows(self, pieces):
        full = jnp.stack(pieces)
        return jnp.concatenate(
            [lax.dynamic_index_in_dim(full, k, axis=0, keepdims=False) for k in self.slot], axis=0
        )

    def to_pieces(self, x):
        full = x.reshape((self.nz, x.shape[0] // self.nz) + x.shape[1:])
        return [lax.dynamic_index_in_dim(full, k, axis=0, keepdims=False) for k in self.order]

    def all_tokens(self, x):
        x = jnp.stack([x, send(x, self.first)])
        x = jnp.stack([x, send(x, self.second)])
        x = jnp.stack([x, send(x, self.core)])
        return x.reshape(-1, x.shape[-1])

    def collect_tokens(self, x, slots):
        x = x.reshape(2, 2, 2, 2, slots, x.shape[-1])
        x = plus(x[0], send(x[1], self.core))
        x = plus(x[0], send(x[1], self.second))
        return x[0].astype(F32) + send(x[1], self.first).astype(F32)

    def to_seqs(self, x, slots):
        x = x.reshape(2, 2, 2, 2, slots, x.shape[-1])
        halves = []
        for dc in range(2):
            even = ((self.c & 1) ^ dc) == 0
            h = x[dc]
            halves.append(jnp.where(even, jnp.swapaxes(h, 0, 1), h))
        x = jnp.stack(halves, axis=0)
        x = jnp.transpose(x, (1, 3, 0, 2, 4, 5))
        return x.reshape(4, 4 * slots, x.shape[-1])

    def from_seqs(self, x, slots):
        x = x.reshape(2, 2, 2, 2, slots, x.shape[-1])
        x = jnp.transpose(x, (2, 0, 3, 1, 4, 5))
        halves = []
        for dc in range(2):
            even = ((self.c & 1) ^ dc) == 0
            h = x[dc]
            halves.append(jnp.where(even, jnp.swapaxes(h, 0, 1), h))
        return jnp.stack(halves, axis=0).reshape(16 * slots, x.shape[-1])


def positions_of(span_order, index, slots):
    span_len = slots // 2
    at = jnp.arange(slots, dtype=jnp.int32)
    pair = lax.dynamic_slice_in_dim(span_order, 2 * index, 2)
    return jnp.where(at < span_len, pair[0], pair[1]) * span_len + at % span_len


def rope_tables(pos):
    frequency = rope_base ** (-2.0 * jnp.arange(HD // 2, dtype=F32) / HD)
    angles = pos.astype(F32)[:, None] * frequency[None, :]
    return jnp.cos(angles), jnp.sin(angles)


def rotate(v, cosines, sines):
    half = HD // 2
    co, si = cosines[None, :, None, :], sines[None, :, None, :]
    one, two = v[..., :half], v[..., half:]
    return jnp.concatenate([one * co - two * si, two * co + one * si], axis=-1)


def unit_rows(x):
    inverse = lax.rsqrt(jnp.mean(x * x, axis=-1, keepdims=True) + epsilon)
    return x * inverse, inverse


def unit_back(scaled, unit, inverse):
    return inverse * (scaled - unit * jnp.mean(scaled * unit, axis=-1, keepdims=True))


def attend(pre, pos, seq_len, cosines, sines):
    seqs, length, _ = pre.shape
    q = rotate(pre[..., :QW].reshape(seqs, length, GROUP, HD), cosines, sines).astype(BF)
    k = rotate(pre[..., QW : QW + HD].reshape(seqs, length, 1, HD), cosines, sines)[:, :, 0].astype(BF)
    v = pre[..., QW + HD :].astype(BF)
    allowed = (pos[None, None, :] <= pos[None, :, None]) & (
        pos[None, None, :] < seq_len[:, None, None]
    )
    scores = jnp.einsum("sqgd,snd->sgqn", q, k, preferred_element_type=F32) * scale
    scores = jnp.where(allowed[:, None], scores, masked_score)
    top = jnp.max(scores, axis=-1, keepdims=True)
    expo = jnp.exp(scores - top)
    probs = expo / jnp.sum(expo, axis=-1, keepdims=True)
    low = probs.astype(BF)
    attended = jnp.einsum("sgqn,snd->sqgd", low, v, preferred_element_type=F32)
    return attended.astype(BF).reshape(seqs, length, QW), (q, k, v, probs, low)


def attend_back(g_att, kept, cosines, sines):
    q, k, v, probs, low = kept
    seqs, length, _ = g_att.shape
    g_att = g_att.reshape(seqs, length, GROUP, HD)
    g_probs = jnp.einsum("sqgd,snd->sgqn", g_att, v, preferred_element_type=F32)
    inner = jnp.sum(probs * g_probs, axis=-1, keepdims=True)
    g_scores = (probs * (g_probs - inner)).astype(BF)
    g_q = jnp.einsum("sgqn,snd->sqgd", g_scores, k, preferred_element_type=F32) * scale
    g_k = jnp.einsum("sgqn,sqgd->snd", g_scores, q, preferred_element_type=F32) * scale
    g_v = jnp.einsum("sgqn,sqgd->snd", low, g_att, preferred_element_type=F32)
    return jnp.concatenate(
        [
            rotate(g_q, cosines, -sines).astype(BF).reshape(seqs, length, QW),
            rotate(g_k[:, :, None], cosines, -sines).astype(BF)[:, :, 0],
            g_v.astype(BF),
        ],
        axis=-1,
    )


def swiglu(gate_up):
    half = gate_up.shape[-1] // 2
    gate, up = gate_up[:, :half], gate_up[:, half:]
    return (jax.nn.silu(gate) * up).astype(BF)


def swiglu_back(gate_up, g_hidden):
    half = gate_up.shape[-1] // 2
    gate, up = gate_up[:, :half], gate_up[:, half:]
    sig = jax.nn.sigmoid(gate)
    g_gate = (g_hidden * up * sig * (1.0 + gate * (1.0 - sig))).astype(BF)
    g_up = (g_hidden * gate * sig).astype(BF)
    return jnp.concatenate([g_gate, g_up], axis=-1)


def pack_attention(w_query, w_key, w_value, gain):
    rows = w_query.shape[0]
    parts = [
        (w.astype(F32) * gain).astype(BF).reshape(rows, KV, w.shape[1] // KV)
        for w in (w_query, w_key, w_value)
    ]
    return jnp.transpose(jnp.concatenate(parts, axis=2), (1, 0, 2))


def unpack_attention(u):
    u = jnp.transpose(u, (1, 0, 2)).astype(F32)
    rows = u.shape[0]
    return (
        u[..., :QW].reshape(rows, KV * QW),
        u[..., QW : QW + HD].reshape(rows, KV * HD),
        u[..., QW + HD :].reshape(rows, KV * HD),
    )


def pack_mlp(w_gate, w_up, gain, nz):
    rows = w_gate.shape[0]

    def columns(w):
        w = (w.astype(F32) * gain).astype(BF).reshape(rows, nz, KV, -1)
        return jnp.transpose(w, (2, 0, 1, 3)).reshape(KV, rows, -1)

    return jnp.concatenate([columns(w_gate), columns(w_up)], axis=2)


def unpack_mlp(u, nz):
    rows = u.shape[1]
    u = u.reshape(KV, rows, 2, nz, -1)
    u = jnp.transpose(u, (2, 1, 3, 0, 4)).reshape(2, rows, -1).astype(F32)
    return u[0], u[1]


SMEM = pl.BlockSpec(memory_space=pltpu.SMEM)
VMEM = pl.BlockSpec(memory_space=pltpu.VMEM)
WIDE = QW + 2 * HD


def kernel_call(body, outs, scratch=(), flops=0, moved=0):
    def call(scalars, *arrays):
        return pl.pallas_call(
            body,
            out_shape=outs,
            in_specs=[SMEM] * len(scalars) + [VMEM] * len(arrays),
            out_specs=jax.tree.map(lambda _: VMEM, outs),
            scratch_shapes=list(scratch),
            compiler_params=pltpu.CompilerParams(vmem_limit_bytes=48 * 1024 * 1024),
            cost_estimate=pl.CostEstimate(flops=flops, bytes_accessed=moved, transcendentals=0),
        )(*scalars, *arrays)

    return call


def block_rows(core, seq, dc, dy, slots):
    dx, m = seq // 2, seq % 2
    even = (core ^ dc) == 0
    s1 = jnp.where(even, dx, dy)
    s2 = jnp.where(even, dy, dx)
    return pl.multiple_of((((dc * 2 + s2) * 2 + s1) * 2 + m) * slots, slots)


def turn(x, cosines, sines):
    half, width = HD // 2, x.shape[1]
    lane = lax.broadcasted_iota(jnp.int32, x.shape, 1) % HD
    partner = jnp.where(lane < half, pltpu.roll(x, width - half, 1), pltpu.roll(x, half, 1))
    return x * cosines + partner * sines


def probabilities(q, k, allowed):
    scores = lax.dot_general(q, k, (((1,), (1,)), ((), ())), preferred_element_type=F32) * scale
    scores = jnp.where(allowed, scores, masked_score)
    expo = jnp.exp(scores - jnp.max(scores, axis=-1, keepdims=True))
    return expo / jnp.sum(expo, axis=-1, keepdims=True)


def heads_of(x):
    return [x[:, h * HD : (h + 1) * HD] for h in range(x.shape[1] // HD)]


def attention_kernel(
    meta, lens, xs, q0, q1, q2, q3, q4, q5, o0, o1, o2, o3, o4, o5, posc, posr, cosines, sines,
    wqkv, wout, qkv, att, branch, xseq,
):
    core = meta[4]
    slots = xs.shape[0] // 16
    step = q0.shape[0]
    for s, parts in enumerate(((q0,), (q1,), (q2, q3), (q4, q5))):
        piece = parts[0][...]
        if len(parts) > 1:
            piece = piece + parts[1][...]
        wqkv[pl.ds(pl.multiple_of(meta[s] * step, step), step), :] = piece
    step = o0.shape[0]
    for s, parts in enumerate(((o0,), (o1,), (o2, o3), (o4, o5))):
        piece = parts[0][...]
        if len(parts) > 1:
            piece = piece + parts[1][...]
        wout[pl.ds(pl.multiple_of(meta[s] * step, step), step), :] = piece

    def one(seq, carry):
        for dc in range(2):
            for dy in range(2):
                at = block_rows(core, seq, dc, dy, slots)
                b = dc * 2 + dy
                xseq[b * slots : (b + 1) * slots, :] = xs[pl.ds(at, slots), :]
        pre = jnp.dot(xseq[...], wqkv[...], preferred_element_type=F32)
        turned = turn(pre, cosines[...], sines[...])
        low = turned.astype(BF)
        qkv[seq] = low
        one_q, two_q, k, v = heads_of(low)
        allowed = (posr[...] <= posc[...]) & (posr[...] < lens[seq])
        mixed = []
        for q in (one_q, two_q):
            p = probabilities(q, k, allowed).astype(BF)
            mixed.append(jnp.dot(p, v, preferred_element_type=F32))
        out = jnp.concatenate(mixed, axis=1).astype(BF)
        for dc in range(2):
            for dy in range(2):
                at = block_rows(core, seq, dc, dy, slots)
                b = dc * 2 + dy
                att[pl.ds(at, slots), :] = out[b * slots : (b + 1) * slots]
        return carry

    lax.fori_loop(0, 4, one, 0)
    rows = xs.shape[0] // 4

    def project(r, carry):
        at = pl.multiple_of(r * rows, rows)
        part = jnp.dot(att[pl.ds(at, rows), :], wout[...], preferred_element_type=F32)
        branch[pl.ds(at, rows), :] = part.astype(BF)
        return carry

    lax.fori_loop(0, 4, project, 0)


def attention_back_kernel(
    meta, lens, g_branch, wout, qkv, posc, posr, cosines, sines, g_pre, gseq
):
    core = meta[4]
    slots = g_branch.shape[0] // 16

    def one(seq, carry):
        for dc in range(2):
            for dy in range(2):
                at = block_rows(core, seq, dc, dy, slots)
                b = dc * 2 + dy
                gseq[b * slots : (b + 1) * slots, :] = g_branch[pl.ds(at, slots), :]
        g_att = lax.dot_general(
            gseq[...], wout[...], (((1,), (1,)), ((), ())), preferred_element_type=F32
        ).astype(BF)
        one_q, two_q, k, v = heads_of(qkv[seq])
        allowed = (posr[...] <= posc[...]) & (posr[...] < lens[seq])
        g_q, g_k, g_v = [], 0.0, 0.0
        for q, g in zip((one_q, two_q), heads_of(g_att)):
            p = probabilities(q, k, allowed)
            g_p = lax.dot_general(g, v, (((1,), (1,)), ((), ())), preferred_element_type=F32)
            inner = jnp.sum(p * g_p, axis=-1, keepdims=True)
            g_s = (p * (g_p - inner)).astype(BF)
            g_q.append(jnp.dot(g_s, k, preferred_element_type=F32) * scale)
            g_k = g_k + lax.dot_general(g_s, q, (((0,), (0,)), ((), ())), preferred_element_type=F32) * scale
            g_v = g_v + lax.dot_general(
                p.astype(BF), g, (((0,), (0,)), ((), ())), preferred_element_type=F32
            )
        full = jnp.concatenate(g_q + [g_k, g_v], axis=1)
        out = turn(full, cosines[...], -sines[...]).astype(BF)
        for dc in range(2):
            for dy in range(2):
                at = block_rows(core, seq, dc, dy, slots)
                b = dc * 2 + dy
                g_pre[pl.ds(at, slots), :] = out[b * slots : (b + 1) * slots]
        return carry

    lax.fori_loop(0, 4, one, 0)


def norm_kernel(source, a, b, residual, xhat, inverse):
    r = source[...].astype(F32) + a[...].astype(F32) + b[...].astype(F32)
    inv = lax.rsqrt(jnp.mean(r * r, axis=-1, keepdims=True) + epsilon)
    residual[...] = r
    inverse[...] = inv
    xhat[...] = (r * inv).astype(BF)


def norm_back_kernel(g_res, source, inverse, a, b, out, low):
    scaled = a[...].astype(F32) + b[...].astype(F32)
    inv = inverse[...]
    unit = source[...].astype(F32) * inv
    g = g_res[...] + inv * (scaled - unit * jnp.mean(scaled * unit, axis=-1, keepdims=True))
    out[...] = g
    low[...] = g.astype(BF)


def norm_back_low_kernel(g_res, source, inverse, a, b, low):
    scaled = a[...].astype(F32) + b[...].astype(F32)
    inv = inverse[...]
    unit = source[...].astype(F32) * inv
    low[...] = (g_res[...] + inv * (scaled - unit * jnp.mean(scaled * unit, axis=-1, keepdims=True))).astype(BF)


def shaped(*shape, dtype=BF):
    return jax.ShapeDtypeStruct(shape, dtype)


def paired(*items):
    return sum(jnp.sum(w.astype(F32) * g, axis=1) for w, g in items)


def on_line(
    hidden_in, lengths, span_order, attn_gain, w_query, w_key, w_value, w_out,
    mlp_gain, w_gate, w_up, w_down, out_grad,
):
    lay = Line()
    _, slots, width = hidden_in.shape
    rows, nz = w_query.shape[0], lay.nz
    tokens = 16 * slots
    length = 4 * slots
    own = 2 * slots
    go = lengths[0] > 0

    wdown = lay.spread(w_down)

    def begin(hidden_in, lengths, span_order, w_query, w_key, w_value, w_out, w_gate, w_up, attn_gain, mlp_gain, out_grad):
        gain = attn_gain.astype(F32)[:, None]
        gain_m = mlp_gain.astype(F32)[:, None]
        o0 = send(w_out, lay.place)
        theirs = send(lengths, lay.xflip)
        qkv_s = pack_attention(w_query, w_key, w_value, gain)
        q0 = lay.exchange(qkv_s)
        source = hidden_in.astype(F32).reshape(own, width)
        unit, inverse = unit_rows(source)
        xhat = unit.astype(BF)
        x1 = send(xhat, lay.first)
        gu_s = pack_mlp(w_gate, w_up, gain_m, nz)
        o0, x1, gu_s, xhat = fence(o0, x1, gu_s, xhat)
        o1 = send(o0, lay.pair)
        o2 = send(o0, lay.inner)
        x01 = jnp.stack([xhat, x1])
        x2 = send(x01, lay.second)
        q0, o1, o2, x2, x01, gu_s = fence(q0, o1, o2, x2, x01, gu_s)
        q0 = q0.reshape(KV * rows, WIDE)
        q1 = send(q0, lay.pair)
        q2 = send(q0, lay.inner)
        o3 = send(o2, lay.outward)
        o4 = send(o1, lay.inner)
        gu0 = lay.exchange(gu_s)
        x0123 = jnp.stack([x01, x2])
        x3 = send(x0123, lay.core)
        q1, q2, o3, o4, x3 = fence(q1, q2, o3, o4, x3)
        q3 = send(q2, lay.outward)
        q4 = send(q1, lay.inner)
        o5 = send(o4, lay.outward)
        xs = jnp.stack([x0123, x3]).reshape(tokens, width)
        pos = jnp.concatenate([positions_of(span_order, lay.c ^ k, slots) for k in (0, 2, 1, 3)])
        usable = (positions_of(span_order, lay.c, slots)[None, :] < lengths[:, None]).astype(F32).reshape(own, 1)
        cosines, sines = rope_tables(pos)
        flat = jnp.concatenate([cosines, cosines], axis=1)
        signed = jnp.concatenate([-sines, sines], axis=1)
        cosines = jnp.concatenate([flat] * 3 + [jnp.ones_like(flat)], axis=1)
        sines = jnp.concatenate([signed] * 3 + [jnp.zeros_like(flat)], axis=1)
        g_res = out_grad.astype(F32).reshape(own, width) * usable
        q3, q4, o5, gu0, xs, cosines, sines, g_res = fence(q3, q4, o5, gu0, xs, cosines, sines, g_res)
        q5 = send(q4, lay.outward)
        seq_len = jnp.concatenate([lengths, theirs])
        return (q0, q1, q2, q3, q4, q5), (o0, o1, o2, o3, o4, o5), xs, gu0, inverse, pos, usable, cosines, sines, g_res, seq_len

    q_pieces, o_pieces, xs, gu0, inverse, pos, usable, cosines, sines, g_res, seq_len = unit_of_work(
        go, begin, hidden_in, lengths, span_order, w_query, w_key, w_value, w_out, w_gate, w_up, attn_gain, mlp_gain, out_grad
    )
    wdown, gu0 = fence(wdown, gu0)
    wgu = lay.spread(gu0.reshape(KV * rows, -1))
    posc = pos.astype(jnp.int32)[:, None]
    posr = pos.astype(jnp.int32)[None, :]
    meta = jnp.stack([k.astype(jnp.int32) for k in lay.order] + [(lay.c & 1).astype(jnp.int32)])

    def halves(x):
        return x.reshape(2, x.shape[0] // 2, width)

    def forward(meta, seq_len, xs, q_pieces, o_pieces, posc, posr, cosines, sines, hidden_in, g_res):
        g_low = g_res.astype(BF)
        e1 = send(g_low, lay.first)
        wqkv, wout, qkv, att, branch = kernel_call(
            attention_kernel,
            (
                shaped(width, WIDE), shaped(QW, width), shaped(4, length, WIDE), shaped(tokens, QW), shaped(tokens, width),
            ),
            scratch=[pltpu.VMEM((length, width), BF)],
            flops=2 * tokens * width * (WIDE + QW),
            moved=12 * 1024 * 1024,
        )((meta, seq_len), xs, *q_pieces, *o_pieces, posc, posr, cosines, sines)
        e1, branch = fence(e1, branch)
        e01 = jnp.stack([g_low, e1])
        e2 = send(e01, lay.second)
        r = halves(branch)
        r = halves(plus(r[0], send(r[1], lay.core)))
        r = halves(plus(r[0], send(r[1], lay.second)))
        got = send(r[1], lay.first)
        residual, xm0, inverse_m = kernel_call(
            norm_kernel, (shaped(own, width, dtype=F32), shaped(own, width), shaped(own, 1, dtype=F32))
        )((), hidden_in.reshape(own, width), r[0], got)
        m1 = send(xm0, lay.first)
        m01 = jnp.stack([xm0, m1])
        m2 = send(m01, lay.second)
        e0123 = jnp.stack([e01, e2])
        e3 = send(e0123, lay.core)
        g_mlp = jnp.stack([e0123, e3]).reshape(tokens, width)
        m0123 = jnp.stack([m01, m2])
        m3 = send(m0123, lay.core)
        xm = jnp.stack([m0123, m3]).reshape(tokens, width)
        return wqkv, wout, qkv, att, residual, inverse_m, xm, g_mlp

    wqkv, wout, qkv, att, residual, inverse_m, xm, g_mlp = unit_of_work(
        go, forward, meta, seq_len, xs, q_pieces, o_pieces, posc, posr, cosines, sines, hidden_in, g_res
    )
    gate_up = mm(xm, wgu)
    hidden = swiglu(gate_up)
    r = halves(mm(hidden, wdown).astype(BF))
    r = halves(plus(r[0], send(r[1], lay.core)))
    u_down = mm_lt(hidden, g_mlp)
    g_gu = swiglu_back(gate_up, mm_rt(g_mlp, wdown))
    r = halves(plus(r[0], send(r[1], lay.second)))
    u_gu = mm_lt(xm, g_gu)
    got = send(r[1], lay.first)
    block_out = (usable * (residual + r[0].astype(F32) + got.astype(F32))).astype(BF).reshape(hidden_in.shape)
    g_nm = mm_rt(g_gu, wgu).astype(BF)
    v_gu = lay.gather_sum(u_gu)
    grad_down = lay.gather_sum(u_down).astype(F32)
    g_nm, block_out = fence(g_nm, block_out)

    def backward(meta, seq_len, g_nm, g_res, residual, inverse_m, wout, qkv, posc, posr, cosines, sines, att, xs, wqkv):
        r = halves(g_nm)
        r = halves(plus(r[0], send(r[1], lay.core)))
        r = halves(plus(r[0], send(r[1], lay.second)))
        got = send(r[1], lay.first)
        g_res2, h0 = kernel_call(
            norm_back_kernel, (shaped(own, width, dtype=F32), shaped(own, width))
        )((), g_res, residual, inverse_m, r[0], got)
        h1 = send(h0, lay.first)
        h01 = jnp.stack([h0, h1])
        h2 = send(h01, lay.second)
        h0123 = jnp.stack([h01, h2])
        h3 = send(h0123, lay.core)
        g_branch = jnp.stack([h0123, h3]).reshape(tokens, width)
        u_out = lay.to_pieces(mm_lt(att, g_branch).astype(BF))
        f5 = send(u_out[3], lay.inward)
        g_pre = kernel_call(
            attention_back_kernel,
            shaped(tokens, WIDE),
            scratch=[pltpu.VMEM((length, width), BF)],
            flops=4 * tokens * width * QW,
            moved=8 * 1024 * 1024,
        )((meta, seq_len), g_branch, wout, qkv, posc, posr, cosines, sines)
        f5, g_pre = fence(f5, g_pre)
        f4 = send(plus(u_out[3], f5), lay.inner)
        f3 = send(u_out[2], lay.inward)
        u_qkv = lay.to_pieces(mm_lt(xs, g_pre).astype(BF))
        u_qkv, f4, f3, g_pre = fence(u_qkv, f4, f3, g_pre)
        c5 = send(u_qkv[3], lay.inward)
        f1 = send(plus(u_out[1], f4), lay.pair)
        f2 = send(plus(u_out[2], f3), lay.inner)
        g_na = halves(mm_rt(g_pre, wqkv).astype(BF))
        return g_res2, g_na, u_qkv, c5, u_out[0], f1, f2

    g_res2, g_na, u_qkv, c5, f0, f1, f2 = unit_of_work(
        go, backward, meta, seq_len, g_nm, g_res, residual, inverse_m, wout, qkv, posc, posr, cosines, sines, att, xs, wqkv
    )
    gain = attn_gain.astype(F32)[:, None]
    gain_m = mlp_gain.astype(F32)[:, None]
    c5, v_gu = fence(c5, v_gu)
    c4 = send(plus(u_qkv[3], c5), lay.inner)
    c3 = send(u_qkv[2], lay.inward)
    r = halves(plus(g_na[0], send(g_na[1], lay.core)))
    v_gu = lay.exchange(v_gu.reshape(KV, rows, -1))
    v_out = (f0.astype(F32) + f1.astype(F32) + f2.astype(F32)).astype(BF)
    c4, c3, r, v_gu = fence(c4, c3, r, v_gu)
    c1 = send(plus(u_qkv[1], c4), lay.pair)
    c2 = send(plus(u_qkv[2], c3), lay.inner)
    r = halves(plus(r[0], send(r[1], lay.second)))
    u_gate, u_up = unpack_mlp(v_gu, nz)
    grad_mlp_gain = paired((w_gate, u_gate), (w_up, u_up))
    grad_gate, grad_up = u_gate * gain_m, u_up * gain_m
    c1, c2, r, grad_gate, grad_up, v_out = fence(c1, c2, r, grad_gate, grad_up, v_out)
    v_qkv = (u_qkv[0].astype(F32) + c1.astype(F32) + c2.astype(F32)).astype(BF)
    v_qkv = lay.exchange(v_qkv.reshape(KV, rows, -1))
    grad_out = send(v_out, lay.back).astype(F32)
    got = send(r[1], lay.first)
    grad_in = kernel_call(norm_back_low_kernel, shaped(own, width))(
        (), g_res2, hidden_in.reshape(own, width), inverse, r[0], got
    ).reshape(hidden_in.shape)
    u_q, u_k, u_v = unpack_attention(v_qkv)
    grad_attn_gain = paired((w_query, u_q), (w_key, u_k), (w_value, u_v))
    return (
        block_out, grad_in, grad_attn_gain, u_q * gain, u_k * gain, u_v * gain, grad_out,
        grad_mlp_gain, grad_gate, grad_up, grad_down,
    )


def anywhere(
    hidden_in, lengths, span_order, attn_gain, w_query, w_key, w_value, w_out,
    mlp_gain, w_gate, w_up, w_down, out_grad,
):
    lay = Layout()
    micro, slots, width = hidden_in.shape
    rows, nz = w_query.shape[0], lay.nz
    gain = attn_gain.astype(F32)[:, None]
    gain_m = mlp_gain.astype(F32)[:, None]
    pos = jnp.concatenate([positions_of(span_order, k, slots) for k in range(lay.ctx)])
    usable = (positions_of(span_order, lay.c, slots)[None, :] < lengths[:, None]).astype(F32)[..., None]
    cosines, sines = rope_tables(pos)
    length = slots * lay.ctx

    def tokens(x):
        return lax.all_gather(x, "ctx", axis=1, tiled=True).reshape(micro * length, width)

    def own(x):
        x = x.astype(BF).reshape(micro, length, width)
        return lax.psum_scatter(x, "ctx", scatter_dimension=1, tiled=True).astype(F32)

    spread, collect = lay.spread, lay.gather_sum
    wqkv = spread(lay.exchange(pack_attention(w_query, w_key, w_value, gain)).reshape(KV * rows, -1))
    wgu = spread(lay.exchange(pack_mlp(w_gate, w_up, gain_m, nz)).reshape(KV * rows, -1))
    wout = spread(send(w_out, lay.place))
    wdown = spread(w_down)
    source = hidden_in.astype(F32)
    unit, inverse = unit_rows(source)
    xs = tokens(unit.astype(BF))
    g_res = out_grad.astype(F32) * usable
    g_mlp = tokens(g_res.astype(BF))
    pre = mm(xs, wqkv).reshape(micro, length, -1)
    attended, kept = attend(pre, pos, lengths, cosines, sines)
    att = attended.reshape(micro * length, QW)
    residual = source + own(mm(att, wout))
    unit_m, inverse_m = unit_rows(residual)
    xm = tokens(unit_m.astype(BF))
    gate_up = mm(xm, wgu)
    hidden = swiglu(gate_up)
    block_out = (usable * (residual + own(mm(hidden, wdown)))).astype(BF)
    grad_down = collect(mm_lt(hidden, g_mlp)).astype(F32)
    g_gu = swiglu_back(gate_up, mm_rt(g_mlp, wdown))
    v_gu = lay.exchange(collect(mm_lt(xm, g_gu)).reshape(KV, rows, -1))
    u_gate, u_up = unpack_mlp(v_gu, nz)
    g_res2 = g_res + unit_back(own(mm_rt(g_gu, wgu)), unit_m, inverse_m)
    g_branch = tokens(g_res2.astype(BF))
    grad_out = send(collect(mm_lt(att, g_branch)), lay.back).astype(F32)
    g_att = mm_rt(g_branch, wout).astype(BF).reshape(micro, length, QW)
    g_pre = attend_back(g_att, kept, cosines, sines).reshape(micro * length, -1)
    v_qkv = lay.exchange(collect(mm_lt(xs, g_pre)).reshape(KV, rows, -1))
    u_q, u_k, u_v = unpack_attention(v_qkv)
    grad_in = (g_res2 + unit_back(own(mm_rt(g_pre, wqkv)), unit, inverse)).astype(BF)
    return (
        block_out, grad_in, paired((w_query, u_q), (w_key, u_k), (w_value, u_v)),
        u_q * gain, u_k * gain, u_v * gain, grad_out,
        paired((w_gate, u_gate), (w_up, u_up)), u_gate * gain_m, u_up * gain_m, grad_down,
    )


def solution(mesh):
    rows = P(AXES, None)
    tokens = P("fsdp", "ctx", None)
    line = mesh.shape["ctx"] == 4 and mesh.shape["fsdp"] == 8
    return jax.shard_map(
        on_line if line else anywhere,
        mesh=mesh,
        in_specs=(tokens, P("fsdp"), P(), P(AXES), rows, rows, rows, rows, P(AXES), rows, rows, rows, tokens),
        out_specs=(tokens, tokens, P(AXES), rows, rows, rows, rows, P(AXES), rows, rows, rows),
        check_vma=False,
    )
```

```python
import jax
import jax.numpy as jnp
import numpy as np
from jax import lax
from jax.experimental import pallas as pl
from jax.experimental.pallas import tpu as pltpu
from jax.sharding import PartitionSpec as P

H = 16
KV = 8
HD = 96
GROUP = H // KV
QW = GROUP * HD
AXES = ("fsdp", "ctx")

epsilon = 1e-05
rope_base = 100000.0
masked_score = -1e30
scale = HD ** (-0.5)
BF = jnp.bfloat16
F32 = jnp.float32


def mm(left, right):
    return jnp.dot(left, right, preferred_element_type=F32)


def mm_lt(left, right):
    return lax.dot_general(left, right, (((0,), (0,)), ((), ())), preferred_element_type=F32)


def mm_rt(left, right):
    return lax.dot_general(left, right, (((1,), (1,)), ((), ())), preferred_element_type=F32)


def plus(a, b):
    return a + b


def send(x, pairs):
    return lax.ppermute(x, AXES, pairs)


def unit_of_work(go, body, *args):
    def idle(*args):
        return jax.tree.map(lambda leaf: jnp.zeros(leaf.shape, leaf.dtype), jax.eval_shape(body, *args))

    return lax.cond(go, body, idle, *args)


def fence(*items):
    return lax.optimization_barrier(items)


class Layout:
    def __init__(self):
        self.ctx = lax.axis_size("ctx")
        self.fsdp = lax.axis_size("fsdp")
        self.tpf = KV // self.ctx
        self.nz = self.fsdp // self.tpf
        self.total = self.fsdp * self.ctx
        self.fast = self.ctx == 4 and self.tpf == 2 and self.nz == 4
        self.f = lax.axis_index("fsdp")
        self.c = lax.axis_index("ctx")
        self.z = self.f // self.tpf
        self.place = [(b, (b % self.nz) * KV + b // self.nz) for b in range(self.total)]
        self.back = [(d, s) for s, d in self.place]

    def exchange(self, x):
        if self.tpf == 1:
            return lax.all_to_all(x, "ctx", split_axis=0, concat_axis=0, tiled=True)
        groups = [[z * KV + i for i in range(KV)] for z in range(self.nz)]
        return lax.all_to_all(
            x, AXES, split_axis=0, concat_axis=0, tiled=True, axis_index_groups=groups
        )

    def lines(self):
        return [[z * KV + i for z in range(self.nz)] for i in range(KV)]

    def spread(self, x):
        if self.tpf == 1:
            return lax.all_gather(x, "fsdp", axis=0, tiled=True)
        return lax.all_gather(x, AXES, axis=0, tiled=True, axis_index_groups=self.lines())

    def gather_sum(self, x):
        x = x.astype(BF)
        if self.tpf == 1:
            return lax.psum_scatter(x, "fsdp", scatter_dimension=0, tiled=True)
        return lax.psum_scatter(
            x, AXES, scatter_dimension=0, tiled=True, axis_index_groups=self.lines()
        )


class Line(Layout):
    def __init__(self):
        super().__init__()
        total = self.total
        self.core = [(d, d ^ 1) for d in range(total)]
        self.first = [(d, d ^ (2 if d & 1 else 4)) for d in range(total)]
        self.second = [(d, d ^ (4 if d & 1 else 2)) for d in range(total)]
        self.xflip = [(d, d ^ 4) for d in range(total)]

        def planes(pairs):
            return [(s * KV + i, d * KV + i) for s, d in pairs for i in range(KV)]

        self.pair = planes([(0, 1), (1, 0), (2, 3), (3, 2)])
        self.inner = planes([(1, 2), (2, 1)])
        self.outward = planes([(1, 0), (2, 3)])
        self.inward = planes([(0, 1), (3, 2)])
        z = self.z
        low = z < 2
        self.order = [z, z ^ 1, jnp.where(low, 2, 1), jnp.where(low, 3, 0)]
        table = ((0, 1, 3, 3), (1, 0, 2, 2), (2, 2, 0, 1), (3, 3, 1, 0))
        self.slot = [
            jnp.where(z == 0, r[0], jnp.where(z == 1, r[1], jnp.where(z == 2, r[2], r[3])))
            for r in table
        ]

    def take_columns(self, x, blocks):
        width = x.shape[-1] // self.nz
        return jnp.concatenate(
            [lax.dynamic_slice_in_dim(x, k * width, width, axis=-1) for k in blocks], axis=-1
        )

    def take_rows(self, pieces):
        full = jnp.stack(pieces)
        return jnp.concatenate(
            [lax.dynamic_index_in_dim(full, k, axis=0, keepdims=False) for k in self.slot], axis=0
        )

    def to_pieces(self, x):
        full = x.reshape((self.nz, x.shape[0] // self.nz) + x.shape[1:])
        return [lax.dynamic_index_in_dim(full, k, axis=0, keepdims=False) for k in self.order]

    def all_tokens(self, x):
        x = jnp.stack([x, send(x, self.first)])
        x = jnp.stack([x, send(x, self.second)])
        x = jnp.stack([x, send(x, self.core)])
        return x.reshape(-1, x.shape[-1])

    def plane_tokens(self, x):
        x = jnp.stack([x, send(x, self.first)])
        x = jnp.stack([x, send(x, self.second)])
        other = send(x, self.core)
        return x.reshape(-1, x.shape[-1]), other.reshape(-1, x.shape[-1])

    def collect_tokens(self, x, slots):
        x = x.reshape(2, 2, 2, 2, slots, x.shape[-1])
        x = plus(x[0], send(x[1], self.core))
        x = plus(x[0], send(x[1], self.second))
        return x[0].astype(F32) + send(x[1], self.first).astype(F32)

    def to_seqs(self, x, slots):
        x = x.reshape(2, 2, 2, 2, slots, x.shape[-1])
        halves = []
        for dc in range(2):
            even = ((self.c & 1) ^ dc) == 0
            h = x[dc]
            halves.append(jnp.where(even, jnp.swapaxes(h, 0, 1), h))
        x = jnp.stack(halves, axis=0)
        x = jnp.transpose(x, (1, 3, 0, 2, 4, 5))
        return x.reshape(4, 4 * slots, x.shape[-1])

    def from_seqs(self, x, slots):
        x = x.reshape(2, 2, 2, 2, slots, x.shape[-1])
        x = jnp.transpose(x, (2, 0, 3, 1, 4, 5))
        halves = []
        for dc in range(2):
            even = ((self.c & 1) ^ dc) == 0
            h = x[dc]
            halves.append(jnp.where(even, jnp.swapaxes(h, 0, 1), h))
        return jnp.stack(halves, axis=0).reshape(16 * slots, x.shape[-1])


def positions_of(span_order, index, slots):
    span_len = slots // 2
    at = jnp.arange(slots, dtype=jnp.int32)
    pair = lax.dynamic_slice_in_dim(span_order, 2 * index, 2)
    return jnp.where(at < span_len, pair[0], pair[1]) * span_len + at % span_len


def rope_tables(pos):
    frequency = rope_base ** (-2.0 * jnp.arange(HD // 2, dtype=F32) / HD)
    angles = pos.astype(F32)[:, None] * frequency[None, :]
    return jnp.cos(angles), jnp.sin(angles)


def rotate(v, cosines, sines):
    half = HD // 2
    co, si = cosines[None, :, None, :], sines[None, :, None, :]
    one, two = v[..., :half], v[..., half:]
    return jnp.concatenate([one * co - two * si, two * co + one * si], axis=-1)


def unit_rows(x):
    inverse = lax.rsqrt(jnp.mean(x * x, axis=-1, keepdims=True) + epsilon)
    return x * inverse, inverse


def unit_back(scaled, unit, inverse):
    return inverse * (scaled - unit * jnp.mean(scaled * unit, axis=-1, keepdims=True))


def attend(pre, pos, seq_len, cosines, sines):
    seqs, length, _ = pre.shape
    q = rotate(pre[..., :QW].reshape(seqs, length, GROUP, HD), cosines, sines).astype(BF)
    k = rotate(pre[..., QW : QW + HD].reshape(seqs, length, 1, HD), cosines, sines)[:, :, 0].astype(BF)
    v = pre[..., QW + HD :].astype(BF)
    allowed = (pos[None, None, :] <= pos[None, :, None]) & (
        pos[None, None, :] < seq_len[:, None, None]
    )
    scores = jnp.einsum("sqgd,snd->sgqn", q, k, preferred_element_type=F32) * scale
    scores = jnp.where(allowed[:, None], scores, masked_score)
    top = jnp.max(scores, axis=-1, keepdims=True)
    expo = jnp.exp(scores - top)
    probs = expo / jnp.sum(expo, axis=-1, keepdims=True)
    low = probs.astype(BF)
    attended = jnp.einsum("sgqn,snd->sqgd", low, v, preferred_element_type=F32)
    return attended.astype(BF).reshape(seqs, length, QW), (q, k, v, probs, low)


def attend_back(g_att, kept, cosines, sines):
    q, k, v, probs, low = kept
    seqs, length, _ = g_att.shape
    g_att = g_att.reshape(seqs, length, GROUP, HD)
    g_probs = jnp.einsum("sqgd,snd->sgqn", g_att, v, preferred_element_type=F32)
    inner = jnp.sum(probs * g_probs, axis=-1, keepdims=True)
    g_scores = (probs * (g_probs - inner)).astype(BF)
    g_q = jnp.einsum("sgqn,snd->sqgd", g_scores, k, preferred_element_type=F32) * scale
    g_k = jnp.einsum("sgqn,sqgd->snd", g_scores, q, preferred_element_type=F32) * scale
    g_v = jnp.einsum("sgqn,sqgd->snd", low, g_att, preferred_element_type=F32)
    return jnp.concatenate(
        [
            rotate(g_q, cosines, -sines).astype(BF).reshape(seqs, length, QW),
            rotate(g_k[:, :, None], cosines, -sines).astype(BF)[:, :, 0],
            g_v.astype(BF),
        ],
        axis=-1,
    )


def swiglu(gate_up):
    half = gate_up.shape[-1] // 2
    gate, up = gate_up[:, :half], gate_up[:, half:]
    return (jax.nn.silu(gate) * up).astype(BF)


def swiglu_back(gate_up, g_hidden):
    half = gate_up.shape[-1] // 2
    gate, up = gate_up[:, :half], gate_up[:, half:]
    sig = jax.nn.sigmoid(gate)
    g_gate = (g_hidden * up * sig * (1.0 + gate * (1.0 - sig))).astype(BF)
    g_up = (g_hidden * gate * sig).astype(BF)
    return jnp.concatenate([g_gate, g_up], axis=-1)


def pack_attention(w_query, w_key, w_value, gain):
    rows = w_query.shape[0]
    parts = [
        (w.astype(F32) * gain).astype(BF).reshape(rows, KV, w.shape[1] // KV)
        for w in (w_query, w_key, w_value)
    ]
    return jnp.transpose(jnp.concatenate(parts, axis=2), (1, 0, 2))


def unpack_attention(u):
    u = jnp.transpose(u, (1, 0, 2)).astype(F32)
    rows = u.shape[0]
    return (
        u[..., :QW].reshape(rows, KV * QW),
        u[..., QW : QW + HD].reshape(rows, KV * HD),
        u[..., QW + HD :].reshape(rows, KV * HD),
    )


def pack_mlp(w_gate, w_up, gain, nz):
    rows = w_gate.shape[0]

    def columns(w):
        w = (w.astype(F32) * gain).astype(BF).reshape(rows, nz, KV, -1)
        return jnp.transpose(w, (2, 0, 1, 3)).reshape(KV, rows, -1)

    return jnp.concatenate([columns(w_gate), columns(w_up)], axis=2)


def unpack_mlp(u, nz):
    rows = u.shape[1]
    u = u.reshape(KV, rows, 2, nz, -1)
    u = jnp.transpose(u, (2, 1, 3, 0, 4)).reshape(2, rows, -1).astype(F32)
    return u[0], u[1]


SMEM = pl.BlockSpec(memory_space=pltpu.SMEM)
VMEM = pl.BlockSpec(memory_space=pltpu.VMEM)
WIDE = QW + 2 * HD
FREE = pl.CostEstimate(flops=0, bytes_accessed=0, transcendentals=0)
ROOM = pltpu.CompilerParams(vmem_limit_bytes=56 * 1024 * 1024)


def shaped(*shape, dtype=BF):
    return jax.ShapeDtypeStruct(shape, dtype)


def kernel_call(body, outs, scratch=()):
    def call(scalars, *arrays):
        return pl.pallas_call(
            body,
            out_shape=outs,
            in_specs=[SMEM] * len(scalars) + [VMEM] * len(arrays),
            out_specs=jax.tree.map(lambda _: VMEM, outs),
            scratch_shapes=list(scratch),
            compiler_params=ROOM,
            cost_estimate=FREE,
        )(*scalars, *arrays)

    return call


def dot(a, b, dims=((1,), (0,))):
    return lax.dot_general(a, b, (dims, ((), ())), preferred_element_type=F32)


LEFT_T = ((0,), (0,))
RIGHT_T = ((1,), (1,))


def block_rows(core, seq, dc, dy, slots):
    dx, m = seq // 2, seq % 2
    even = (core ^ dc) == 0
    s1 = jnp.where(even, dx, dy)
    s2 = jnp.where(even, dy, dx)
    return pl.multiple_of(((s2 * 2 + s1) * 2 + m) * slots, slots)


def blocks_of(slots):
    for dc in range(2):
        for dy in range(2):
            b = dc * 2 + dy
            yield dc, dy, slice(b * slots, (b + 1) * slots)


def spans_of(spans, ctx):
    out = []
    for dc in range(2):
        for dy in range(2):
            other = ctx ^ (dy * 2 + dc)
            out += [spans[2 * other], spans[2 * other + 1]]
    return out


def along(held, length, axis, shape):
    at = lax.broadcasted_iota(jnp.int32, shape, axis)
    step = length // len(held)
    pos = at % step
    for i, span in enumerate(held):
        pos = pos + jnp.where(at // step == i, span * step, 0)
    return pos


def rotary_rows(held, table, out):
    step = out.shape[0] // len(held)
    for i, span in enumerate(held):
        out[i * step : (i + 1) * step, :] = table[pl.ds(pl.multiple_of(span * step, step), step), :]


def turn(x, cosines, sines):
    half, width = HD // 2, x.shape[1]
    lane = lax.broadcasted_iota(jnp.int32, x.shape, 1) % HD
    partner = jnp.where(lane < half, pltpu.roll(x, width - half, 1), pltpu.roll(x, half, 1))
    return x * cosines + partner * sines


def probabilities(q, k, allowed):
    scores = jnp.where(allowed, dot(q, k, RIGHT_T) * scale, masked_score)
    expo = jnp.exp(scores - jnp.max(scores, axis=-1, keepdims=True))
    return expo / jnp.sum(expo, axis=-1, keepdims=True)


def heads_of(x):
    return [x[:, h * HD : (h + 1) * HD] for h in range(x.shape[1] // HD)]


def assemble(meta, pieces, out):
    p0, p1, p2, p3, p4, p5 = pieces
    step = p0.shape[0]
    for s, parts in enumerate(((p0,), (p1,), (p2, p3), (p4, p5))):
        piece = parts[0][...]
        if len(parts) > 1:
            piece = piece + parts[1][...]
        out[pl.ds(pl.multiple_of(meta[s] * step, step), step), :] = piece


def fetch_qkv(full, out):
    step = full.shape[2]
    for z in range(full.shape[0]):
        out[z * step : (z + 1) * step, :] = full[z, :step, :]


def fetch_out(full, out):
    nz, total, step = full.shape
    count = out.shape[1] // step
    rows = (total - step) // count
    for z in range(nz):
        for k in range(count):
            out[z * rows : (z + 1) * rows, k * step : (k + 1) * step] = full[
                z, step + k * rows : step + (k + 1) * rows, :
            ]


def stacked_columns(x, cut):
    return jnp.concatenate([x[:, k : k + cut] for k in range(0, x.shape[1], cut)], axis=0)


def column(row):
    n = row.shape[1]
    same = lax.broadcasted_iota(jnp.int32, (n, n), 0) == lax.broadcasted_iota(jnp.int32, (n, n), 1)
    return jnp.sum(jnp.where(same, row, 0.0), axis=1, keepdims=True)


def row_of(col):
    n = col.shape[0]
    same = lax.broadcasted_iota(jnp.int32, (n, n), 0) == lax.broadcasted_iota(jnp.int32, (n, n), 1)
    return jnp.sum(jnp.where(same, col, 0.0), axis=0, keepdims=True)


def pack_attention_kernel(wq, wk, wv, gain, out):
    g = column(gain[...].astype(F32))
    q, k, v = ((w[...].astype(F32) * g).astype(BF) for w in (wq, wk, wv))
    for j in range(KV):
        out[j, :, :QW] = q[:, j * QW : (j + 1) * QW]
        out[j, :, QW : QW + HD] = k[:, j * HD : (j + 1) * HD]
        out[j, :, QW + HD :] = v[:, j * HD : (j + 1) * HD]


def pack_mlp_kernel(wg, wu, gain, out):
    g = column(gain[...].astype(F32))
    half = out.shape[2] // 2
    blocks = 4
    hid = half // blocks
    for h, w in enumerate((wg, wu)):
        x = (w[...].astype(F32) * g).astype(BF)
        for z in range(blocks):
            for j in range(KV):
                out[j, :, h * half + z * hid : h * half + (z + 1) * hid] = x[
                    :, (z * KV + j) * hid : (z * KV + j + 1) * hid
                ]


def unpack_attention_kernel(u, wq, wk, wv, gain, gq, gk, gv, total):
    g = column(gain[...].astype(F32))
    acc = jnp.zeros(g.shape, F32)
    for j in range(KV):
        x = u[j].astype(F32)
        for w, out, lo, n in ((wq, gq, 0, QW), (wk, gk, QW, HD), (wv, gv, QW + HD, HD)):
            part = x[:, lo : lo + n]
            out[:, j * n : (j + 1) * n] = part * g
            acc += jnp.sum(part * w[:, j * n : (j + 1) * n].astype(F32), axis=1, keepdims=True)
    total[...] = row_of(acc)


def unpack_mlp_kernel(u, wg, wu, gain, gg, gu, total):
    g = column(gain[...].astype(F32))
    acc = jnp.zeros(g.shape, F32)
    half = wg.shape[1] // KV
    blocks = 4
    hid = half // blocks
    for j in range(KV):
        x = u[j].astype(F32)
        for h, (w, out) in enumerate(((wg, gg), (wu, gu))):
            for z in range(blocks):
                at = slice((z * KV + j) * hid, (z * KV + j + 1) * hid)
                part = x[:, h * half + z * hid : h * half + (z + 1) * hid]
                out[:, at] = part * g
                acc += jnp.sum(part * w[:, at].astype(F32), axis=1, keepdims=True)
    total[...] = row_of(acc)


def usable_rows(lens, spans, ctx, shape):
    at = lax.broadcasted_iota(jnp.int32, shape, 0)
    slots = shape[0] // 2
    slot, step = at % slots, slots // 2
    pos = jnp.where(slot < step, spans[2 * ctx], spans[2 * ctx + 1]) * step + slot % step
    length = jnp.where(at < slots, lens[0], lens[1])
    return (pos < length).astype(F32)


def prepare_kernel(meta, lens, spans, x, g, xhat, inverse, g_low):
    v = x[...].astype(F32)
    inv = lax.rsqrt(jnp.mean(v * v, axis=-1, keepdims=True) + epsilon)
    inverse[...] = inv
    xhat[...] = (v * inv).astype(BF)
    g_low[...] = (g[...].astype(F32) * usable_rows(lens, spans, meta[5], inverse.shape)).astype(BF)


def finish_kernel(meta, lens, spans, residual, a, b, out):
    total = residual[...] + a[...].astype(F32) + b[...].astype(F32)
    out[...] = (total * usable_rows(lens, spans, meta[5], (total.shape[0], 1))).astype(BF)


def attention_kernel(
    meta, lens, spans, xa, xb, full, cos_table, sin_table, wqkv, qkv, att, xseq, cosines, sines
):
    core, ctx = meta[4], meta[5]
    slots = xa.shape[0] // 8
    length = xseq.shape[0]
    fetch_qkv(full, wqkv)
    held = spans_of(spans, ctx)
    rotary_rows(held, cos_table, cosines)
    rotary_rows(held, sin_table, sines)
    posc = along(held, length, 0, (length, length))
    posr = along(held, length, 1, (length, length))
    causal = posr <= posc

    def one(seq, carry):
        for dc, dy, rows in blocks_of(slots):
            xseq[rows, :] = (xa, xb)[dc][pl.ds(block_rows(core, seq, dc, dy, slots), slots), :]
        low = turn(dot(xseq[...], wqkv[...]), cosines[...], sines[...]).astype(BF)
        qkv[seq] = low
        one_q, two_q, k, v = heads_of(low)
        allowed = causal & (posr < lens[seq])
        mixed = [dot(probabilities(q, k, allowed).astype(BF), v) for q in (one_q, two_q)]
        out = jnp.concatenate(mixed, axis=1).astype(BF)
        for dc, dy, rows in blocks_of(slots):
            att[dc, pl.ds(block_rows(core, seq, dc, dy, slots), slots), :] = out[rows]
        return carry

    lax.fori_loop(0, 4, one, 0)


def project_kernel(att, full, wout, mine, theirs):
    fetch_out(full, wout)
    theirs[...] = dot(att[1], wout[...]).astype(BF)
    mine[...] = dot(att[0], wout[...]).astype(BF)


def attention_back_kernel(
    meta, lens, spans, ga, gb, att, wout, wqkv, qkv, xa, xb, cos_table, sin_table,
    mine, theirs, u0, u1, u2, u3, g_pre, gseq, cosines, sines, out_grad
):
    core, ctx = meta[4], meta[5]
    slots = ga.shape[0] // 8
    length = gseq.shape[0]
    held = spans_of(spans, ctx)
    rotary_rows(held, cos_table, cosines)
    rotary_rows(held, sin_table, sines)
    posc = along(held, length, 0, (length, length))
    posr = along(held, length, 1, (length, length))
    causal = posr <= posc

    def one(seq, carry):
        for dc, dy, rows in blocks_of(slots):
            gseq[rows, :] = (ga, gb)[dc][pl.ds(block_rows(core, seq, dc, dy, slots), slots), :]
        g_att = dot(gseq[...], wout[...], RIGHT_T).astype(BF)
        one_q, two_q, k, v = heads_of(qkv[seq])
        allowed = causal & (posr < lens[seq])
        g_q, g_k, g_v = [], 0.0, 0.0
        for q, g in zip((one_q, two_q), heads_of(g_att)):
            p = probabilities(q, k, allowed)
            g_p = dot(g, v, RIGHT_T)
            g_s = (p * (g_p - jnp.sum(p * g_p, axis=-1, keepdims=True))).astype(BF)
            g_q.append(dot(g_s, k) * scale)
            g_k = g_k + dot(g_s, q, LEFT_T) * scale
            g_v = g_v + dot(p.astype(BF), g, LEFT_T)
        full = jnp.concatenate(g_q + [g_k, g_v], axis=1)
        out = turn(full, cosines[...], -sines[...]).astype(BF)
        for dc, dy, rows in blocks_of(slots):
            g_pre[dc, pl.ds(block_rows(core, seq, dc, dy, slots), slots), :] = out[rows]
        return carry

    lax.fori_loop(0, 4, one, 0)
    out_grad[...] = (dot(att[0], ga[...], LEFT_T) + dot(att[1], gb[...], LEFT_T)).astype(BF)
    step = xa.shape[1] // 4
    block = u0.shape[1]
    count = out_grad.shape[1] // block
    low = out_grad.shape[0] // 4
    for s, u in enumerate((u0, u1, u2, u3)):
        at = pl.ds(pl.multiple_of(meta[s] * step, step), step)
        u[:step, :] = (dot(xa[:, at], g_pre[0], LEFT_T) + dot(xb[:, at], g_pre[1], LEFT_T)).astype(BF)
        at = pl.ds(pl.multiple_of(meta[s] * low, low), low)
        for k in range(count):
            u[step + k * low : step + (k + 1) * low, :] = out_grad[at, k * block : (k + 1) * block]
    theirs[...] = dot(g_pre[1], wqkv[...], RIGHT_T).astype(BF)
    mine[...] = dot(g_pre[0], wqkv[...], RIGHT_T).astype(BF)


def mlp_kernel(
    meta, ma, mb, ea, eb, wgu, d0, d1, d2, d3, d4, d5, down_mine, down_theirs, mine, theirs, hidden, g_gu, wdown
):
    half = wgu.shape[1] // 2
    assemble(meta, (d0, d1, d2, d3, d4, d5), wdown)
    for part, x, g, down, back in ((1, mb, eb, down_theirs, theirs), (0, ma, ea, down_mine, mine)):
        gate_up = dot(x[...], wgu[...])
        gate, up = gate_up[:, :half], gate_up[:, half:]
        sig = 1.0 / (1.0 + jnp.exp(-gate))
        act = gate * sig
        hid = (act * up).astype(BF)
        hidden[part] = hid
        g_hidden = dot(g[...], wdown[...], RIGHT_T)
        g_gu[part, :, :half] = (g_hidden * up * sig * (1.0 + gate * (1.0 - sig))).astype(BF)
        g_gu[part, :, half:] = (g_hidden * act).astype(BF)
        down[...] = dot(hid, wdown[...]).astype(BF)
        back[...] = dot(g_gu[part], wgu[...], RIGHT_T).astype(BF)


def mlp_grad_kernel(ma, mb, ea, eb, hidden, g_gu, u):
    nz, _, wide = u.shape
    piece = ma.shape[1] // nz
    step = hidden.shape[2] // nz
    for z in range(nz):
        at = slice(z * piece, (z + 1) * piece)
        both = dot(ma[:, at], g_gu[0], LEFT_T) + dot(mb[:, at], g_gu[1], LEFT_T)
        u[z, :piece, :] = both.astype(BF)
        at = slice(z * step, (z + 1) * step)
        both = (dot(hidden[0, :, at], ea[...], LEFT_T) + dot(hidden[1, :, at], eb[...], LEFT_T)).astype(BF)
        u[z, piece : piece + step, :] = both[:, :wide]
        rest = both.shape[1] - wide
        u[z, piece + step :, :rest] = both[: step // 2, wide:]
        u[z, piece + step :, rest:] = both[step // 2 :, wide:]


def unpack_down_kernel(u, out):
    step, wide = out.shape[0], u.shape[1]
    rest = out.shape[1] - wide
    out[:, :wide] = u[:step, :].astype(F32)
    out[: step // 2, wide:] = u[step:, :rest].astype(F32)
    out[step // 2 :, wide:] = u[step:, rest:].astype(F32)


def norm_kernel(source, a, b, residual, xhat, inverse):
    r = source[...].astype(F32) + a[...].astype(F32) + b[...].astype(F32)
    inv = lax.rsqrt(jnp.mean(r * r, axis=-1, keepdims=True) + epsilon)
    residual[...] = r
    inverse[...] = inv
    xhat[...] = (r * inv).astype(BF)


def norm_back(g_res, source, inverse, a, b):
    scaled = a[...].astype(F32) + b[...].astype(F32)
    inv = inverse[...]
    unit = source[...].astype(F32) * inv
    back = inv * (scaled - unit * jnp.mean(scaled * unit, axis=-1, keepdims=True))
    return g_res[...].astype(F32) + back


def norm_back_kernel(g_res, source, inverse, a, b, out, low):
    g = norm_back(g_res, source, inverse, a, b)
    out[...] = g
    low[...] = g.astype(BF)


def norm_back_low_kernel(g_res, source, inverse, a, b, low):
    low[...] = norm_back(g_res, source, inverse, a, b).astype(BF)


def rotary_constants(total):
    frequency = rope_base ** (-2.0 * np.arange(HD // 2, dtype=np.float32) / HD).astype(np.float32)
    angles = np.arange(total, dtype=np.float32)[:, None] * frequency[None, :].astype(np.float32)
    c, s = np.cos(angles), np.sin(angles)
    flat, signed = np.concatenate([c, c], 1), np.concatenate([-s, s], 1)
    cosines = np.concatenate([flat] * (GROUP + 1) + [np.ones_like(flat)], 1)
    sines = np.concatenate([signed] * (GROUP + 1) + [np.zeros_like(flat)], 1)
    return jnp.asarray(cosines, F32), jnp.asarray(sines, F32)


def paired(*items):
    return sum(jnp.sum(w.astype(F32) * g, axis=1) for w, g in items)


def on_line(
    hidden_in, lengths, span_order, attn_gain, w_query, w_key, w_value, w_out,
    mlp_gain, w_gate, w_up, w_down, out_grad,
):
    lay = Line()
    _, slots, width = hidden_in.shape
    rows, nz = w_query.shape[0], lay.nz
    tokens, length, own = 16 * slots, 4 * slots, 2 * slots
    go = lengths[0] > 0
    meta = jnp.stack([k.astype(jnp.int32) for k in (*lay.order, lay.c & 1, lay.c)])
    gain, gain_m = attn_gain[None, :], mlp_gain[None, :]
    cos_table, sin_table = rotary_constants(length)

    def halves(x):
        return x.reshape(2, x.shape[0] // 2, width)

    wide = w_gate.shape[1] * 2 // KV
    cut = wide // 2
    tables = [pltpu.VMEM((length, WIDE), F32)] * 2

    def flat(x):
        return x.reshape(-1, width)

    d1 = send(w_down, lay.pair)
    d2 = send(w_down, lay.inner)
    q0 = lay.exchange(
        kernel_call(pack_attention_kernel, shaped(KV, rows, WIDE))((), w_query, w_key, w_value, gain)
    )
    theirs = send(lengths, lay.xflip)
    o0 = send(w_out, lay.place)
    gu_s = kernel_call(pack_mlp_kernel, shaped(KV, rows, wide))((), w_gate, w_up, gain_m)
    xhat, inverse, g_low = kernel_call(
        prepare_kernel, (shaped(own, width), shaped(own, 1, dtype=F32), shaped(own, width))
    )((meta, lengths, span_order), hidden_in.reshape(own, width), out_grad.reshape(own, width))
    q0, d1, d2, theirs, gu_s, xhat, g_low = fence(q0, d1, d2, theirs, gu_s, xhat, g_low)
    d3 = send(d2, lay.outward)
    d4 = send(d1, lay.inner)
    x1 = send(xhat, lay.first)
    attn_piece = jnp.concatenate([q0.reshape(KV * rows, WIDE), stacked_columns(o0, WIDE)], axis=0)
    d3, d4, x1, attn_piece = fence(d3, d4, x1, attn_piece)
    attn_full = lay.spread(attn_piece)

    def gather(xhat, x1, g_low, gu_s):
        gu0 = lay.exchange(gu_s)
        x01 = jnp.stack([xhat, x1])
        x2 = send(x01, lay.second)
        x2, gu0, x01, g_low = fence(x2, gu0, x01, g_low)
        x0123 = jnp.stack([x01, x2])
        x3 = send(x0123, lay.core)
        e1 = send(g_low, lay.first)
        x3, x0123, e1 = fence(x3, x0123, e1)
        e01 = jnp.stack([g_low, e1])
        return x0123, x3, gu0, e01

    xa, xb, gu0, e01 = unit_of_work(go, gather, xhat, x1, g_low, gu_s)
    attn_full, gu0 = fence(attn_full, gu0)
    wgu = lay.spread(gu0.reshape(KV * rows, wide))
    attn_full = attn_full.reshape(nz, -1, WIDE)
    seq_len = jnp.concatenate([lengths, theirs])

    def forward(meta, seq_len, span_order, xa, xb, attn_full, cos_table, sin_table, hidden_in, e01, d4):
        e2 = send(e01, lay.second)
        wqkv, qkv, att = kernel_call(
            attention_kernel,
            (shaped(width, WIDE), shaped(4, length, WIDE), shaped(2, tokens // 2, QW)),
            scratch=[pltpu.VMEM((length, width), BF)] + tables,
        )((meta, seq_len, span_order), flat(xa), flat(xb), attn_full, cos_table, sin_table)
        wqkv, qkv, att, e2 = fence(wqkv, qkv, att, e2)
        wout, mine, other = kernel_call(
            project_kernel, (shaped(QW, width), shaped(tokens // 2, width), shaped(tokens // 2, width))
        )((), att, attn_full)
        got = send(other, lay.core)
        r = halves(plus(mine, got))
        e0123 = jnp.stack([e01, e2])
        r, e0123 = fence(r, e0123)
        got = send(r[1], lay.second)
        e3 = send(e0123, lay.core)
        got, e3, r = fence(got, e3, r)
        r = halves(plus(r[0], got))
        got = send(r[1], lay.first)
        residual, xm0, inverse_m = kernel_call(
            norm_kernel, (shaped(own, width, dtype=F32), shaped(own, width), shaped(own, 1, dtype=F32))
        )((), hidden_in.reshape(own, width), r[0], got)
        m01 = jnp.stack([xm0, send(xm0, lay.first)])
        m01, d4 = fence(m01, d4)
        m2 = send(m01, lay.second)
        d5 = send(d4, lay.outward)
        m2, d5 = fence(m2, d5)
        ma = jnp.stack([m01, m2])
        mb = send(ma, lay.core)
        return wqkv, qkv, att, wout, residual, inverse_m, flat(ma), flat(mb), flat(e0123), flat(e3), d5

    wqkv, qkv, att, wout, residual, inverse_m, ma, mb, ea, eb, d5 = unit_of_work(
        go, forward, meta, seq_len, span_order, xa, xb, attn_full, cos_table, sin_table, hidden_in, e01, d4
    )
    half_rows = shaped(tokens // 2, width)
    down_mine, down_other, mine, other, hidden, g_gu = kernel_call(
        mlp_kernel,
        (half_rows, half_rows, half_rows, half_rows, shaped(2, tokens // 2, cut), shaped(2, tokens // 2, wide)),
        scratch=[pltpu.VMEM((cut, width), BF)],
    )((meta,), ma, mb, ea, eb, wgu, w_down, d1, d2, d3, d4, d5)
    got = send(other, lay.core)
    low = w_down.shape[0]
    piece = KV * rows + low * width // wide
    u_mlp = kernel_call(mlp_grad_kernel, shaped(nz, piece, wide))((), ma, mb, ea, eb, hidden, g_gu)
    r = plus(mine, got)
    r, u_mlp = fence(r, u_mlp)
    v_mlp = lay.gather_sum(u_mlp.reshape(nz * piece, wide))
    both = KV * rows + QW // nz * width // WIDE

    def backward(
        meta, seq_len, lengths, span_order, r, down_mine, down_other, g_low, residual, inverse_m, att, wqkv, wout, qkv,
        xa, xb, cos_table, sin_table,
    ):
        r = halves(r)
        r = halves(plus(r[0], send(r[1], lay.second)))
        got = send(r[1], lay.first)
        got_down = send(down_other, lay.core)
        g_res2, h0 = kernel_call(
            norm_back_kernel, (shaped(own, width, dtype=F32), shaped(own, width))
        )((), g_low, residual, inverse_m, r[0], got)
        ga, gb = lay.plane_tokens(h0)
        d = halves(plus(down_mine, got_down))
        ga, gb, d = fence(ga, gb, d)
        got_down = send(d[1], lay.second)
        mine, other, u0, u1, u2, u3 = kernel_call(
            attention_back_kernel,
            [half_rows, half_rows] + [shaped(both, WIDE)] * nz,
            scratch=[pltpu.VMEM((2, tokens // 2, WIDE), BF), pltpu.VMEM((length, width), BF)]
            + tables
            + [pltpu.VMEM((QW, width), BF)],
        )(
            (meta, seq_len, span_order), ga, gb, att, wout, wqkv, qkv, flat(xa), flat(xb), cos_table, sin_table
        )
        got_down, mine, other, u0, u1, u2, u3 = fence(got_down, mine, other, u0, u1, u2, u3)
        c5 = send(u3, lay.inward)
        got = send(other, lay.core)
        d = halves(plus(d[0], got_down))
        got_down = send(d[1], lay.first)
        c5, got, d, got_down = fence(c5, got, d, got_down)
        c4 = send(plus(u3, c5), lay.inner)
        c3 = send(u2, lay.inward)
        r = halves(plus(mine, got))
        got = send(r[1], lay.second)
        block_out = kernel_call(finish_kernel, shaped(own, width))(
            (meta, lengths, span_order), residual, d[0], got_down
        )
        c4, c3, r, got, block_out = fence(c4, c3, r, got, block_out)
        r = halves(plus(r[0], got))
        return g_res2, block_out, r[0], r[1], plus(u1, c4), plus(u2, c3), u0

    g_res2, block_out, ra, rb, c4, c3, c0 = unit_of_work(
        go, backward, meta, seq_len, lengths, span_order, r, down_mine, down_other, g_low, residual, inverse_m, att, wqkv,
        wout, qkv, xa, xb, cos_table, sin_table,
    )
    c4, v_mlp = fence(c4, v_mlp)
    c1 = send(c4, lay.pair)
    c2 = send(c3, lay.inner)
    got = send(rb, lay.first)
    v_gu = lay.exchange(v_mlp[: KV * rows].reshape(KV, rows, wide))
    grad_down = kernel_call(unpack_down_kernel, shaped(low, width, dtype=F32))((), v_mlp[KV * rows :])
    c1, c2, got, v_gu, grad_down = fence(c1, c2, got, v_gu, grad_down)
    v = plus(plus(c0, c1), c2)
    v_qkv = lay.exchange(v[: KV * rows].reshape(KV, rows, WIDE))
    v_out = jnp.concatenate(list(v[KV * rows :].reshape(width // WIDE, -1, WIDE)), axis=1)
    grad_out = send(v_out, lay.back)
    grad_in = kernel_call(norm_back_low_kernel, shaped(own, width))(
        (), g_res2, hidden_in.reshape(own, width), inverse, ra, got
    )
    grad_gate, grad_up, total_m = kernel_call(
        unpack_mlp_kernel, (shaped(*w_gate.shape, dtype=F32), shaped(*w_up.shape, dtype=F32), shaped(1, rows, dtype=F32))
    )((), v_gu, w_gate, w_up, gain_m)
    grad_out, v_qkv, grad_in, grad_gate, grad_up, total_m = fence(
        grad_out, v_qkv, grad_in, grad_gate, grad_up, total_m
    )
    grad_query, grad_key, grad_value, total = kernel_call(
        unpack_attention_kernel,
        tuple(shaped(*w.shape, dtype=F32) for w in (w_query, w_key, w_value)) + (shaped(1, rows, dtype=F32),),
    )((), v_qkv, w_query, w_key, w_value, gain)
    return (
        block_out.reshape(hidden_in.shape), grad_in.reshape(hidden_in.shape), total[0], grad_query, grad_key, grad_value,
        grad_out.astype(F32), total_m[0], grad_gate, grad_up, grad_down,
    )


def anywhere(
    hidden_in, lengths, span_order, attn_gain, w_query, w_key, w_value, w_out,
    mlp_gain, w_gate, w_up, w_down, out_grad,
):
    lay = Layout()
    micro, slots, width = hidden_in.shape
    rows, nz = w_query.shape[0], lay.nz
    gain = attn_gain.astype(F32)[:, None]
    gain_m = mlp_gain.astype(F32)[:, None]
    pos = jnp.concatenate([positions_of(span_order, k, slots) for k in range(lay.ctx)])
    usable = (positions_of(span_order, lay.c, slots)[None, :] < lengths[:, None]).astype(F32)[..., None]
    cosines, sines = rope_tables(pos)
    length = slots * lay.ctx

    def tokens(x):
        return lax.all_gather(x, "ctx", axis=1, tiled=True).reshape(micro * length, width)

    def own(x):
        x = x.astype(BF).reshape(micro, length, width)
        return lax.psum_scatter(x, "ctx", scatter_dimension=1, tiled=True).astype(F32)

    spread, collect = lay.spread, lay.gather_sum
    wqkv = spread(lay.exchange(pack_attention(w_query, w_key, w_value, gain)).reshape(KV * rows, -1))
    wgu = spread(lay.exchange(pack_mlp(w_gate, w_up, gain_m, nz)).reshape(KV * rows, -1))
    wout = spread(send(w_out, lay.place))
    wdown = spread(w_down)
    source = hidden_in.astype(F32)
    unit, inverse = unit_rows(source)
    xs = tokens(unit.astype(BF))
    g_res = out_grad.astype(F32) * usable
    g_mlp = tokens(g_res.astype(BF))
    pre = mm(xs, wqkv).reshape(micro, length, -1)
    attended, kept = attend(pre, pos, lengths, cosines, sines)
    att = attended.reshape(micro * length, QW)
    residual = source + own(mm(att, wout))
    unit_m, inverse_m = unit_rows(residual)
    xm = tokens(unit_m.astype(BF))
    gate_up = mm(xm, wgu)
    hidden = swiglu(gate_up)
    block_out = (usable * (residual + own(mm(hidden, wdown)))).astype(BF)
    grad_down = collect(mm_lt(hidden, g_mlp)).astype(F32)
    g_gu = swiglu_back(gate_up, mm_rt(g_mlp, wdown))
    v_gu = lay.exchange(collect(mm_lt(xm, g_gu)).reshape(KV, rows, -1))
    u_gate, u_up = unpack_mlp(v_gu, nz)
    g_res2 = g_res + unit_back(own(mm_rt(g_gu, wgu)), unit_m, inverse_m)
    g_branch = tokens(g_res2.astype(BF))
    grad_out = send(collect(mm_lt(att, g_branch)), lay.back).astype(F32)
    g_att = mm_rt(g_branch, wout).astype(BF).reshape(micro, length, QW)
    g_pre = attend_back(g_att, kept, cosines, sines).reshape(micro * length, -1)
    v_qkv = lay.exchange(collect(mm_lt(xs, g_pre)).reshape(KV, rows, -1))
    u_q, u_k, u_v = unpack_attention(v_qkv)
    grad_in = (g_res2 + unit_back(own(mm_rt(g_pre, wqkv)), unit, inverse)).astype(BF)
    return (
        block_out, grad_in, paired((w_query, u_q), (w_key, u_k), (w_value, u_v)),
        u_q * gain, u_k * gain, u_v * gain, grad_out,
        paired((w_gate, u_gate), (w_up, u_up)), u_gate * gain_m, u_up * gain_m, grad_down,
    )


def solution(mesh):
    rows = P(AXES, None)
    tokens = P("fsdp", "ctx", None)
    line = mesh.shape["ctx"] == 4 and mesh.shape["fsdp"] == 8
    return jax.shard_map(
        on_line if line else anywhere,
        mesh=mesh,
        in_specs=(tokens, P("fsdp"), P(), P(AXES), rows, rows, rows, rows, P(AXES), rows, rows, rows, tokens),
        out_specs=(tokens, tokens, P(AXES), rows, rows, rows, rows, P(AXES), rows, rows, rows),
        check_vma=False,
    )
```

```python
import jax
import jax.numpy as jnp
import numpy as np
from jax import lax
from jax.experimental import pallas as pl
from jax.experimental.pallas import tpu as pltpu
from jax.sharding import PartitionSpec as P

H = 16
KV = 8
HD = 96
GROUP = H // KV
QW = GROUP * HD
AXES = ("fsdp", "ctx")

epsilon = 1e-05
rope_base = 100000.0
masked_score = -1e30
scale = HD ** (-0.5)
BF = jnp.bfloat16
F32 = jnp.float32


def mm(left, right):
    return jnp.dot(left, right, preferred_element_type=F32)


def mm_lt(left, right):
    return lax.dot_general(left, right, (((0,), (0,)), ((), ())), preferred_element_type=F32)


def mm_rt(left, right):
    return lax.dot_general(left, right, (((1,), (1,)), ((), ())), preferred_element_type=F32)


def plus(a, b):
    return a + b


def send(x, pairs):
    return lax.ppermute(x, AXES, pairs)


def unit_of_work(go, body, *args):
    def idle(*args):
        return jax.tree.map(lambda leaf: jnp.zeros(leaf.shape, leaf.dtype), jax.eval_shape(body, *args))

    return lax.cond(go, body, idle, *args)


def fence(*items):
    return lax.optimization_barrier(items)


class Layout:
    def __init__(self):
        self.ctx = lax.axis_size("ctx")
        self.fsdp = lax.axis_size("fsdp")
        self.tpf = KV // self.ctx
        self.nz = self.fsdp // self.tpf
        self.total = self.fsdp * self.ctx
        self.fast = self.ctx == 4 and self.tpf == 2 and self.nz == 4
        self.f = lax.axis_index("fsdp")
        self.c = lax.axis_index("ctx")
        self.z = self.f // self.tpf
        self.place = [(b, (b % self.nz) * KV + b // self.nz) for b in range(self.total)]
        self.back = [(d, s) for s, d in self.place]

    def exchange(self, x):
        if self.tpf == 1:
            return lax.all_to_all(x, "ctx", split_axis=0, concat_axis=0, tiled=True)
        groups = [[z * KV + i for i in range(KV)] for z in range(self.nz)]
        return lax.all_to_all(
            x, AXES, split_axis=0, concat_axis=0, tiled=True, axis_index_groups=groups
        )

    def lines(self):
        return [[z * KV + i for z in range(self.nz)] for i in range(KV)]

    def spread(self, x):
        if self.tpf == 1:
            return lax.all_gather(x, "fsdp", axis=0, tiled=True)
        return lax.all_gather(x, AXES, axis=0, tiled=True, axis_index_groups=self.lines())

    def gather_sum(self, x):
        x = x.astype(BF)
        if self.tpf == 1:
            return lax.psum_scatter(x, "fsdp", scatter_dimension=0, tiled=True)
        return lax.psum_scatter(
            x, AXES, scatter_dimension=0, tiled=True, axis_index_groups=self.lines()
        )


class Line(Layout):
    def __init__(self):
        super().__init__()
        total = self.total
        self.core = [(d, d ^ 1) for d in range(total)]
        self.first = [(d, d ^ (2 if d & 1 else 4)) for d in range(total)]
        self.second = [(d, d ^ (4 if d & 1 else 2)) for d in range(total)]
        self.xflip = [(d, d ^ 4) for d in range(total)]

        def planes(pairs):
            return [(s * KV + i, d * KV + i) for s, d in pairs for i in range(KV)]

        self.pair = planes([(0, 1), (1, 0), (2, 3), (3, 2)])
        self.inner = planes([(1, 2), (2, 1)])
        self.outward = planes([(1, 0), (2, 3)])
        self.inward = planes([(0, 1), (3, 2)])
        z = self.z
        low = z < 2
        self.order = [z, z ^ 1, jnp.where(low, 2, 1), jnp.where(low, 3, 0)]
        table = ((0, 1, 3, 3), (1, 0, 2, 2), (2, 2, 0, 1), (3, 3, 1, 0))
        self.slot = [
            jnp.where(z == 0, r[0], jnp.where(z == 1, r[1], jnp.where(z == 2, r[2], r[3])))
            for r in table
        ]

    def take_columns(self, x, blocks):
        width = x.shape[-1] // self.nz
        return jnp.concatenate(
            [lax.dynamic_slice_in_dim(x, k * width, width, axis=-1) for k in blocks], axis=-1
        )

    def take_rows(self, pieces):
        full = jnp.stack(pieces)
        return jnp.concatenate(
            [lax.dynamic_index_in_dim(full, k, axis=0, keepdims=False) for k in self.slot], axis=0
        )

    def to_pieces(self, x):
        full = x.reshape((self.nz, x.shape[0] // self.nz) + x.shape[1:])
        return [lax.dynamic_index_in_dim(full, k, axis=0, keepdims=False) for k in self.order]

    def all_tokens(self, x):
        x = jnp.stack([x, send(x, self.first)])
        x = jnp.stack([x, send(x, self.second)])
        x = jnp.stack([x, send(x, self.core)])
        return x.reshape(-1, x.shape[-1])

    def plane_tokens(self, x):
        x = jnp.stack([x, send(x, self.first)])
        x = jnp.stack([x, send(x, self.second)])
        other = send(x, self.core)
        return x.reshape(-1, x.shape[-1]), other.reshape(-1, x.shape[-1])

    def collect_tokens(self, x, slots):
        x = x.reshape(2, 2, 2, 2, slots, x.shape[-1])
        x = plus(x[0], send(x[1], self.core))
        x = plus(x[0], send(x[1], self.second))
        return x[0].astype(F32) + send(x[1], self.first).astype(F32)

    def to_seqs(self, x, slots):
        x = x.reshape(2, 2, 2, 2, slots, x.shape[-1])
        halves = []
        for dc in range(2):
            even = ((self.c & 1) ^ dc) == 0
            h = x[dc]
            halves.append(jnp.where(even, jnp.swapaxes(h, 0, 1), h))
        x = jnp.stack(halves, axis=0)
        x = jnp.transpose(x, (1, 3, 0, 2, 4, 5))
        return x.reshape(4, 4 * slots, x.shape[-1])

    def from_seqs(self, x, slots):
        x = x.reshape(2, 2, 2, 2, slots, x.shape[-1])
        x = jnp.transpose(x, (2, 0, 3, 1, 4, 5))
        halves = []
        for dc in range(2):
            even = ((self.c & 1) ^ dc) == 0
            h = x[dc]
            halves.append(jnp.where(even, jnp.swapaxes(h, 0, 1), h))
        return jnp.stack(halves, axis=0).reshape(16 * slots, x.shape[-1])


def positions_of(span_order, index, slots):
    span_len = slots // 2
    at = jnp.arange(slots, dtype=jnp.int32)
    pair = lax.dynamic_slice_in_dim(span_order, 2 * index, 2)
    return jnp.where(at < span_len, pair[0], pair[1]) * span_len + at % span_len


def rope_tables(pos):
    frequency = rope_base ** (-2.0 * jnp.arange(HD // 2, dtype=F32) / HD)
    angles = pos.astype(F32)[:, None] * frequency[None, :]
    return jnp.cos(angles), jnp.sin(angles)


def rotate(v, cosines, sines):
    half = HD // 2
    co, si = cosines[None, :, None, :], sines[None, :, None, :]
    one, two = v[..., :half], v[..., half:]
    return jnp.concatenate([one * co - two * si, two * co + one * si], axis=-1)


def unit_rows(x):
    inverse = lax.rsqrt(jnp.mean(x * x, axis=-1, keepdims=True) + epsilon)
    return x * inverse, inverse


def unit_back(scaled, unit, inverse):
    return inverse * (scaled - unit * jnp.mean(scaled * unit, axis=-1, keepdims=True))


def attend(pre, pos, seq_len, cosines, sines):
    seqs, length, _ = pre.shape
    q = rotate(pre[..., :QW].reshape(seqs, length, GROUP, HD), cosines, sines).astype(BF)
    k = rotate(pre[..., QW : QW + HD].reshape(seqs, length, 1, HD), cosines, sines)[:, :, 0].astype(BF)
    v = pre[..., QW + HD :].astype(BF)
    allowed = (pos[None, None, :] <= pos[None, :, None]) & (
        pos[None, None, :] < seq_len[:, None, None]
    )
    scores = jnp.einsum("sqgd,snd->sgqn", q, k, preferred_element_type=F32) * scale
    scores = jnp.where(allowed[:, None], scores, masked_score)
    top = jnp.max(scores, axis=-1, keepdims=True)
    expo = jnp.exp(scores - top)
    probs = expo / jnp.sum(expo, axis=-1, keepdims=True)
    low = probs.astype(BF)
    attended = jnp.einsum("sgqn,snd->sqgd", low, v, preferred_element_type=F32)
    return attended.astype(BF).reshape(seqs, length, QW), (q, k, v, probs, low)


def attend_back(g_att, kept, cosines, sines):
    q, k, v, probs, low = kept
    seqs, length, _ = g_att.shape
    g_att = g_att.reshape(seqs, length, GROUP, HD)
    g_probs = jnp.einsum("sqgd,snd->sgqn", g_att, v, preferred_element_type=F32)
    inner = jnp.sum(probs * g_probs, axis=-1, keepdims=True)
    g_scores = (probs * (g_probs - inner)).astype(BF)
    g_q = jnp.einsum("sgqn,snd->sqgd", g_scores, k, preferred_element_type=F32) * scale
    g_k = jnp.einsum("sgqn,sqgd->snd", g_scores, q, preferred_element_type=F32) * scale
    g_v = jnp.einsum("sgqn,sqgd->snd", low, g_att, preferred_element_type=F32)
    return jnp.concatenate(
        [
            rotate(g_q, cosines, -sines).astype(BF).reshape(seqs, length, QW),
            rotate(g_k[:, :, None], cosines, -sines).astype(BF)[:, :, 0],
            g_v.astype(BF),
        ],
        axis=-1,
    )


def swiglu(gate_up):
    half = gate_up.shape[-1] // 2
    gate, up = gate_up[:, :half], gate_up[:, half:]
    return (jax.nn.silu(gate) * up).astype(BF)


def swiglu_back(gate_up, g_hidden):
    half = gate_up.shape[-1] // 2
    gate, up = gate_up[:, :half], gate_up[:, half:]
    sig = jax.nn.sigmoid(gate)
    g_gate = (g_hidden * up * sig * (1.0 + gate * (1.0 - sig))).astype(BF)
    g_up = (g_hidden * gate * sig).astype(BF)
    return jnp.concatenate([g_gate, g_up], axis=-1)


def pack_attention(w_query, w_key, w_value, gain):
    rows = w_query.shape[0]
    parts = [
        (w.astype(F32) * gain).astype(BF).reshape(rows, KV, w.shape[1] // KV)
        for w in (w_query, w_key, w_value)
    ]
    return jnp.transpose(jnp.concatenate(parts, axis=2), (1, 0, 2))


def unpack_attention(u):
    u = jnp.transpose(u, (1, 0, 2)).astype(F32)
    rows = u.shape[0]
    return (
        u[..., :QW].reshape(rows, KV * QW),
        u[..., QW : QW + HD].reshape(rows, KV * HD),
        u[..., QW + HD :].reshape(rows, KV * HD),
    )


def pack_mlp(w_gate, w_up, gain, nz):
    rows = w_gate.shape[0]

    def columns(w):
        w = (w.astype(F32) * gain).astype(BF).reshape(rows, nz, KV, -1)
        return jnp.transpose(w, (2, 0, 1, 3)).reshape(KV, rows, -1)

    return jnp.concatenate([columns(w_gate), columns(w_up)], axis=2)


def unpack_mlp(u, nz):
    rows = u.shape[1]
    u = u.reshape(KV, rows, 2, nz, -1)
    u = jnp.transpose(u, (2, 1, 3, 0, 4)).reshape(2, rows, -1).astype(F32)
    return u[0], u[1]


SMEM = pl.BlockSpec(memory_space=pltpu.SMEM)
VMEM = pl.BlockSpec(memory_space=pltpu.VMEM)
WIDE = QW + 2 * HD
FREE = pl.CostEstimate(flops=0, bytes_accessed=0, transcendentals=0)
ROOM = pltpu.CompilerParams(vmem_limit_bytes=56 * 1024 * 1024)


def shaped(*shape, dtype=BF):
    return jax.ShapeDtypeStruct(shape, dtype)


def kernel_call(body, outs, scratch=()):
    def call(scalars, *arrays):
        return pl.pallas_call(
            body,
            out_shape=outs,
            in_specs=[SMEM] * len(scalars) + [VMEM] * len(arrays),
            out_specs=jax.tree.map(lambda _: VMEM, outs),
            scratch_shapes=list(scratch),
            compiler_params=ROOM,
            cost_estimate=FREE,
        )(*scalars, *arrays)

    return call


def moving_call(body, outs, scratch=(), copies=1):
    def call(scalars, *arrays):
        anywhere_spec = pl.BlockSpec(memory_space=pl.ANY)
        return pl.pallas_call(
            body,
            out_shape=outs,
            in_specs=[SMEM] * len(scalars) + [pl.BlockSpec(memory_space=pltpu.HBM)] * len(arrays),
            out_specs=jax.tree.map(lambda _: anywhere_spec, outs),
            scratch_shapes=list(scratch) + [pltpu.SemaphoreType.DMA((copies,))],
            compiler_params=ROOM,
            cost_estimate=FREE,
        )(*scalars, *arrays)

    return call


class Copies:
    def __init__(self, sems):
        self.sems = sems
        self.used = 0

    def start(self, source, target):
        copy = pltpu.make_async_copy(source, target, self.sems.at[self.used])
        self.used += 1
        copy.start()
        return copy


def vmem(*arrays):
    return [pltpu.VMEM(a.shape, a.dtype) for a in arrays]


def dot(a, b, dims=((1,), (0,))):
    return lax.dot_general(a, b, (dims, ((), ())), preferred_element_type=F32)


LEFT_T = ((0,), (0,))
RIGHT_T = ((1,), (1,))


def block_rows(core, seq, dc, dy, slots):
    dx, m = seq // 2, seq % 2
    even = (core ^ dc) == 0
    s1 = jnp.where(even, dx, dy)
    s2 = jnp.where(even, dy, dx)
    return pl.multiple_of(((s2 * 2 + s1) * 2 + m) * slots, slots)


def blocks_of(slots):
    for dc in range(2):
        for dy in range(2):
            b = dc * 2 + dy
            yield dc, dy, slice(b * slots, (b + 1) * slots)


def spans_of(spans, ctx):
    out = []
    for dc in range(2):
        for dy in range(2):
            other = ctx ^ (dy * 2 + dc)
            out += [spans[2 * other], spans[2 * other + 1]]
    return out


def along(held, length, axis, shape):
    at = lax.broadcasted_iota(jnp.int32, shape, axis) % length
    step = length // len(held)
    pos = at % step
    for i, span in enumerate(held):
        pos = pos + jnp.where(at // step == i, span * step, 0)
    return pos


def rotary_rows(held, table, out):
    step = out.shape[0] // len(held)
    for i, span in enumerate(held):
        out[i * step : (i + 1) * step, :] = table[pl.ds(pl.multiple_of(span * step, step), step), :]


def rotary_copies(copies, held, table, out):
    step = out.shape[0] // len(held)
    return [
        copies.start(table.at[pl.ds(pl.multiple_of(span * step, step), step)], out.at[pl.ds(i * step, step)])
        for i, span in enumerate(held)
    ]


def turn(x, cosines, sines):
    half, width = HD // 2, x.shape[1]
    lane = lax.broadcasted_iota(jnp.int32, x.shape, 1) % HD
    partner = jnp.where(lane < half, pltpu.roll(x, width - half, 1), pltpu.roll(x, half, 1))
    return x * cosines + partner * sines


def probabilities(q, k, allowed):
    scores = jnp.where(allowed, dot(q, k, RIGHT_T) * scale, masked_score)
    expo = jnp.exp(scores - jnp.max(scores, axis=-1, keepdims=True))
    return expo / jnp.sum(expo, axis=-1, keepdims=True)


def heads_of(x):
    return [x[:, h * HD : (h + 1) * HD] for h in range(x.shape[1] // HD)]


def assemble(meta, pieces, out):
    p0, p1, p2, p3, p4, p5 = pieces
    step = p0.shape[0]
    for s, parts in enumerate(((p0,), (p1,), (p2, p3), (p4, p5))):
        piece = parts[0][...]
        if len(parts) > 1:
            piece = piece + parts[1][...]
        out[pl.ds(pl.multiple_of(meta[s] * step, step), step), :] = piece


def fetch_qkv(full, out):
    step = full.shape[2]
    for z in range(full.shape[0]):
        out[z * step : (z + 1) * step, :] = full[z, :step, :]


def fetch_out(full, out):
    nz, total, step = full.shape
    count = out.shape[1] // step
    rows = (total - step) // count
    for z in range(nz):
        for k in range(count):
            out[z * rows : (z + 1) * rows, k * step : (k + 1) * step] = full[
                z, step + k * rows : step + (k + 1) * rows, :
            ]


def stacked_columns(x, cut):
    return jnp.concatenate([x[:, k : k + cut] for k in range(0, x.shape[1], cut)], axis=0)


def column(row):
    n = row.shape[1]
    same = lax.broadcasted_iota(jnp.int32, (n, n), 0) == lax.broadcasted_iota(jnp.int32, (n, n), 1)
    return jnp.sum(jnp.where(same, row, 0.0), axis=1, keepdims=True)


def row_of(col):
    n = col.shape[0]
    same = lax.broadcasted_iota(jnp.int32, (n, n), 0) == lax.broadcasted_iota(jnp.int32, (n, n), 1)
    return jnp.sum(jnp.where(same, col, 0.0), axis=0, keepdims=True)


def pack_attention_kernel(wq, wk, wv, gain, out):
    g = column(gain[...].astype(F32))
    q, k, v = ((w[...].astype(F32) * g).astype(BF) for w in (wq, wk, wv))
    for j in range(KV):
        out[j, :, :QW] = q[:, j * QW : (j + 1) * QW]
        out[j, :, QW : QW + HD] = k[:, j * HD : (j + 1) * HD]
        out[j, :, QW + HD :] = v[:, j * HD : (j + 1) * HD]


def pack_mlp_kernel(wg, wu, gain, out):
    g = column(gain[...].astype(F32))
    half = out.shape[2] // 2
    blocks = 4
    hid = half // blocks
    for h, w in enumerate((wg, wu)):
        x = (w[...].astype(F32) * g).astype(BF)
        for z in range(blocks):
            for j in range(KV):
                out[j, :, h * half + z * hid : h * half + (z + 1) * hid] = x[
                    :, (z * KV + j) * hid : (z * KV + j + 1) * hid
                ]


def unpack_attention_kernel(u, wq, wk, wv, gain, gq, gk, gv, total):
    g = column(gain[...].astype(F32))
    acc = jnp.zeros(g.shape, F32)
    for j in range(KV):
        x = u[j].astype(F32)
        for w, out, lo, n in ((wq, gq, 0, QW), (wk, gk, QW, HD), (wv, gv, QW + HD, HD)):
            part = x[:, lo : lo + n]
            out[:, j * n : (j + 1) * n] = part * g
            acc += jnp.sum(part * w[:, j * n : (j + 1) * n].astype(F32), axis=1, keepdims=True)
    total[...] = row_of(acc)


def unpack_mlp_kernel(u, wg, wu, gain, gg, gu, total):
    g = column(gain[...].astype(F32))
    acc = jnp.zeros(g.shape, F32)
    half = wg.shape[1] // KV
    blocks = 4
    hid = half // blocks
    for j in range(KV):
        x = u[j].astype(F32)
        for h, (w, out) in enumerate(((wg, gg), (wu, gu))):
            for z in range(blocks):
                at = slice((z * KV + j) * hid, (z * KV + j + 1) * hid)
                part = x[:, h * half + z * hid : h * half + (z + 1) * hid]
                out[:, at] = part * g
                acc += jnp.sum(part * w[:, at].astype(F32), axis=1, keepdims=True)
    total[...] = row_of(acc)


def usable_rows(lens, spans, ctx, shape):
    at = lax.broadcasted_iota(jnp.int32, shape, 0)
    slots = shape[0] // 2
    slot, step = at % slots, slots // 2
    pos = jnp.where(slot < step, spans[2 * ctx], spans[2 * ctx + 1]) * step + slot % step
    length = jnp.where(at < slots, lens[0], lens[1])
    return (pos < length).astype(F32)


def prepare_kernel(meta, lens, spans, x, g, xhat, inverse, g_low):
    v = x[...].astype(F32)
    inv = lax.rsqrt(jnp.mean(v * v, axis=-1, keepdims=True) + epsilon)
    inverse[...] = inv
    xhat[...] = (v * inv).astype(BF)
    g_low[...] = (g[...].astype(F32) * usable_rows(lens, spans, meta[5], inverse.shape)).astype(BF)


def finish_kernel(meta, lens, spans, residual, a, b, out):
    total = residual[...] + a[...].astype(F32) + b[...].astype(F32)
    out[...] = (total * usable_rows(lens, spans, meta[5], (total.shape[0], 1))).astype(BF)


def attention_kernel(
    meta, lens, spans, xa, xb, full, cos_table, sin_table, wqkv, qkv, att, xseq, cosines, sines
):
    core, ctx = meta[4], meta[5]
    slots = xa.shape[0] // 8
    length = xseq.shape[0]
    fetch_qkv(full, wqkv)
    held = spans_of(spans, ctx)
    rotary_rows(held, cos_table, cosines)
    rotary_rows(held, sin_table, sines)
    posc = along(held, length, 0, (GROUP * length, length))
    posr = along(held, length, 1, (GROUP * length, length))
    causal = posr <= posc

    def one(seq, carry):
        for dc, dy, rows in blocks_of(slots):
            xseq[rows, :] = (xa, xb)[dc][pl.ds(block_rows(core, seq, dc, dy, slots), slots), :]
        low = turn(dot(xseq[...], wqkv[...]), cosines[...], sines[...]).astype(BF)
        qkv[seq] = low
        one_q, two_q, k, v = heads_of(low)
        q = jnp.concatenate([one_q, two_q], axis=0)
        allowed = causal & (posr < lens[seq])
        mixed = dot(probabilities(q, k, allowed).astype(BF), v)
        out = jnp.concatenate([mixed[:length], mixed[length:]], axis=1).astype(BF)
        for dc, dy, rows in blocks_of(slots):
            att[dc, pl.ds(block_rows(core, seq, dc, dy, slots), slots), :] = out[rows]
        return carry

    lax.fori_loop(0, 4, one, 0, unroll=True)


def project_kernel(att, full, wout, mine, theirs):
    fetch_out(full, wout)
    theirs[...] = dot(att[1], wout[...]).astype(BF)
    mine[...] = dot(att[0], wout[...]).astype(BF)


def attention_back_kernel(
    meta, lens, spans,
    h_ga, h_gb, h_att, h_wout, h_wqkv, h_qkv, h_xa, h_xb, cos_table, sin_table,
    o_mine, o_theirs, o0, o1, o2, o3,
    ga, gb, att, wout, wqkv, qkv, xa, xb, mine, theirs, u0, u1, u2, u3, g_pre, gseq, cosines, sines, out_grad, sems,
):
    copies = Copies(sems)
    held = spans_of(spans, meta[5])
    first = [copies.start(h, v) for h, v in ((h_wout, wout), (h_qkv, qkv), (h_ga, ga), (h_gb, gb))]
    first += rotary_copies(copies, held, cos_table, cosines) + rotary_copies(copies, held, sin_table, sines)
    for c in first:
        c.wait()
    later = [copies.start(h, v) for h, v in ((h_xa, xa), (h_xb, xb), (h_att, att), (h_wqkv, wqkv))]
    core, ctx = meta[4], meta[5]
    slots = ga.shape[0] // 8
    length = gseq.shape[0]
    posc = along(held, length, 0, (GROUP * length, length))
    posr = along(held, length, 1, (GROUP * length, length))
    causal = posr <= posc

    def one(seq, carry):
        for dc, dy, rows in blocks_of(slots):
            gseq[rows, :] = (ga, gb)[dc][pl.ds(block_rows(core, seq, dc, dy, slots), slots), :]
        g_att = dot(gseq[...], wout[...], RIGHT_T).astype(BF)
        one_q, two_q, k, v = heads_of(qkv[seq])
        q = jnp.concatenate([one_q, two_q], axis=0)
        g = jnp.concatenate(heads_of(g_att), axis=0)
        allowed = causal & (posr < lens[seq])
        p = probabilities(q, k, allowed)
        g_p = dot(g, v, RIGHT_T)
        g_s = (p * (g_p - jnp.sum(p * g_p, axis=-1, keepdims=True))).astype(BF)
        g_q = dot(g_s, k) * scale
        g_k = dot(g_s, q, LEFT_T) * scale
        g_v = dot(p.astype(BF), g, LEFT_T)
        full = jnp.concatenate([g_q[:length], g_q[length:], g_k, g_v], axis=1)
        out = turn(full, cosines[...], -sines[...]).astype(BF)
        for dc, dy, rows in blocks_of(slots):
            g_pre[dc, pl.ds(block_rows(core, seq, dc, dy, slots), slots), :] = out[rows]
        return carry

    lax.fori_loop(0, 4, one, 0, unroll=True)
    for c in later:
        c.wait()
    gone = []
    out_grad[...] = (dot(att[0], ga[...], LEFT_T) + dot(att[1], gb[...], LEFT_T)).astype(BF)
    step = xa.shape[1] // 4
    block = u0.shape[1]
    count = out_grad.shape[1] // block
    low = out_grad.shape[0] // 4
    for s, u, o in ((3, u3, o3), (2, u2, o2), (1, u1, o1), (0, u0, o0)):
        at = pl.ds(pl.multiple_of(meta[s] * step, step), step)
        u[:step, :] = (dot(xa[:, at], g_pre[0], LEFT_T) + dot(xb[:, at], g_pre[1], LEFT_T)).astype(BF)
        at = pl.ds(pl.multiple_of(meta[s] * low, low), low)
        for k in range(count):
            u[step + k * low : step + (k + 1) * low, :] = out_grad[at, k * block : (k + 1) * block]
        gone.append(copies.start(u, o))
    theirs[...] = dot(g_pre[1], wqkv[...], RIGHT_T).astype(BF)
    gone.append(copies.start(theirs, o_theirs))
    mine[...] = dot(g_pre[0], wqkv[...], RIGHT_T).astype(BF)
    gone.append(copies.start(mine, o_mine))
    for c in gone:
        c.wait()


def mlp_kernel(
    meta,
    h_ma, h_mb, h_ea, h_eb, h_wgu, h0, h1, h2, h3, h4, h5,
    o_down_mine, o_down_theirs, o_mine, o_theirs, o_u,
    ma, mb, ea, eb, wgu, d0, d1, d2, d3, d4, d5, down_mine, down_theirs, mine, theirs, u, hidden, g_gu, wdown, sems,
):
    copies = Copies(sems)
    came = [copies.start(h_wgu, wgu), copies.start(h_mb, mb)]
    pieces = (d0, d1, d2, d3, d4, d5)
    downs = [copies.start(h, d) for h, d in zip((h0, h1, h2, h3, h4, h5), pieces)]
    came_eb = copies.start(h_eb, eb)
    came_ma = copies.start(h_ma, ma)
    came_ea = copies.start(h_ea, ea)
    gone = []
    half = wgu.shape[1] // 2
    for c in came:
        c.wait()
    for part, x, g, down, back, o_down, o_back in (
        (1, mb, eb, down_theirs, theirs, o_down_theirs, o_theirs),
        (0, ma, ea, down_mine, mine, o_down_mine, o_mine),
    ):
        if part == 0:
            came_ma.wait()
        gate_up = dot(x[...], wgu[...])
        gate, up = gate_up[:, :half], gate_up[:, half:]
        sig = 1.0 / (1.0 + jnp.exp(-gate))
        act = gate * sig
        hid = (act * up).astype(BF)
        hidden[part] = hid
        if part == 1:
            for c in downs:
                c.wait()
            assemble(meta, pieces, wdown)
            came_eb.wait()
        else:
            came_ea.wait()
        g_hidden = dot(g[...], wdown[...], RIGHT_T)
        g_gu[part, :, :half] = (g_hidden * up * sig * (1.0 + gate * (1.0 - sig))).astype(BF)
        g_gu[part, :, half:] = (g_hidden * act).astype(BF)
        back[...] = dot(g_gu[part], wgu[...], RIGHT_T).astype(BF)
        gone.append(copies.start(back, o_back))
        down[...] = dot(hid, wdown[...]).astype(BF)
        gone.append(copies.start(down, o_down))
    nz, _, wide = u.shape
    piece = ma.shape[1] // nz
    step = hidden.shape[2] // nz
    for z in range(nz):
        at = slice(z * piece, (z + 1) * piece)
        both = dot(ma[:, at], g_gu[0], LEFT_T) + dot(mb[:, at], g_gu[1], LEFT_T)
        u[z, :piece, :] = both.astype(BF)
        at = slice(z * step, (z + 1) * step)
        both = (dot(hidden[0, :, at], ea[...], LEFT_T) + dot(hidden[1, :, at], eb[...], LEFT_T)).astype(BF)
        u[z, piece : piece + step, :] = both[:, :wide]
        rest = both.shape[1] - wide
        u[z, piece + step :, :rest] = both[: step // 2, wide:]
        u[z, piece + step :, rest:] = both[step // 2 :, wide:]
        gone.append(copies.start(u.at[z], o_u.at[z]))
    for c in gone:
        c.wait()


def unpack_down_kernel(u, out):
    step, wide = out.shape[0], u.shape[1]
    rest = out.shape[1] - wide
    out[:, :wide] = u[:step, :].astype(F32)
    out[: step // 2, wide:] = u[step:, :rest].astype(F32)
    out[step // 2 :, wide:] = u[step:, rest:].astype(F32)


def norm_kernel(source, a, b, residual, xhat, inverse):
    r = source[...].astype(F32) + a[...].astype(F32) + b[...].astype(F32)
    inv = lax.rsqrt(jnp.mean(r * r, axis=-1, keepdims=True) + epsilon)
    residual[...] = r
    inverse[...] = inv
    xhat[...] = (r * inv).astype(BF)


def norm_back(g_res, source, inverse, a, b):
    scaled = a[...].astype(F32) + b[...].astype(F32)
    inv = inverse[...]
    unit = source[...].astype(F32) * inv
    back = inv * (scaled - unit * jnp.mean(scaled * unit, axis=-1, keepdims=True))
    return g_res[...].astype(F32) + back


def norm_back_kernel(g_res, source, inverse, a, b, out, low):
    g = norm_back(g_res, source, inverse, a, b)
    out[...] = g
    low[...] = g.astype(BF)


def norm_back_low_kernel(g_res, source, inverse, a, b, low):
    low[...] = norm_back(g_res, source, inverse, a, b).astype(BF)


def rotary_constants(total):
    frequency = rope_base ** (-2.0 * np.arange(HD // 2, dtype=np.float32) / HD).astype(np.float32)
    angles = np.arange(total, dtype=np.float32)[:, None] * frequency[None, :].astype(np.float32)
    c, s = np.cos(angles), np.sin(angles)
    flat, signed = np.concatenate([c, c], 1), np.concatenate([-s, s], 1)
    cosines = np.concatenate([flat] * (GROUP + 1) + [np.ones_like(flat)], 1)
    sines = np.concatenate([signed] * (GROUP + 1) + [np.zeros_like(flat)], 1)
    return jnp.asarray(cosines, F32), jnp.asarray(sines, F32)


def paired(*items):
    return sum(jnp.sum(w.astype(F32) * g, axis=1) for w, g in items)


def on_line(
    hidden_in, lengths, span_order, attn_gain, w_query, w_key, w_value, w_out,
    mlp_gain, w_gate, w_up, w_down, out_grad,
):
    lay = Line()
    _, slots, width = hidden_in.shape
    rows, nz = w_query.shape[0], lay.nz
    tokens, length, own = 16 * slots, 4 * slots, 2 * slots
    go = lengths[0] > 0
    meta = jnp.stack([k.astype(jnp.int32) for k in (*lay.order, lay.c & 1, lay.c)])
    gain, gain_m = attn_gain[None, :], mlp_gain[None, :]
    cos_table, sin_table = rotary_constants(length)

    def halves(x):
        return x.reshape(2, x.shape[0] // 2, width)

    wide = w_gate.shape[1] * 2 // KV
    cut = wide // 2
    tables = [pltpu.VMEM((length, WIDE), F32)] * 2

    def flat(x):
        return x.reshape(-1, width)

    d1 = send(w_down, lay.pair)
    d2 = send(w_down, lay.inner)
    q0 = lay.exchange(
        kernel_call(pack_attention_kernel, shaped(KV, rows, WIDE))((), w_query, w_key, w_value, gain)
    )
    theirs = send(lengths, lay.xflip)
    o0 = send(w_out, lay.place)
    gu_s = kernel_call(pack_mlp_kernel, shaped(KV, rows, wide))((), w_gate, w_up, gain_m)
    xhat, inverse, g_low = kernel_call(
        prepare_kernel, (shaped(own, width), shaped(own, 1, dtype=F32), shaped(own, width))
    )((meta, lengths, span_order), hidden_in.reshape(own, width), out_grad.reshape(own, width))
    q0, d1, d2, theirs, gu_s, xhat, g_low = fence(q0, d1, d2, theirs, gu_s, xhat, g_low)
    d3 = send(d2, lay.outward)
    d4 = send(d1, lay.inner)
    x1 = send(xhat, lay.first)
    attn_piece = jnp.concatenate([q0.reshape(KV * rows, WIDE), stacked_columns(o0, WIDE)], axis=0)
    d3, d4, x1, attn_piece = fence(d3, d4, x1, attn_piece)
    attn_full = lay.spread(attn_piece)

    def gather(xhat, x1, g_low, gu_s):
        gu0 = lay.exchange(gu_s)
        x01 = jnp.stack([xhat, x1])
        x2 = send(x01, lay.second)
        x2, gu0, x01, g_low = fence(x2, gu0, x01, g_low)
        x0123 = jnp.stack([x01, x2])
        x3 = send(x0123, lay.core)
        e1 = send(g_low, lay.first)
        x3, x0123, e1 = fence(x3, x0123, e1)
        e01 = jnp.stack([g_low, e1])
        return x0123, x3, gu0, e01

    xa, xb, gu0, e01 = unit_of_work(go, gather, xhat, x1, g_low, gu_s)
    attn_full, gu0 = fence(attn_full, gu0)
    wgu = lay.spread(gu0.reshape(KV * rows, wide))
    attn_full = attn_full.reshape(nz, -1, WIDE)
    seq_len = jnp.concatenate([lengths, theirs])

    def forward(meta, seq_len, span_order, xa, xb, attn_full, cos_table, sin_table, hidden_in, e01, d4):
        e2 = send(e01, lay.second)
        wqkv, qkv, att = kernel_call(
            attention_kernel,
            (shaped(width, WIDE), shaped(4, length, WIDE), shaped(2, tokens // 2, QW)),
            scratch=[pltpu.VMEM((length, width), BF)] + tables,
        )((meta, seq_len, span_order), flat(xa), flat(xb), attn_full, cos_table, sin_table)
        wqkv, qkv, att, e2 = fence(wqkv, qkv, att, e2)
        wout, mine, other = kernel_call(
            project_kernel, (shaped(QW, width), shaped(tokens // 2, width), shaped(tokens // 2, width))
        )((), att, attn_full)
        got = send(other, lay.core)
        r = halves(plus(mine, got))
        e0123 = jnp.stack([e01, e2])
        r, e0123 = fence(r, e0123)
        got = send(r[1], lay.second)
        e3 = send(e0123, lay.core)
        got, e3, r = fence(got, e3, r)
        r = halves(plus(r[0], got))
        got = send(r[1], lay.first)
        residual, xm0, inverse_m = kernel_call(
            norm_kernel, (shaped(own, width, dtype=F32), shaped(own, width), shaped(own, 1, dtype=F32))
        )((), hidden_in.reshape(own, width), r[0], got)
        m01 = jnp.stack([xm0, send(xm0, lay.first)])
        m01, d4 = fence(m01, d4)
        m2 = send(m01, lay.second)
        d5 = send(d4, lay.outward)
        m2, d5 = fence(m2, d5)
        ma = jnp.stack([m01, m2])
        mb = send(ma, lay.core)
        return wqkv, qkv, att, wout, residual, inverse_m, flat(ma), flat(mb), flat(e0123), flat(e3), d5

    wqkv, qkv, att, wout, residual, inverse_m, ma, mb, ea, eb, d5 = unit_of_work(
        go, forward, meta, seq_len, span_order, xa, xb, attn_full, cos_table, sin_table, hidden_in, e01, d4
    )
    half_rows = shaped(tokens // 2, width)
    low = w_down.shape[0]
    piece = KV * rows + low * width // wide
    outs = (half_rows, half_rows, half_rows, half_rows, shaped(nz, piece, wide))
    ins = (ma, mb, ea, eb, wgu, w_down, d1, d2, d3, d4, d5)
    down_mine, down_other, mine, other, u_mlp = moving_call(
        mlp_kernel,
        outs,
        scratch=vmem(*ins, *outs)
        + [pltpu.VMEM((2, tokens // 2, cut), BF), pltpu.VMEM((2, tokens // 2, wide), BF), pltpu.VMEM((cut, width), BF)],
        copies=len(ins) + 4 + nz,
    )((meta,), *ins)
    v_mlp = lay.gather_sum(u_mlp.reshape(nz * piece, wide))
    both = KV * rows + QW // nz * width // WIDE

    def backward(
        meta, seq_len, lengths, span_order, mine, other, down_mine, down_other, g_low, residual, inverse_m, att, wqkv, wout, qkv,
        xa, xb, cos_table, sin_table,
    ):
        r = halves(plus(mine, send(other, lay.core)))
        r = halves(plus(r[0], send(r[1], lay.second)))
        got = send(r[1], lay.first)
        got_down = send(down_other, lay.core)
        g_res2, h0 = kernel_call(
            norm_back_kernel, (shaped(own, width, dtype=F32), shaped(own, width))
        )((), g_low, residual, inverse_m, r[0], got)
        ga, gb = lay.plane_tokens(h0)
        d = halves(plus(down_mine, got_down))
        ga, gb, d = fence(ga, gb, d)
        got_down = send(d[1], lay.second)
        outs = [half_rows, half_rows] + [shaped(both, WIDE)] * nz
        ins = (ga, gb, att, wout, wqkv, qkv, flat(xa), flat(xb))
        mine, other, u0, u1, u2, u3 = moving_call(
            attention_back_kernel,
            outs,
            scratch=vmem(*ins, *outs)
            + [pltpu.VMEM((2, tokens // 2, WIDE), BF), pltpu.VMEM((length, width), BF)]
            + tables
            + [pltpu.VMEM((QW, width), BF)],
            copies=len(ins) + len(outs) + 16,
        )((meta, seq_len, span_order), *ins, cos_table, sin_table)
        got_down, mine, other, u0, u1, u2, u3 = fence(got_down, mine, other, u0, u1, u2, u3)
        d = halves(plus(d[0], got_down))
        return g_res2, mine, other, d[0], d[1], u3, u2, u1, u0

    g_res2, mine, other, da, db, u3, u2, u1, u0 = unit_of_work(
        go, backward, meta, seq_len, lengths, span_order, mine, other, down_mine, down_other, g_low, residual, inverse_m, att, wqkv,
        wout, qkv, xa, xb, cos_table, sin_table,
    )
    got = send(other, lay.core)
    got, mine = fence(got, mine)
    c5 = send(u3, lay.inward)
    r = halves(plus(mine, got))
    got = send(r[1], lay.second)
    v_gu = v_mlp[: KV * rows]
    c5, r, got, v_gu = fence(c5, r, got, v_gu)
    c4 = send(plus(u3, c5), lay.inner)
    c3 = send(u2, lay.inward)
    r = halves(plus(r[0], got))
    got = send(r[1], lay.first)
    got_down = send(db, lay.first)
    c4, c3, r, got, got_down = fence(c4, c3, r, got, got_down)
    c1 = send(plus(u1, c4), lay.pair)
    c2 = send(plus(u2, c3), lay.inner)
    v_gu = lay.exchange(v_gu.reshape(KV, rows, wide))
    grad_down = kernel_call(unpack_down_kernel, shaped(low, width, dtype=F32))((), v_mlp[KV * rows :])
    block_out = kernel_call(finish_kernel, shaped(own, width))(
        (meta, lengths, span_order), residual, da, got_down
    )
    grad_in = kernel_call(norm_back_low_kernel, shaped(own, width))(
        (), g_res2, hidden_in.reshape(own, width), inverse, r[0], got
    )
    c1, c2, v_gu, grad_down, block_out, grad_in = fence(c1, c2, v_gu, grad_down, block_out, grad_in)
    c0 = u0
    v = plus(plus(c0, c1), c2)
    v_qkv = lay.exchange(v[: KV * rows].reshape(KV, rows, WIDE))
    v_out = jnp.concatenate(list(v[KV * rows :].reshape(width // WIDE, -1, WIDE)), axis=1)
    grad_out = send(v_out, lay.back)
    grad_gate, grad_up, total_m = kernel_call(
        unpack_mlp_kernel, (shaped(*w_gate.shape, dtype=F32), shaped(*w_up.shape, dtype=F32), shaped(1, rows, dtype=F32))
    )((), v_gu, w_gate, w_up, gain_m)
    grad_out, v_qkv, grad_gate, grad_up, total_m = fence(grad_out, v_qkv, grad_gate, grad_up, total_m)
    grad_query, grad_key, grad_value, total = kernel_call(
        unpack_attention_kernel,
        tuple(shaped(*w.shape, dtype=F32) for w in (w_query, w_key, w_value)) + (shaped(1, rows, dtype=F32),),
    )((), v_qkv, w_query, w_key, w_value, gain)
    return (
        block_out.reshape(hidden_in.shape), grad_in.reshape(hidden_in.shape), total[0], grad_query, grad_key, grad_value,
        grad_out.astype(F32), total_m[0], grad_gate, grad_up, grad_down,
    )


def anywhere(
    hidden_in, lengths, span_order, attn_gain, w_query, w_key, w_value, w_out,
    mlp_gain, w_gate, w_up, w_down, out_grad,
):
    lay = Layout()
    micro, slots, width = hidden_in.shape
    rows, nz = w_query.shape[0], lay.nz
    gain = attn_gain.astype(F32)[:, None]
    gain_m = mlp_gain.astype(F32)[:, None]
    pos = jnp.concatenate([positions_of(span_order, k, slots) for k in range(lay.ctx)])
    usable = (positions_of(span_order, lay.c, slots)[None, :] < lengths[:, None]).astype(F32)[..., None]
    cosines, sines = rope_tables(pos)
    length = slots * lay.ctx

    def tokens(x):
        return lax.all_gather(x, "ctx", axis=1, tiled=True).reshape(micro * length, width)

    def own(x):
        x = x.astype(BF).reshape(micro, length, width)
        return lax.psum_scatter(x, "ctx", scatter_dimension=1, tiled=True).astype(F32)

    spread, collect = lay.spread, lay.gather_sum
    wqkv = spread(lay.exchange(pack_attention(w_query, w_key, w_value, gain)).reshape(KV * rows, -1))
    wgu = spread(lay.exchange(pack_mlp(w_gate, w_up, gain_m, nz)).reshape(KV * rows, -1))
    wout = spread(send(w_out, lay.place))
    wdown = spread(w_down)
    source = hidden_in.astype(F32)
    unit, inverse = unit_rows(source)
    xs = tokens(unit.astype(BF))
    g_res = out_grad.astype(F32) * usable
    g_mlp = tokens(g_res.astype(BF))
    pre = mm(xs, wqkv).reshape(micro, length, -1)
    attended, kept = attend(pre, pos, lengths, cosines, sines)
    att = attended.reshape(micro * length, QW)
    residual = source + own(mm(att, wout))
    unit_m, inverse_m = unit_rows(residual)
    xm = tokens(unit_m.astype(BF))
    gate_up = mm(xm, wgu)
    hidden = swiglu(gate_up)
    block_out = (usable * (residual + own(mm(hidden, wdown)))).astype(BF)
    grad_down = collect(mm_lt(hidden, g_mlp)).astype(F32)
    g_gu = swiglu_back(gate_up, mm_rt(g_mlp, wdown))
    v_gu = lay.exchange(collect(mm_lt(xm, g_gu)).reshape(KV, rows, -1))
    u_gate, u_up = unpack_mlp(v_gu, nz)
    g_res2 = g_res + unit_back(own(mm_rt(g_gu, wgu)), unit_m, inverse_m)
    g_branch = tokens(g_res2.astype(BF))
    grad_out = send(collect(mm_lt(att, g_branch)), lay.back).astype(F32)
    g_att = mm_rt(g_branch, wout).astype(BF).reshape(micro, length, QW)
    g_pre = attend_back(g_att, kept, cosines, sines).reshape(micro * length, -1)
    v_qkv = lay.exchange(collect(mm_lt(xs, g_pre)).reshape(KV, rows, -1))
    u_q, u_k, u_v = unpack_attention(v_qkv)
    grad_in = (g_res2 + unit_back(own(mm_rt(g_pre, wqkv)), unit, inverse)).astype(BF)
    return (
        block_out, grad_in, paired((w_query, u_q), (w_key, u_k), (w_value, u_v)),
        u_q * gain, u_k * gain, u_v * gain, grad_out,
        paired((w_gate, u_gate), (w_up, u_up)), u_gate * gain_m, u_up * gain_m, grad_down,
    )


def solution(mesh):
    rows = P(AXES, None)
    tokens = P("fsdp", "ctx", None)
    line = mesh.shape["ctx"] == 4 and mesh.shape["fsdp"] == 8
    return jax.shard_map(
        on_line if line else anywhere,
        mesh=mesh,
        in_specs=(tokens, P("fsdp"), P(), P(AXES), rows, rows, rows, rows, P(AXES), rows, rows, rows, tokens),
        out_specs=(tokens, tokens, P(AXES), rows, rows, rows, rows, P(AXES), rows, rows, rows),
        check_vma=False,
    )
```

```python
import jax
import jax.numpy as jnp
import numpy as np
from jax import lax
from jax.experimental import pallas as pl
from jax.experimental.pallas import tpu as pltpu
from jax.sharding import PartitionSpec as P

H = 16
KV = 8
HD = 96
GROUP = H // KV
QW = GROUP * HD
AXES = ("fsdp", "ctx")

epsilon = 1e-05
rope_base = 100000.0
masked_score = -1e30
scale = HD ** (-0.5)
BF = jnp.bfloat16
F32 = jnp.float32


def mm(left, right):
    return jnp.dot(left, right, preferred_element_type=F32)


def mm_lt(left, right):
    return lax.dot_general(left, right, (((0,), (0,)), ((), ())), preferred_element_type=F32)


def mm_rt(left, right):
    return lax.dot_general(left, right, (((1,), (1,)), ((), ())), preferred_element_type=F32)


def plus(a, b):
    return a + b


def send(x, pairs):
    return lax.ppermute(x, AXES, pairs)


def unit_of_work(go, body, *args):
    def idle(*args):
        return jax.tree.map(lambda leaf: jnp.zeros(leaf.shape, leaf.dtype), jax.eval_shape(body, *args))

    return lax.cond(go, body, idle, *args)


def fence(*items):
    return lax.optimization_barrier(items)


class Layout:
    def __init__(self):
        self.ctx = lax.axis_size("ctx")
        self.fsdp = lax.axis_size("fsdp")
        self.tpf = KV // self.ctx
        self.nz = self.fsdp // self.tpf
        self.total = self.fsdp * self.ctx
        self.fast = self.ctx == 4 and self.tpf == 2 and self.nz == 4
        self.f = lax.axis_index("fsdp")
        self.c = lax.axis_index("ctx")
        self.z = self.f // self.tpf
        self.place = [(b, (b % self.nz) * KV + b // self.nz) for b in range(self.total)]
        self.back = [(d, s) for s, d in self.place]

    def exchange(self, x):
        if self.tpf == 1:
            return lax.all_to_all(x, "ctx", split_axis=0, concat_axis=0, tiled=True)
        groups = [[z * KV + i for i in range(KV)] for z in range(self.nz)]
        return lax.all_to_all(
            x, AXES, split_axis=0, concat_axis=0, tiled=True, axis_index_groups=groups
        )

    def lines(self):
        return [[z * KV + i for z in range(self.nz)] for i in range(KV)]

    def spread(self, x):
        if self.tpf == 1:
            return lax.all_gather(x, "fsdp", axis=0, tiled=True)
        return lax.all_gather(x, AXES, axis=0, tiled=True, axis_index_groups=self.lines())

    def gather_sum(self, x):
        x = x.astype(BF)
        if self.tpf == 1:
            return lax.psum_scatter(x, "fsdp", scatter_dimension=0, tiled=True)
        return lax.psum_scatter(
            x, AXES, scatter_dimension=0, tiled=True, axis_index_groups=self.lines()
        )


class Line(Layout):
    def __init__(self):
        super().__init__()
        total = self.total
        self.core = [(d, d ^ 1) for d in range(total)]
        self.first = [(d, d ^ (2 if d & 1 else 4)) for d in range(total)]
        self.second = [(d, d ^ (4 if d & 1 else 2)) for d in range(total)]
        self.xflip = [(d, d ^ 4) for d in range(total)]

        def planes(pairs):
            return [(s * KV + i, d * KV + i) for s, d in pairs for i in range(KV)]

        self.pair = planes([(0, 1), (1, 0), (2, 3), (3, 2)])
        self.inner = planes([(1, 2), (2, 1)])
        self.outward = planes([(1, 0), (2, 3)])
        self.inward = planes([(0, 1), (3, 2)])
        z = self.z
        low = z < 2
        self.order = [z, z ^ 1, jnp.where(low, 2, 1), jnp.where(low, 3, 0)]
        table = ((0, 1, 3, 3), (1, 0, 2, 2), (2, 2, 0, 1), (3, 3, 1, 0))
        self.slot = [
            jnp.where(z == 0, r[0], jnp.where(z == 1, r[1], jnp.where(z == 2, r[2], r[3])))
            for r in table
        ]

    def take_columns(self, x, blocks):
        width = x.shape[-1] // self.nz
        return jnp.concatenate(
            [lax.dynamic_slice_in_dim(x, k * width, width, axis=-1) for k in blocks], axis=-1
        )

    def take_rows(self, pieces):
        full = jnp.stack(pieces)
        return jnp.concatenate(
            [lax.dynamic_index_in_dim(full, k, axis=0, keepdims=False) for k in self.slot], axis=0
        )

    def to_pieces(self, x):
        full = x.reshape((self.nz, x.shape[0] // self.nz) + x.shape[1:])
        return [lax.dynamic_index_in_dim(full, k, axis=0, keepdims=False) for k in self.order]

    def all_tokens(self, x):
        x = jnp.stack([x, send(x, self.first)])
        x = jnp.stack([x, send(x, self.second)])
        x = jnp.stack([x, send(x, self.core)])
        return x.reshape(-1, x.shape[-1])

    def plane_tokens(self, x):
        x = jnp.stack([x, send(x, self.first)])
        x = jnp.stack([x, send(x, self.second)])
        other = send(x, self.core)
        return x.reshape(-1, x.shape[-1]), other.reshape(-1, x.shape[-1])

    def collect_tokens(self, x, slots):
        x = x.reshape(2, 2, 2, 2, slots, x.shape[-1])
        x = plus(x[0], send(x[1], self.core))
        x = plus(x[0], send(x[1], self.second))
        return x[0].astype(F32) + send(x[1], self.first).astype(F32)

    def to_seqs(self, x, slots):
        x = x.reshape(2, 2, 2, 2, slots, x.shape[-1])
        halves = []
        for dc in range(2):
            even = ((self.c & 1) ^ dc) == 0
            h = x[dc]
            halves.append(jnp.where(even, jnp.swapaxes(h, 0, 1), h))
        x = jnp.stack(halves, axis=0)
        x = jnp.transpose(x, (1, 3, 0, 2, 4, 5))
        return x.reshape(4, 4 * slots, x.shape[-1])

    def from_seqs(self, x, slots):
        x = x.reshape(2, 2, 2, 2, slots, x.shape[-1])
        x = jnp.transpose(x, (2, 0, 3, 1, 4, 5))
        halves = []
        for dc in range(2):
            even = ((self.c & 1) ^ dc) == 0
            h = x[dc]
            halves.append(jnp.where(even, jnp.swapaxes(h, 0, 1), h))
        return jnp.stack(halves, axis=0).reshape(16 * slots, x.shape[-1])


def positions_of(span_order, index, slots):
    span_len = slots // 2
    at = jnp.arange(slots, dtype=jnp.int32)
    pair = lax.dynamic_slice_in_dim(span_order, 2 * index, 2)
    return jnp.where(at < span_len, pair[0], pair[1]) * span_len + at % span_len


def rope_tables(pos):
    frequency = rope_base ** (-2.0 * jnp.arange(HD // 2, dtype=F32) / HD)
    angles = pos.astype(F32)[:, None] * frequency[None, :]
    return jnp.cos(angles), jnp.sin(angles)


def rotate(v, cosines, sines):
    half = HD // 2
    co, si = cosines[None, :, None, :], sines[None, :, None, :]
    one, two = v[..., :half], v[..., half:]
    return jnp.concatenate([one * co - two * si, two * co + one * si], axis=-1)


def unit_rows(x):
    inverse = lax.rsqrt(jnp.mean(x * x, axis=-1, keepdims=True) + epsilon)
    return x * inverse, inverse


def unit_back(scaled, unit, inverse):
    return inverse * (scaled - unit * jnp.mean(scaled * unit, axis=-1, keepdims=True))


def attend(pre, pos, seq_len, cosines, sines):
    seqs, length, _ = pre.shape
    q = rotate(pre[..., :QW].reshape(seqs, length, GROUP, HD), cosines, sines).astype(BF)
    k = rotate(pre[..., QW : QW + HD].reshape(seqs, length, 1, HD), cosines, sines)[:, :, 0].astype(BF)
    v = pre[..., QW + HD :].astype(BF)
    allowed = (pos[None, None, :] <= pos[None, :, None]) & (
        pos[None, None, :] < seq_len[:, None, None]
    )
    scores = jnp.einsum("sqgd,snd->sgqn", q, k, preferred_element_type=F32) * scale
    scores = jnp.where(allowed[:, None], scores, masked_score)
    top = jnp.max(scores, axis=-1, keepdims=True)
    expo = jnp.exp(scores - top)
    probs = expo / jnp.sum(expo, axis=-1, keepdims=True)
    low = probs.astype(BF)
    attended = jnp.einsum("sgqn,snd->sqgd", low, v, preferred_element_type=F32)
    return attended.astype(BF).reshape(seqs, length, QW), (q, k, v, probs, low)


def attend_back(g_att, kept, cosines, sines):
    q, k, v, probs, low = kept
    seqs, length, _ = g_att.shape
    g_att = g_att.reshape(seqs, length, GROUP, HD)
    g_probs = jnp.einsum("sqgd,snd->sgqn", g_att, v, preferred_element_type=F32)
    inner = jnp.sum(probs * g_probs, axis=-1, keepdims=True)
    g_scores = (probs * (g_probs - inner)).astype(BF)
    g_q = jnp.einsum("sgqn,snd->sqgd", g_scores, k, preferred_element_type=F32) * scale
    g_k = jnp.einsum("sgqn,sqgd->snd", g_scores, q, preferred_element_type=F32) * scale
    g_v = jnp.einsum("sgqn,sqgd->snd", low, g_att, preferred_element_type=F32)
    return jnp.concatenate(
        [
            rotate(g_q, cosines, -sines).astype(BF).reshape(seqs, length, QW),
            rotate(g_k[:, :, None], cosines, -sines).astype(BF)[:, :, 0],
            g_v.astype(BF),
        ],
        axis=-1,
    )


def swiglu(gate_up):
    half = gate_up.shape[-1] // 2
    gate, up = gate_up[:, :half], gate_up[:, half:]
    return (jax.nn.silu(gate) * up).astype(BF)


def swiglu_back(gate_up, g_hidden):
    half = gate_up.shape[-1] // 2
    gate, up = gate_up[:, :half], gate_up[:, half:]
    sig = jax.nn.sigmoid(gate)
    g_gate = (g_hidden * up * sig * (1.0 + gate * (1.0 - sig))).astype(BF)
    g_up = (g_hidden * gate * sig).astype(BF)
    return jnp.concatenate([g_gate, g_up], axis=-1)


def pack_attention(w_query, w_key, w_value, gain):
    rows = w_query.shape[0]
    parts = [
        (w.astype(F32) * gain).astype(BF).reshape(rows, KV, w.shape[1] // KV)
        for w in (w_query, w_key, w_value)
    ]
    return jnp.transpose(jnp.concatenate(parts, axis=2), (1, 0, 2))


def unpack_attention(u):
    u = jnp.transpose(u, (1, 0, 2)).astype(F32)
    rows = u.shape[0]
    return (
        u[..., :QW].reshape(rows, KV * QW),
        u[..., QW : QW + HD].reshape(rows, KV * HD),
        u[..., QW + HD :].reshape(rows, KV * HD),
    )


def pack_mlp(w_gate, w_up, gain, nz):
    rows = w_gate.shape[0]

    def columns(w):
        w = (w.astype(F32) * gain).astype(BF).reshape(rows, nz, KV, -1)
        return jnp.transpose(w, (2, 0, 1, 3)).reshape(KV, rows, -1)

    return jnp.concatenate([columns(w_gate), columns(w_up)], axis=2)


def unpack_mlp(u, nz):
    rows = u.shape[1]
    u = u.reshape(KV, rows, 2, nz, -1)
    u = jnp.transpose(u, (2, 1, 3, 0, 4)).reshape(2, rows, -1).astype(F32)
    return u[0], u[1]


SMEM = pl.BlockSpec(memory_space=pltpu.SMEM)
VMEM = pl.BlockSpec(memory_space=pltpu.VMEM)
WIDE = QW + 2 * HD
FREE = pl.CostEstimate(flops=0, bytes_accessed=0, transcendentals=0)
ROOM = pltpu.CompilerParams(vmem_limit_bytes=56 * 1024 * 1024)


def shaped(*shape, dtype=BF):
    return jax.ShapeDtypeStruct(shape, dtype)


def kernel_call(body, outs, scratch=()):
    def call(scalars, *arrays):
        return pl.pallas_call(
            body,
            out_shape=outs,
            in_specs=[SMEM] * len(scalars) + [VMEM] * len(arrays),
            out_specs=jax.tree.map(lambda _: VMEM, outs),
            scratch_shapes=list(scratch),
            compiler_params=ROOM,
            cost_estimate=FREE,
        )(*scalars, *arrays)

    return call


def moving_call(body, outs, scratch=(), copies=1):
    def call(scalars, *arrays):
        anywhere_spec = pl.BlockSpec(memory_space=pl.ANY)
        return pl.pallas_call(
            body,
            out_shape=outs,
            in_specs=[SMEM] * len(scalars) + [pl.BlockSpec(memory_space=pltpu.HBM)] * len(arrays),
            out_specs=jax.tree.map(lambda _: anywhere_spec, outs),
            scratch_shapes=list(scratch) + [pltpu.SemaphoreType.DMA((copies,))],
            compiler_params=ROOM,
            cost_estimate=FREE,
        )(*scalars, *arrays)

    return call


class Copies:
    def __init__(self, sems):
        self.sems = sems
        self.used = 0

    def start(self, source, target):
        copy = pltpu.make_async_copy(source, target, self.sems.at[self.used])
        self.used += 1
        copy.start()
        return copy


def vmem(*arrays):
    return [pltpu.VMEM(a.shape, a.dtype) for a in arrays]


def dot(a, b, dims=((1,), (0,))):
    return lax.dot_general(a, b, (dims, ((), ())), preferred_element_type=F32)


LEFT_T = ((0,), (0,))
RIGHT_T = ((1,), (1,))


def block_rows(core, seq, dc, dy, slots):
    dx, m = seq // 2, seq % 2
    even = (core ^ dc) == 0
    s1 = jnp.where(even, dx, dy)
    s2 = jnp.where(even, dy, dx)
    return pl.multiple_of(((s2 * 2 + s1) * 2 + m) * slots, slots)


def blocks_of(slots):
    for dc in range(2):
        for dy in range(2):
            b = dc * 2 + dy
            yield dc, dy, slice(b * slots, (b + 1) * slots)


def spans_of(spans, ctx):
    out = []
    for dc in range(2):
        for dy in range(2):
            other = ctx ^ (dy * 2 + dc)
            out += [spans[2 * other], spans[2 * other + 1]]
    return out


def along(held, length, axis, shape):
    at = lax.broadcasted_iota(jnp.int32, shape, axis) % length
    step = length // len(held)
    pos = at % step
    for i, span in enumerate(held):
        pos = pos + jnp.where(at // step == i, span * step, 0)
    return pos


def rotary_rows(held, table, out):
    step = out.shape[0] // len(held)
    for i, span in enumerate(held):
        out[i * step : (i + 1) * step, :] = table[pl.ds(pl.multiple_of(span * step, step), step), :]


def rotary_copies(copies, held, table, out):
    step = out.shape[0] // len(held)
    return [
        copies.start(table.at[pl.ds(pl.multiple_of(span * step, step), step)], out.at[pl.ds(i * step, step)])
        for i, span in enumerate(held)
    ]


def turn(x, cosines, sines):
    half, width = HD // 2, x.shape[1]
    lane = lax.broadcasted_iota(jnp.int32, x.shape, 1) % HD
    partner = jnp.where(lane < half, pltpu.roll(x, width - half, 1), pltpu.roll(x, half, 1))
    return x * cosines + partner * sines


def probabilities(q, k, allowed):
    scores = jnp.where(allowed, dot(q, k, RIGHT_T) * scale, masked_score)
    expo = jnp.exp(scores - jnp.max(scores, axis=-1, keepdims=True))
    return expo / jnp.sum(expo, axis=-1, keepdims=True)


def heads_of(x):
    return [x[:, h * HD : (h + 1) * HD] for h in range(x.shape[1] // HD)]


def assemble(meta, pieces, out):
    p0, p1, p2, p3, p4, p5 = pieces
    step = p0.shape[0]
    for s, parts in enumerate(((p0,), (p1,), (p2, p3), (p4, p5))):
        piece = parts[0][...]
        if len(parts) > 1:
            piece = piece + parts[1][...]
        out[pl.ds(pl.multiple_of(meta[s] * step, step), step), :] = piece


def fetch_qkv(full, out):
    step = full.shape[2]
    for z in range(full.shape[0]):
        out[z * step : (z + 1) * step, :] = full[z, :step, :]


def fetch_out(full, out):
    nz, total, step = full.shape
    count = out.shape[1] // step
    rows = (total - step) // count
    for z in range(nz):
        for k in range(count):
            out[z * rows : (z + 1) * rows, k * step : (k + 1) * step] = full[
                z, step + k * rows : step + (k + 1) * rows, :
            ]


def stacked_columns(x, cut):
    return jnp.concatenate([x[:, k : k + cut] for k in range(0, x.shape[1], cut)], axis=0)


def column(row):
    n = row.shape[1]
    same = lax.broadcasted_iota(jnp.int32, (n, n), 0) == lax.broadcasted_iota(jnp.int32, (n, n), 1)
    return jnp.sum(jnp.where(same, row, 0.0), axis=1, keepdims=True)


def row_of(col):
    n = col.shape[0]
    same = lax.broadcasted_iota(jnp.int32, (n, n), 0) == lax.broadcasted_iota(jnp.int32, (n, n), 1)
    return jnp.sum(jnp.where(same, col, 0.0), axis=0, keepdims=True)


def pack_attention_kernel(wq, wk, wv, gain, out):
    g = column(gain[...].astype(F32))
    q, k, v = ((w[...].astype(F32) * g).astype(BF) for w in (wq, wk, wv))
    for j in range(KV):
        out[j] = jnp.concatenate(
            [q[:, j * QW : (j + 1) * QW], k[:, j * HD : (j + 1) * HD], v[:, j * HD : (j + 1) * HD]], axis=1
        )


def pack_mlp_kernel(wg, wu, gain, out):
    g = column(gain[...].astype(F32))
    half = out.shape[2] // 2
    blocks = 4
    hid = half // blocks
    for h, w in enumerate((wg, wu)):
        x = (w[...].astype(F32) * g).astype(BF)
        for z in range(blocks):
            for j in range(KV):
                out[j, :, h * half + z * hid : h * half + (z + 1) * hid] = x[
                    :, (z * KV + j) * hid : (z * KV + j + 1) * hid
                ]


def unpack_attention_kernel(u, wq, wk, wv, gain, gq, gk, gv, total):
    g = column(gain[...].astype(F32))
    acc = jnp.zeros(g.shape, F32)
    for w, out, lo, n in ((wq, gq, 0, QW), (wk, gk, QW, HD), (wv, gv, QW + HD, HD)):
        part = jnp.concatenate([u[j, :, lo : lo + n] for j in range(KV)], axis=1).astype(F32)
        out[...] = part * g
        acc += jnp.sum(part * w[...].astype(F32), axis=1, keepdims=True)
    total[...] = row_of(acc)


def unpack_mlp_kernel(u, wg, wu, gain, gg, gu, total):
    g = column(gain[...].astype(F32))
    acc = jnp.zeros(g.shape, F32)
    half = wg.shape[1] // KV
    blocks = 4
    hid = half // blocks
    for j in range(KV):
        x = u[j].astype(F32)
        for h, (w, out) in enumerate(((wg, gg), (wu, gu))):
            for z in range(blocks):
                at = slice((z * KV + j) * hid, (z * KV + j + 1) * hid)
                part = x[:, h * half + z * hid : h * half + (z + 1) * hid]
                out[:, at] = part * g
                acc += jnp.sum(part * w[:, at].astype(F32), axis=1, keepdims=True)
    total[...] = row_of(acc)


def usable_rows(lens, spans, ctx, shape):
    at = lax.broadcasted_iota(jnp.int32, shape, 0)
    slots = shape[0] // 2
    slot, step = at % slots, slots // 2
    pos = jnp.where(slot < step, spans[2 * ctx], spans[2 * ctx + 1]) * step + slot % step
    length = jnp.where(at < slots, lens[0], lens[1])
    return (pos < length).astype(F32)


def prepare_kernel(meta, lens, spans, x, g, xhat, inverse, g_low):
    v = x[...].astype(F32)
    inv = lax.rsqrt(jnp.mean(v * v, axis=-1, keepdims=True) + epsilon)
    inverse[...] = inv
    xhat[...] = (v * inv).astype(BF)
    g_low[...] = (g[...].astype(F32) * usable_rows(lens, spans, meta[5], inverse.shape)).astype(BF)


def finish_kernel(meta, lens, spans, residual, a, b, out):
    total = residual[...] + a[...].astype(F32) + b[...].astype(F32)
    out[...] = (total * usable_rows(lens, spans, meta[5], (total.shape[0], 1))).astype(BF)


def attention_kernel(
    meta, lens, spans, xa, xb, full, cos_table, sin_table, wqkv, qkv, att, xseq, cosines, sines
):
    core, ctx = meta[4], meta[5]
    slots = xa.shape[0] // 8
    length = xseq.shape[0]
    fetch_qkv(full, wqkv)
    held = spans_of(spans, ctx)
    rotary_rows(held, cos_table, cosines)
    rotary_rows(held, sin_table, sines)
    posc = along(held, length, 0, (GROUP * length, length))
    posr = along(held, length, 1, (GROUP * length, length))
    causal = posr <= posc

    def one(seq, carry):
        for dc, dy, rows in blocks_of(slots):
            xseq[rows, :] = (xa, xb)[dc][pl.ds(block_rows(core, seq, dc, dy, slots), slots), :]
        low = turn(dot(xseq[...], wqkv[...]), cosines[...], sines[...]).astype(BF)
        qkv[seq] = low
        one_q, two_q, k, v = heads_of(low)
        q = jnp.concatenate([one_q, two_q], axis=0)
        allowed = causal & (posr < lens[seq])
        mixed = dot(probabilities(q, k, allowed).astype(BF), v)
        out = jnp.concatenate([mixed[:length], mixed[length:]], axis=1).astype(BF)
        for dc, dy, rows in blocks_of(slots):
            att[dc, pl.ds(block_rows(core, seq, dc, dy, slots), slots), :] = out[rows]
        return carry

    lax.fori_loop(0, 4, one, 0, unroll=True)


def project_kernel(att, full, wout, mine, theirs):
    fetch_out(full, wout)
    theirs[...] = dot(att[1], wout[...]).astype(BF)
    mine[...] = dot(att[0], wout[...]).astype(BF)


def attention_back_kernel(
    meta, lens, spans,
    h_ga, h_gb, h_att, h_wout, h_wqkv, h_qkv, h_xa, h_xb, cos_table, sin_table,
    o_mine, o_theirs, o0, o1, o2, o3,
    ga, gb, att, wout, wqkv, qkv, xa, xb, mine, theirs, u0, u1, u2, u3, g_pre, gseq, cosines, sines, out_grad, sems,
):
    copies = Copies(sems)
    held = spans_of(spans, meta[5])
    first = [copies.start(h, v) for h, v in ((h_wout, wout), (h_qkv, qkv), (h_ga, ga), (h_gb, gb))]
    first += rotary_copies(copies, held, cos_table, cosines) + rotary_copies(copies, held, sin_table, sines)
    for c in first:
        c.wait()
    later = [copies.start(h, v) for h, v in ((h_xa, xa), (h_xb, xb), (h_att, att), (h_wqkv, wqkv))]
    core, ctx = meta[4], meta[5]
    slots = ga.shape[0] // 8
    length = gseq.shape[0]
    posc = along(held, length, 0, (GROUP * length, length))
    posr = along(held, length, 1, (GROUP * length, length))
    causal = posr <= posc

    def one(seq, carry):
        for dc, dy, rows in blocks_of(slots):
            gseq[rows, :] = (ga, gb)[dc][pl.ds(block_rows(core, seq, dc, dy, slots), slots), :]
        g_att = dot(gseq[...], wout[...], RIGHT_T).astype(BF)
        one_q, two_q, k, v = heads_of(qkv[seq])
        q = jnp.concatenate([one_q, two_q], axis=0)
        g = jnp.concatenate(heads_of(g_att), axis=0)
        allowed = causal & (posr < lens[seq])
        p = probabilities(q, k, allowed)
        g_p = dot(g, v, RIGHT_T)
        g_s = (p * (g_p - jnp.sum(p * g_p, axis=-1, keepdims=True))).astype(BF)
        g_q = dot(g_s, k) * scale
        g_k = dot(g_s, q, LEFT_T) * scale
        g_v = dot(p.astype(BF), g, LEFT_T)
        full = jnp.concatenate([g_q[:length], g_q[length:], g_k, g_v], axis=1)
        out = turn(full, cosines[...], -sines[...]).astype(BF)
        for dc, dy, rows in blocks_of(slots):
            g_pre[dc, pl.ds(block_rows(core, seq, dc, dy, slots), slots), :] = out[rows]
        return carry

    lax.fori_loop(0, 4, one, 0, unroll=True)
    for c in later:
        c.wait()
    gone = []
    out_grad[...] = (dot(att[0], ga[...], LEFT_T) + dot(att[1], gb[...], LEFT_T)).astype(BF)
    step = xa.shape[1] // 4
    block = u0.shape[1]
    count = out_grad.shape[1] // block
    low = out_grad.shape[0] // 4
    for s, u, o in ((3, u3, o3), (2, u2, o2), (1, u1, o1), (0, u0, o0)):
        at = pl.ds(pl.multiple_of(meta[s] * step, step), step)
        u[:step, :] = (dot(xa[:, at], g_pre[0], LEFT_T) + dot(xb[:, at], g_pre[1], LEFT_T)).astype(BF)
        at = pl.ds(pl.multiple_of(meta[s] * low, low), low)
        for k in range(count):
            u[step + k * low : step + (k + 1) * low, :] = out_grad[at, k * block : (k + 1) * block]
        gone.append(copies.start(u, o))
    theirs[...] = dot(g_pre[1], wqkv[...], RIGHT_T).astype(BF)
    gone.append(copies.start(theirs, o_theirs))
    mine[...] = dot(g_pre[0], wqkv[...], RIGHT_T).astype(BF)
    gone.append(copies.start(mine, o_mine))
    for c in gone:
        c.wait()


def mlp_kernel(
    meta,
    h_ma, h_mb, h_ea, h_eb, h_wgu, h0, h1, h2, h3, h4, h5,
    o_down_mine, o_down_theirs, o_mine, o_theirs, o_u,
    ma, mb, ea, eb, wgu, d0, d1, d2, d3, d4, d5, down_mine, down_theirs, mine, theirs, u, hidden, g_gu, wdown, sems,
):
    copies = Copies(sems)
    came = [copies.start(h_wgu, wgu), copies.start(h_mb, mb)]
    pieces = (d0, d1, d2, d3, d4, d5)
    downs = [copies.start(h, d) for h, d in zip((h0, h1, h2, h3, h4, h5), pieces)]
    came_eb = copies.start(h_eb, eb)
    came_ma = copies.start(h_ma, ma)
    came_ea = copies.start(h_ea, ea)
    gone = []
    half = wgu.shape[1] // 2
    for c in came:
        c.wait()
    for part, x, g, down, back, o_down, o_back in (
        (1, mb, eb, down_theirs, theirs, o_down_theirs, o_theirs),
        (0, ma, ea, down_mine, mine, o_down_mine, o_mine),
    ):
        if part == 0:
            came_ma.wait()
        gate_up = dot(x[...], wgu[...])
        gate, up = gate_up[:, :half], gate_up[:, half:]
        sig = 1.0 / (1.0 + jnp.exp(-gate))
        act = gate * sig
        hid = (act * up).astype(BF)
        hidden[part] = hid
        if part == 1:
            for c in downs:
                c.wait()
            assemble(meta, pieces, wdown)
            came_eb.wait()
        else:
            came_ea.wait()
        g_hidden = dot(g[...], wdown[...], RIGHT_T)
        g_gu[part, :, :half] = (g_hidden * up * sig * (1.0 + gate * (1.0 - sig))).astype(BF)
        g_gu[part, :, half:] = (g_hidden * act).astype(BF)
        back[...] = dot(g_gu[part], wgu[...], RIGHT_T).astype(BF)
        gone.append(copies.start(back, o_back))
        down[...] = dot(hid, wdown[...]).astype(BF)
        gone.append(copies.start(down, o_down))
    nz, _, wide = u.shape
    piece = ma.shape[1] // nz
    step = hidden.shape[2] // nz
    for z in range(nz):
        at = slice(z * piece, (z + 1) * piece)
        both = dot(ma[:, at], g_gu[0], LEFT_T) + dot(mb[:, at], g_gu[1], LEFT_T)
        u[z, :piece, :] = both.astype(BF)
        at = slice(z * step, (z + 1) * step)
        both = (dot(hidden[0, :, at], ea[...], LEFT_T) + dot(hidden[1, :, at], eb[...], LEFT_T)).astype(BF)
        u[z, piece : piece + step, :] = both[:, :wide]
        rest = both.shape[1] - wide
        u[z, piece + step :, :rest] = both[: step // 2, wide:]
        u[z, piece + step :, rest:] = both[step // 2 :, wide:]
        gone.append(copies.start(u.at[z], o_u.at[z]))
    for c in gone:
        c.wait()


def unpack_down_kernel(u, out):
    step, wide = out.shape[0], u.shape[1]
    rest = out.shape[1] - wide
    out[:, :wide] = u[:step, :].astype(F32)
    out[: step // 2, wide:] = u[step:, :rest].astype(F32)
    out[step // 2 :, wide:] = u[step:, rest:].astype(F32)


def sums_kernel(a, b, c, d, ab, cd):
    ab[...] = a[...] + b[...]
    cd[...] = c[...] + d[...]


def last_sum_kernel(a, b, c, qkv, out):
    total = (a[...].astype(F32) + b[...].astype(F32) + c[...].astype(F32)).astype(BF)
    blocks, rows, width = qkv.shape
    for j in range(blocks):
        qkv[j] = total[j * rows : (j + 1) * rows]
    low = out.shape[0]
    for k in range(out.shape[1] // width):
        at = blocks * rows + k * low
        out[:, k * width : (k + 1) * width] = total[at : at + low]


def norm_kernel(source, a, b, residual, xhat, inverse):
    r = source[...].astype(F32) + a[...].astype(F32) + b[...].astype(F32)
    inv = lax.rsqrt(jnp.mean(r * r, axis=-1, keepdims=True) + epsilon)
    residual[...] = r
    inverse[...] = inv
    xhat[...] = (r * inv).astype(BF)


def norm_back(g_res, source, inverse, a, b):
    scaled = a[...].astype(F32) + b[...].astype(F32)
    inv = inverse[...]
    unit = source[...].astype(F32) * inv
    back = inv * (scaled - unit * jnp.mean(scaled * unit, axis=-1, keepdims=True))
    return g_res[...].astype(F32) + back


def norm_back_kernel(g_res, source, inverse, a, b, out, low):
    g = norm_back(g_res, source, inverse, a, b)
    out[...] = g
    low[...] = g.astype(BF)


def norm_back_low_kernel(g_res, source, inverse, a, b, low):
    low[...] = norm_back(g_res, source, inverse, a, b).astype(BF)


def rotary_constants(total):
    frequency = rope_base ** (-2.0 * np.arange(HD // 2, dtype=np.float32) / HD).astype(np.float32)
    angles = np.arange(total, dtype=np.float32)[:, None] * frequency[None, :].astype(np.float32)
    c, s = np.cos(angles), np.sin(angles)
    flat, signed = np.concatenate([c, c], 1), np.concatenate([-s, s], 1)
    cosines = np.concatenate([flat] * (GROUP + 1) + [np.ones_like(flat)], 1)
    sines = np.concatenate([signed] * (GROUP + 1) + [np.zeros_like(flat)], 1)
    return jnp.asarray(cosines, F32), jnp.asarray(sines, F32)


def paired(*items):
    return sum(jnp.sum(w.astype(F32) * g, axis=1) for w, g in items)


def on_line(
    hidden_in, lengths, span_order, attn_gain, w_query, w_key, w_value, w_out,
    mlp_gain, w_gate, w_up, w_down, out_grad,
):
    lay = Line()
    _, slots, width = hidden_in.shape
    rows, nz = w_query.shape[0], lay.nz
    tokens, length, own = 16 * slots, 4 * slots, 2 * slots
    go = lengths[0] > 0
    meta = jnp.stack([k.astype(jnp.int32) for k in (*lay.order, lay.c & 1, lay.c)])
    gain, gain_m = attn_gain[None, :], mlp_gain[None, :]
    cos_table, sin_table = rotary_constants(length)

    def halves(x):
        return x.reshape(2, x.shape[0] // 2, width)

    wide = w_gate.shape[1] * 2 // KV
    cut = wide // 2
    tables = [pltpu.VMEM((length, WIDE), F32)] * 2

    def flat(x):
        return x.reshape(-1, width)

    d1 = send(w_down, lay.pair)
    d2 = send(w_down, lay.inner)
    q0 = lay.exchange(
        kernel_call(pack_attention_kernel, shaped(KV, rows, WIDE))((), w_query, w_key, w_value, gain)
    )
    theirs = send(lengths, lay.xflip)
    o0 = send(w_out, lay.place)
    gu_s = kernel_call(pack_mlp_kernel, shaped(KV, rows, wide))((), w_gate, w_up, gain_m)
    xhat, inverse, g_low = kernel_call(
        prepare_kernel, (shaped(own, width), shaped(own, 1, dtype=F32), shaped(own, width))
    )((meta, lengths, span_order), hidden_in.reshape(own, width), out_grad.reshape(own, width))
    q0, d1, d2, theirs, gu_s, xhat, g_low = fence(q0, d1, d2, theirs, gu_s, xhat, g_low)
    d3 = send(d2, lay.outward)
    d4 = send(d1, lay.inner)
    x1 = send(xhat, lay.first)
    attn_piece = jnp.concatenate([q0.reshape(KV * rows, WIDE), stacked_columns(o0, WIDE)], axis=0)
    d3, d4, x1, attn_piece = fence(d3, d4, x1, attn_piece)
    attn_full = lay.spread(attn_piece)

    def gather(xhat, x1, g_low, gu_s):
        gu0 = lay.exchange(gu_s)
        x01 = jnp.stack([xhat, x1])
        x2 = send(x01, lay.second)
        x2, gu0, x01, g_low = fence(x2, gu0, x01, g_low)
        x0123 = jnp.stack([x01, x2])
        x3 = send(x0123, lay.core)
        e1 = send(g_low, lay.first)
        x3, x0123, e1 = fence(x3, x0123, e1)
        e01 = jnp.stack([g_low, e1])
        return x0123, x3, gu0, e01

    xa, xb, gu0, e01 = unit_of_work(go, gather, xhat, x1, g_low, gu_s)
    attn_full, gu0 = fence(attn_full, gu0)
    wgu = lay.spread(gu0.reshape(KV * rows, wide))
    attn_full = attn_full.reshape(nz, -1, WIDE)
    seq_len = jnp.concatenate([lengths, theirs])

    def forward(meta, seq_len, span_order, xa, xb, attn_full, cos_table, sin_table, hidden_in, e01, d4):
        e2 = send(e01, lay.second)
        wqkv, qkv, att = kernel_call(
            attention_kernel,
            (shaped(width, WIDE), shaped(4, length, WIDE), shaped(2, tokens // 2, QW)),
            scratch=[pltpu.VMEM((length, width), BF)] + tables,
        )((meta, seq_len, span_order), flat(xa), flat(xb), attn_full, cos_table, sin_table)
        wqkv, qkv, att, e2 = fence(wqkv, qkv, att, e2)
        wout, mine, other = kernel_call(
            project_kernel, (shaped(QW, width), shaped(tokens // 2, width), shaped(tokens // 2, width))
        )((), att, attn_full)
        got = send(other, lay.core)
        r = halves(plus(mine, got))
        e0123 = jnp.stack([e01, e2])
        r, e0123 = fence(r, e0123)
        got = send(r[1], lay.second)
        e3 = send(e0123, lay.core)
        got, e3, r = fence(got, e3, r)
        r = halves(plus(r[0], got))
        got = send(r[1], lay.first)
        residual, xm0, inverse_m = kernel_call(
            norm_kernel, (shaped(own, width, dtype=F32), shaped(own, width), shaped(own, 1, dtype=F32))
        )((), hidden_in.reshape(own, width), r[0], got)
        m01 = jnp.stack([xm0, send(xm0, lay.first)])
        m01, d4 = fence(m01, d4)
        m2 = send(m01, lay.second)
        d5 = send(d4, lay.outward)
        m2, d5 = fence(m2, d5)
        ma = jnp.stack([m01, m2])
        mb = send(ma, lay.core)
        return wqkv, qkv, att, wout, residual, inverse_m, flat(ma), flat(mb), flat(e0123), flat(e3), d5

    wqkv, qkv, att, wout, residual, inverse_m, ma, mb, ea, eb, d5 = unit_of_work(
        go, forward, meta, seq_len, span_order, xa, xb, attn_full, cos_table, sin_table, hidden_in, e01, d4
    )
    half_rows = shaped(tokens // 2, width)
    low = w_down.shape[0]
    piece = KV * rows + low * width // wide
    outs = (half_rows, half_rows, half_rows, half_rows, shaped(nz, piece, wide))
    ins = (ma, mb, ea, eb, wgu, w_down, d1, d2, d3, d4, d5)
    down_mine, down_other, mine, other, u_mlp = moving_call(
        mlp_kernel,
        outs,
        scratch=vmem(*ins, *outs)
        + [pltpu.VMEM((2, tokens // 2, cut), BF), pltpu.VMEM((2, tokens // 2, wide), BF), pltpu.VMEM((cut, width), BF)],
        copies=len(ins) + 4 + nz,
    )((meta,), *ins)
    v_mlp = lay.gather_sum(u_mlp.reshape(nz * piece, wide))
    both = KV * rows + QW // nz * width // WIDE

    def backward(
        meta, seq_len, lengths, span_order, mine, other, down_mine, down_other, g_low, residual, inverse_m, att, wqkv, wout, qkv,
        xa, xb, cos_table, sin_table,
    ):
        got = send(other, lay.core)
        got, mine = fence(got, mine.astype(F32))
        r = halves((mine + got.astype(F32)).astype(BF))
        r = halves(plus(r[0], send(r[1], lay.second)))
        got = send(r[1], lay.first)
        got_down = send(down_other, lay.core)
        g_res2, h0 = kernel_call(
            norm_back_kernel, (shaped(own, width, dtype=F32), shaped(own, width))
        )((), g_low, residual, inverse_m, r[0], got)
        ga, gb = lay.plane_tokens(h0)
        d = halves(plus(down_mine, got_down))
        ga, gb, d = fence(ga, gb, d)
        got_down = send(d[1], lay.second)
        outs = [half_rows, half_rows] + [shaped(both, WIDE)] * nz
        ins = (ga, gb, att, wout, wqkv, qkv, flat(xa), flat(xb))
        mine, other, u0, u1, u2, u3 = moving_call(
            attention_back_kernel,
            outs,
            scratch=vmem(*ins, *outs)
            + [pltpu.VMEM((2, tokens // 2, WIDE), BF), pltpu.VMEM((length, width), BF)]
            + tables
            + [pltpu.VMEM((QW, width), BF)],
            copies=len(ins) + len(outs) + 16,
        )((meta, seq_len, span_order), *ins, cos_table, sin_table)
        got_down, mine, other, u0, u1, u2, u3 = fence(got_down, mine, other, u0, u1, u2, u3)
        d = halves(plus(d[0], got_down))
        return g_res2, mine, other, d[0], d[1], u3, u2, u1, u0

    g_res2, mine, other, da, db, u3, u2, u1, u0 = unit_of_work(
        go, backward, meta, seq_len, lengths, span_order, mine, other, down_mine, down_other, g_low, residual, inverse_m, att, wqkv,
        wout, qkv, xa, xb, cos_table, sin_table,
    )
    got = send(other, lay.core)
    got, mine = fence(got, mine)
    c5 = send(u3, lay.inward)
    r = halves(plus(mine, got))
    got = send(r[1], lay.second)
    v_gu = v_mlp[: KV * rows]
    c5, r, got, v_gu = fence(c5, r, got, v_gu)
    c4 = send(plus(u3, c5), lay.inner)
    c3 = send(u2, lay.inward)
    r = halves(plus(r[0], got))
    got = send(r[1], lay.first)
    got_down = send(db, lay.first)
    c4, c3, r, got, got_down = fence(c4, c3, r, got, got_down)
    c1, c2 = kernel_call(sums_kernel, (shaped(both, WIDE), shaped(both, WIDE)))((), u1, c4, u2, c3)
    c1 = send(c1, lay.pair)
    c2 = send(c2, lay.inner)
    v_gu = lay.exchange(v_gu.reshape(KV, rows, wide))
    grad_down = kernel_call(unpack_down_kernel, shaped(low, width, dtype=F32))((), v_mlp[KV * rows :])
    block_out = kernel_call(finish_kernel, shaped(own, width))(
        (meta, lengths, span_order), residual, da, got_down
    )
    grad_in = kernel_call(norm_back_low_kernel, shaped(own, width))(
        (), g_res2, hidden_in.reshape(own, width), inverse, r[0], got
    )
    c1, c2, v_gu, grad_down, block_out, grad_in = fence(c1, c2, v_gu, grad_down, block_out, grad_in)
    c0 = u0
    v_qkv, v_out = kernel_call(last_sum_kernel, (shaped(KV, rows, WIDE), shaped(*w_out.shape)))((), c0, c1, c2)
    v_qkv = lay.exchange(v_qkv)
    grad_out = send(v_out, lay.back)
    grad_gate, grad_up, total_m = kernel_call(
        unpack_mlp_kernel, (shaped(*w_gate.shape, dtype=F32), shaped(*w_up.shape, dtype=F32), shaped(1, rows, dtype=F32))
    )((), v_gu, w_gate, w_up, gain_m)
    grad_out, v_qkv, grad_gate, grad_up, total_m = fence(grad_out.astype(F32), v_qkv, grad_gate, grad_up, total_m)
    grad_query, grad_key, grad_value, total = kernel_call(
        unpack_attention_kernel,
        tuple(shaped(*w.shape, dtype=F32) for w in (w_query, w_key, w_value)) + (shaped(1, rows, dtype=F32),),
    )((), v_qkv, w_query, w_key, w_value, gain)
    return (
        block_out.reshape(hidden_in.shape), grad_in.reshape(hidden_in.shape), total[0], grad_query, grad_key, grad_value,
        grad_out, total_m[0], grad_gate, grad_up, grad_down,
    )


def anywhere(
    hidden_in, lengths, span_order, attn_gain, w_query, w_key, w_value, w_out,
    mlp_gain, w_gate, w_up, w_down, out_grad,
):
    lay = Layout()
    micro, slots, width = hidden_in.shape
    rows, nz = w_query.shape[0], lay.nz
    gain = attn_gain.astype(F32)[:, None]
    gain_m = mlp_gain.astype(F32)[:, None]
    pos = jnp.concatenate([positions_of(span_order, k, slots) for k in range(lay.ctx)])
    usable = (positions_of(span_order, lay.c, slots)[None, :] < lengths[:, None]).astype(F32)[..., None]
    cosines, sines = rope_tables(pos)
    length = slots * lay.ctx

    def tokens(x):
        return lax.all_gather(x, "ctx", axis=1, tiled=True).reshape(micro * length, width)

    def own(x):
        x = x.astype(BF).reshape(micro, length, width)
        return lax.psum_scatter(x, "ctx", scatter_dimension=1, tiled=True).astype(F32)

    spread, collect = lay.spread, lay.gather_sum
    wqkv = spread(lay.exchange(pack_attention(w_query, w_key, w_value, gain)).reshape(KV * rows, -1))
    wgu = spread(lay.exchange(pack_mlp(w_gate, w_up, gain_m, nz)).reshape(KV * rows, -1))
    wout = spread(send(w_out, lay.place))
    wdown = spread(w_down)
    source = hidden_in.astype(F32)
    unit, inverse = unit_rows(source)
    xs = tokens(unit.astype(BF))
    g_res = out_grad.astype(F32) * usable
    g_mlp = tokens(g_res.astype(BF))
    pre = mm(xs, wqkv).reshape(micro, length, -1)
    attended, kept = attend(pre, pos, lengths, cosines, sines)
    att = attended.reshape(micro * length, QW)
    residual = source + own(mm(att, wout))
    unit_m, inverse_m = unit_rows(residual)
    xm = tokens(unit_m.astype(BF))
    gate_up = mm(xm, wgu)
    hidden = swiglu(gate_up)
    block_out = (usable * (residual + own(mm(hidden, wdown)))).astype(BF)
    grad_down = collect(mm_lt(hidden, g_mlp)).astype(F32)
    g_gu = swiglu_back(gate_up, mm_rt(g_mlp, wdown))
    v_gu = lay.exchange(collect(mm_lt(xm, g_gu)).reshape(KV, rows, -1))
    u_gate, u_up = unpack_mlp(v_gu, nz)
    g_res2 = g_res + unit_back(own(mm_rt(g_gu, wgu)), unit_m, inverse_m)
    g_branch = tokens(g_res2.astype(BF))
    grad_out = send(collect(mm_lt(att, g_branch)), lay.back).astype(F32)
    g_att = mm_rt(g_branch, wout).astype(BF).reshape(micro, length, QW)
    g_pre = attend_back(g_att, kept, cosines, sines).reshape(micro * length, -1)
    v_qkv = lay.exchange(collect(mm_lt(xs, g_pre)).reshape(KV, rows, -1))
    u_q, u_k, u_v = unpack_attention(v_qkv)
    grad_in = (g_res2 + unit_back(own(mm_rt(g_pre, wqkv)), unit, inverse)).astype(BF)
    return (
        block_out, grad_in, paired((w_query, u_q), (w_key, u_k), (w_value, u_v)),
        u_q * gain, u_k * gain, u_v * gain, grad_out,
        paired((w_gate, u_gate), (w_up, u_up)), u_gate * gain_m, u_up * gain_m, grad_down,
    )


def solution(mesh):
    rows = P(AXES, None)
    tokens = P("fsdp", "ctx", None)
    line = mesh.shape["ctx"] == 4 and mesh.shape["fsdp"] == 8
    return jax.shard_map(
        on_line if line else anywhere,
        mesh=mesh,
        in_specs=(tokens, P("fsdp"), P(), P(AXES), rows, rows, rows, rows, P(AXES), rows, rows, rows, tokens),
        out_specs=(tokens, tokens, P(AXES), rows, rows, rows, rows, P(AXES), rows, rows, rows),
        check_vma=False,
    )
```

```python
import jax
import jax.numpy as jnp
import numpy as np
from jax import lax
from jax.experimental import pallas as pl
from jax.experimental.pallas import tpu as pltpu
from jax.sharding import PartitionSpec as P

H = 16
KV = 8
HD = 96
GROUP = H // KV
QW = GROUP * HD
AXES = ("fsdp", "ctx")

epsilon = 1e-05
rope_base = 100000.0
masked_score = -1e30
scale = HD ** (-0.5)
BF = jnp.bfloat16
F32 = jnp.float32


def mm(left, right):
    return jnp.dot(left, right, preferred_element_type=F32)


def mm_lt(left, right):
    return lax.dot_general(left, right, (((0,), (0,)), ((), ())), preferred_element_type=F32)


def mm_rt(left, right):
    return lax.dot_general(left, right, (((1,), (1,)), ((), ())), preferred_element_type=F32)


def plus(a, b):
    return a + b


def send(x, pairs):
    return lax.ppermute(x, AXES, pairs)


def unit_of_work(go, body, *args):
    def idle(*args):
        return jax.tree.map(lambda leaf: jnp.zeros(leaf.shape, leaf.dtype), jax.eval_shape(body, *args))

    return lax.cond(go, body, idle, *args)


def fence(*items):
    return lax.optimization_barrier(items)


class Layout:
    def __init__(self):
        self.ctx = lax.axis_size("ctx")
        self.fsdp = lax.axis_size("fsdp")
        self.tpf = KV // self.ctx
        self.nz = self.fsdp // self.tpf
        self.total = self.fsdp * self.ctx
        self.fast = self.ctx == 4 and self.tpf == 2 and self.nz == 4
        self.f = lax.axis_index("fsdp")
        self.c = lax.axis_index("ctx")
        self.z = self.f // self.tpf
        self.place = [(b, (b % self.nz) * KV + b // self.nz) for b in range(self.total)]
        self.back = [(d, s) for s, d in self.place]

    def exchange(self, x):
        if self.tpf == 1:
            return lax.all_to_all(x, "ctx", split_axis=0, concat_axis=0, tiled=True)
        groups = [[z * KV + i for i in range(KV)] for z in range(self.nz)]
        return lax.all_to_all(
            x, AXES, split_axis=0, concat_axis=0, tiled=True, axis_index_groups=groups
        )

    def lines(self):
        return [[z * KV + i for z in range(self.nz)] for i in range(KV)]

    def spread(self, x):
        if self.tpf == 1:
            return lax.all_gather(x, "fsdp", axis=0, tiled=True)
        return lax.all_gather(x, AXES, axis=0, tiled=True, axis_index_groups=self.lines())

    def gather_sum(self, x):
        x = x.astype(BF)
        if self.tpf == 1:
            return lax.psum_scatter(x, "fsdp", scatter_dimension=0, tiled=True)
        return lax.psum_scatter(
            x, AXES, scatter_dimension=0, tiled=True, axis_index_groups=self.lines()
        )


class Line(Layout):
    def __init__(self):
        super().__init__()
        total = self.total
        self.core = [(d, d ^ 1) for d in range(total)]
        self.first = [(d, d ^ (2 if d & 1 else 4)) for d in range(total)]
        self.second = [(d, d ^ (4 if d & 1 else 2)) for d in range(total)]
        self.xflip = [(d, d ^ 4) for d in range(total)]

        def planes(pairs):
            return [(s * KV + i, d * KV + i) for s, d in pairs for i in range(KV)]

        self.pair = planes([(0, 1), (1, 0), (2, 3), (3, 2)])
        self.inner = planes([(1, 2), (2, 1)])
        self.outward = planes([(1, 0), (2, 3)])
        self.inward = planes([(0, 1), (3, 2)])
        z = self.z
        low = z < 2
        self.order = [z, z ^ 1, jnp.where(low, 2, 1), jnp.where(low, 3, 0)]
        table = ((0, 1, 3, 3), (1, 0, 2, 2), (2, 2, 0, 1), (3, 3, 1, 0))
        self.slot = [
            jnp.where(z == 0, r[0], jnp.where(z == 1, r[1], jnp.where(z == 2, r[2], r[3])))
            for r in table
        ]

    def take_columns(self, x, blocks):
        width = x.shape[-1] // self.nz
        return jnp.concatenate(
            [lax.dynamic_slice_in_dim(x, k * width, width, axis=-1) for k in blocks], axis=-1
        )

    def take_rows(self, pieces):
        full = jnp.stack(pieces)
        return jnp.concatenate(
            [lax.dynamic_index_in_dim(full, k, axis=0, keepdims=False) for k in self.slot], axis=0
        )

    def to_pieces(self, x):
        full = x.reshape((self.nz, x.shape[0] // self.nz) + x.shape[1:])
        return [lax.dynamic_index_in_dim(full, k, axis=0, keepdims=False) for k in self.order]

    def all_tokens(self, x):
        x = jnp.stack([x, send(x, self.first)])
        x = jnp.stack([x, send(x, self.second)])
        x = jnp.stack([x, send(x, self.core)])
        return x.reshape(-1, x.shape[-1])

    def plane_tokens(self, x):
        x = jnp.stack([x, send(x, self.first)])
        x = jnp.stack([x, send(x, self.second)])
        other = send(x, self.core)
        return x.reshape(-1, x.shape[-1]), other.reshape(-1, x.shape[-1])

    def collect_tokens(self, x, slots):
        x = x.reshape(2, 2, 2, 2, slots, x.shape[-1])
        x = plus(x[0], send(x[1], self.core))
        x = plus(x[0], send(x[1], self.second))
        return x[0].astype(F32) + send(x[1], self.first).astype(F32)

    def to_seqs(self, x, slots):
        x = x.reshape(2, 2, 2, 2, slots, x.shape[-1])
        halves = []
        for dc in range(2):
            even = ((self.c & 1) ^ dc) == 0
            h = x[dc]
            halves.append(jnp.where(even, jnp.swapaxes(h, 0, 1), h))
        x = jnp.stack(halves, axis=0)
        x = jnp.transpose(x, (1, 3, 0, 2, 4, 5))
        return x.reshape(4, 4 * slots, x.shape[-1])

    def from_seqs(self, x, slots):
        x = x.reshape(2, 2, 2, 2, slots, x.shape[-1])
        x = jnp.transpose(x, (2, 0, 3, 1, 4, 5))
        halves = []
        for dc in range(2):
            even = ((self.c & 1) ^ dc) == 0
            h = x[dc]
            halves.append(jnp.where(even, jnp.swapaxes(h, 0, 1), h))
        return jnp.stack(halves, axis=0).reshape(16 * slots, x.shape[-1])


def positions_of(span_order, index, slots):
    span_len = slots // 2
    at = jnp.arange(slots, dtype=jnp.int32)
    pair = lax.dynamic_slice_in_dim(span_order, 2 * index, 2)
    return jnp.where(at < span_len, pair[0], pair[1]) * span_len + at % span_len


def rope_tables(pos):
    frequency = rope_base ** (-2.0 * jnp.arange(HD // 2, dtype=F32) / HD)
    angles = pos.astype(F32)[:, None] * frequency[None, :]
    return jnp.cos(angles), jnp.sin(angles)


def rotate(v, cosines, sines):
    half = HD // 2
    co, si = cosines[None, :, None, :], sines[None, :, None, :]
    one, two = v[..., :half], v[..., half:]
    return jnp.concatenate([one * co - two * si, two * co + one * si], axis=-1)


def unit_rows(x):
    inverse = lax.rsqrt(jnp.mean(x * x, axis=-1, keepdims=True) + epsilon)
    return x * inverse, inverse


def unit_back(scaled, unit, inverse):
    return inverse * (scaled - unit * jnp.mean(scaled * unit, axis=-1, keepdims=True))


def attend(pre, pos, seq_len, cosines, sines):
    seqs, length, _ = pre.shape
    q = rotate(pre[..., :QW].reshape(seqs, length, GROUP, HD), cosines, sines).astype(BF)
    k = rotate(pre[..., QW : QW + HD].reshape(seqs, length, 1, HD), cosines, sines)[:, :, 0].astype(BF)
    v = pre[..., QW + HD :].astype(BF)
    allowed = (pos[None, None, :] <= pos[None, :, None]) & (
        pos[None, None, :] < seq_len[:, None, None]
    )
    scores = jnp.einsum("sqgd,snd->sgqn", q, k, preferred_element_type=F32) * scale
    scores = jnp.where(allowed[:, None], scores, masked_score)
    top = jnp.max(scores, axis=-1, keepdims=True)
    expo = jnp.exp(scores - top)
    probs = expo / jnp.sum(expo, axis=-1, keepdims=True)
    low = probs.astype(BF)
    attended = jnp.einsum("sgqn,snd->sqgd", low, v, preferred_element_type=F32)
    return attended.astype(BF).reshape(seqs, length, QW), (q, k, v, probs, low)


def attend_back(g_att, kept, cosines, sines):
    q, k, v, probs, low = kept
    seqs, length, _ = g_att.shape
    g_att = g_att.reshape(seqs, length, GROUP, HD)
    g_probs = jnp.einsum("sqgd,snd->sgqn", g_att, v, preferred_element_type=F32)
    inner = jnp.sum(probs * g_probs, axis=-1, keepdims=True)
    g_scores = (probs * (g_probs - inner)).astype(BF)
    g_q = jnp.einsum("sgqn,snd->sqgd", g_scores, k, preferred_element_type=F32) * scale
    g_k = jnp.einsum("sgqn,sqgd->snd", g_scores, q, preferred_element_type=F32) * scale
    g_v = jnp.einsum("sgqn,sqgd->snd", low, g_att, preferred_element_type=F32)
    return jnp.concatenate(
        [
            rotate(g_q, cosines, -sines).astype(BF).reshape(seqs, length, QW),
            rotate(g_k[:, :, None], cosines, -sines).astype(BF)[:, :, 0],
            g_v.astype(BF),
        ],
        axis=-1,
    )


def swiglu(gate_up):
    half = gate_up.shape[-1] // 2
    gate, up = gate_up[:, :half], gate_up[:, half:]
    return (jax.nn.silu(gate) * up).astype(BF)


def swiglu_back(gate_up, g_hidden):
    half = gate_up.shape[-1] // 2
    gate, up = gate_up[:, :half], gate_up[:, half:]
    sig = jax.nn.sigmoid(gate)
    g_gate = (g_hidden * up * sig * (1.0 + gate * (1.0 - sig))).astype(BF)
    g_up = (g_hidden * gate * sig).astype(BF)
    return jnp.concatenate([g_gate, g_up], axis=-1)


def pack_attention(w_query, w_key, w_value, gain):
    rows = w_query.shape[0]
    parts = [
        (w.astype(F32) * gain).astype(BF).reshape(rows, KV, w.shape[1] // KV)
        for w in (w_query, w_key, w_value)
    ]
    return jnp.transpose(jnp.concatenate(parts, axis=2), (1, 0, 2))


def unpack_attention(u):
    u = jnp.transpose(u, (1, 0, 2)).astype(F32)
    rows = u.shape[0]
    return (
        u[..., :QW].reshape(rows, KV * QW),
        u[..., QW : QW + HD].reshape(rows, KV * HD),
        u[..., QW + HD :].reshape(rows, KV * HD),
    )


def pack_mlp(w_gate, w_up, gain, nz):
    rows = w_gate.shape[0]

    def columns(w):
        w = (w.astype(F32) * gain).astype(BF).reshape(rows, nz, KV, -1)
        return jnp.transpose(w, (2, 0, 1, 3)).reshape(KV, rows, -1)

    return jnp.concatenate([columns(w_gate), columns(w_up)], axis=2)


def unpack_mlp(u, nz):
    rows = u.shape[1]
    u = u.reshape(KV, rows, 2, nz, -1)
    u = jnp.transpose(u, (2, 1, 3, 0, 4)).reshape(2, rows, -1).astype(F32)
    return u[0], u[1]


SMEM = pl.BlockSpec(memory_space=pltpu.SMEM)
VMEM = pl.BlockSpec(memory_space=pltpu.VMEM)
WIDE = QW + 2 * HD
FREE = pl.CostEstimate(flops=0, bytes_accessed=0, transcendentals=0)
ROOM = pltpu.CompilerParams(vmem_limit_bytes=56 * 1024 * 1024)


def shaped(*shape, dtype=BF):
    return jax.ShapeDtypeStruct(shape, dtype)


def kernel_call(body, outs, scratch=()):
    def call(scalars, *arrays):
        return pl.pallas_call(
            body,
            out_shape=outs,
            in_specs=[SMEM] * len(scalars) + [VMEM] * len(arrays),
            out_specs=jax.tree.map(lambda _: VMEM, outs),
            scratch_shapes=list(scratch),
            compiler_params=ROOM,
            cost_estimate=FREE,
        )(*scalars, *arrays)

    return call


def moving_call(body, outs, scratch=(), copies=1):
    def call(scalars, *arrays):
        anywhere_spec = pl.BlockSpec(memory_space=pl.ANY)
        return pl.pallas_call(
            body,
            out_shape=outs,
            in_specs=[SMEM] * len(scalars) + [pl.BlockSpec(memory_space=pltpu.HBM)] * len(arrays),
            out_specs=jax.tree.map(lambda _: anywhere_spec, outs),
            scratch_shapes=list(scratch) + [pltpu.SemaphoreType.DMA((copies,))],
            compiler_params=ROOM,
            cost_estimate=FREE,
        )(*scalars, *arrays)

    return call


class Copies:
    def __init__(self, sems):
        self.sems = sems
        self.used = 0

    def start(self, source, target):
        copy = pltpu.make_async_copy(source, target, self.sems.at[self.used])
        self.used += 1
        copy.start()
        return copy


def vmem(*arrays):
    return [pltpu.VMEM(a.shape, a.dtype) for a in arrays]


def dot(a, b, dims=((1,), (0,))):
    return lax.dot_general(a, b, (dims, ((), ())), preferred_element_type=F32)


LEFT_T = ((0,), (0,))
RIGHT_T = ((1,), (1,))


def block_rows(core, seq, dc, dy, slots):
    dx, m = seq // 2, seq % 2
    even = (core ^ dc) == 0
    s1 = jnp.where(even, dx, dy)
    s2 = jnp.where(even, dy, dx)
    return pl.multiple_of(((s2 * 2 + s1) * 2 + m) * slots, slots)


def blocks_of(slots):
    for dc in range(2):
        for dy in range(2):
            b = dc * 2 + dy
            yield dc, dy, slice(b * slots, (b + 1) * slots)


def spans_of(spans, ctx):
    out = []
    for dc in range(2):
        for dy in range(2):
            other = ctx ^ (dy * 2 + dc)
            out += [spans[2 * other], spans[2 * other + 1]]
    return out


def along(held, length, axis, shape):
    at = lax.broadcasted_iota(jnp.int32, shape, axis) % length
    step = length // len(held)
    pos = at % step
    for i, span in enumerate(held):
        pos = pos + jnp.where(at // step == i, span * step, 0)
    return pos


def rotary_rows(held, table, out):
    step = out.shape[0] // len(held)
    for i, span in enumerate(held):
        out[i * step : (i + 1) * step, :] = table[pl.ds(pl.multiple_of(span * step, step), step), :]


def rotary_copies(copies, held, table, out):
    step = out.shape[0] // len(held)
    return [
        copies.start(table.at[pl.ds(pl.multiple_of(span * step, step), step)], out.at[pl.ds(i * step, step)])
        for i, span in enumerate(held)
    ]


def turn(x, cosines, sines):
    half, width = HD // 2, x.shape[1]
    lane = lax.broadcasted_iota(jnp.int32, x.shape, 1) % HD
    partner = jnp.where(lane < half, pltpu.roll(x, width - half, 1), pltpu.roll(x, half, 1))
    return x * cosines + partner * sines


def probabilities(q, k, allowed):
    scores = jnp.where(allowed, dot(q, k, RIGHT_T) * scale, masked_score)
    expo = jnp.exp(scores - jnp.max(scores, axis=-1, keepdims=True))
    return expo / jnp.sum(expo, axis=-1, keepdims=True)


def heads_of(x):
    return [x[:, h * HD : (h + 1) * HD] for h in range(x.shape[1] // HD)]


def assemble(meta, pieces, out):
    p0, p1, p2, p3, p4, p5 = pieces
    step = p0.shape[0]
    for s, parts in enumerate(((p0,), (p1,), (p2, p3), (p4, p5))):
        piece = parts[0][...]
        if len(parts) > 1:
            piece = piece + parts[1][...]
        out[pl.ds(pl.multiple_of(meta[s] * step, step), step), :] = piece


def fetch_qkv(full, out):
    step = full.shape[2]
    for z in range(full.shape[0]):
        out[z * step : (z + 1) * step, :] = full[z, :step, :]


def fetch_out(full, out):
    nz, total, step = full.shape
    count = out.shape[1] // step
    rows = (total - step) // count
    for z in range(nz):
        for k in range(count):
            out[z * rows : (z + 1) * rows, k * step : (k + 1) * step] = full[
                z, step + k * rows : step + (k + 1) * rows, :
            ]


def stacked_columns(x, cut):
    return jnp.concatenate([x[:, k : k + cut] for k in range(0, x.shape[1], cut)], axis=0)


def column(row):
    n = row.shape[1]
    same = lax.broadcasted_iota(jnp.int32, (n, n), 0) == lax.broadcasted_iota(jnp.int32, (n, n), 1)
    return jnp.sum(jnp.where(same, row, 0.0), axis=1, keepdims=True)


def row_of(col):
    n = col.shape[0]
    same = lax.broadcasted_iota(jnp.int32, (n, n), 0) == lax.broadcasted_iota(jnp.int32, (n, n), 1)
    return jnp.sum(jnp.where(same, col, 0.0), axis=0, keepdims=True)


def pack_attention_kernel(wq, wk, wv, gain, out):
    g = column(gain[...].astype(F32))
    q, k, v = ((w[...].astype(F32) * g).astype(BF) for w in (wq, wk, wv))
    for j in range(KV):
        out[j] = jnp.concatenate(
            [q[:, j * QW : (j + 1) * QW], k[:, j * HD : (j + 1) * HD], v[:, j * HD : (j + 1) * HD]], axis=1
        )


def pack_mlp_kernel(wg, wu, gain, out):
    g = column(gain[...].astype(F32))
    half = out.shape[2] // 2
    blocks = 4
    hid = half // blocks
    for h, w in enumerate((wg, wu)):
        x = (w[...].astype(F32) * g).astype(BF)
        for z in range(blocks):
            for j in range(KV):
                out[j, :, h * half + z * hid : h * half + (z + 1) * hid] = x[
                    :, (z * KV + j) * hid : (z * KV + j + 1) * hid
                ]


def unpack_attention_kernel(u, wq, wk, wv, gain, gq, gk, gv, total):
    g = column(gain[...].astype(F32))
    acc = jnp.zeros(g.shape, F32)
    for w, out, lo, n in ((wq, gq, 0, QW), (wk, gk, QW, HD), (wv, gv, QW + HD, HD)):
        part = jnp.concatenate([u[j, :, lo : lo + n] for j in range(KV)], axis=1).astype(F32)
        out[...] = part * g
        acc += jnp.sum(part * w[...].astype(F32), axis=1, keepdims=True)
    total[...] = row_of(acc)


def unpack_mlp_kernel(u, wg, wu, gain, gg, gu, total):
    g = column(gain[...].astype(F32))
    acc = jnp.zeros(g.shape, F32)
    half = wg.shape[1] // KV
    blocks = 4
    hid = half // blocks
    for j in range(KV):
        x = u[j].astype(F32)
        for h, (w, out) in enumerate(((wg, gg), (wu, gu))):
            for z in range(blocks):
                at = slice((z * KV + j) * hid, (z * KV + j + 1) * hid)
                part = x[:, h * half + z * hid : h * half + (z + 1) * hid]
                out[:, at] = part * g
                acc += jnp.sum(part * w[:, at].astype(F32), axis=1, keepdims=True)
    total[...] = row_of(acc)


def usable_rows(lens, spans, ctx, shape):
    at = lax.broadcasted_iota(jnp.int32, shape, 0)
    slots = shape[0] // 2
    slot, step = at % slots, slots // 2
    pos = jnp.where(slot < step, spans[2 * ctx], spans[2 * ctx + 1]) * step + slot % step
    length = jnp.where(at < slots, lens[0], lens[1])
    return (pos < length).astype(F32)


def prepare_kernel(meta, lens, spans, x, g, xhat, inverse, g_low):
    v = x[...].astype(F32)
    inv = lax.rsqrt(jnp.mean(v * v, axis=-1, keepdims=True) + epsilon)
    inverse[...] = inv
    xhat[...] = (v * inv).astype(BF)
    g_low[...] = (g[...].astype(F32) * usable_rows(lens, spans, meta[5], inverse.shape)).astype(BF)


def finish_kernel(meta, lens, spans, residual, a, b, out):
    total = residual[...] + a[...].astype(F32) + b[...].astype(F32)
    out[...] = (total * usable_rows(lens, spans, meta[5], (total.shape[0], 1))).astype(BF)


def attention_kernel(
    meta, lens, spans, xa, xb, full, cos_table, sin_table, wqkv, qkv, att, xseq, cosines, sines
):
    core, ctx = meta[4], meta[5]
    slots = xa.shape[0] // 8
    length = xseq.shape[0]
    fetch_qkv(full, wqkv)
    held = spans_of(spans, ctx)
    rotary_rows(held, cos_table, cosines)
    rotary_rows(held, sin_table, sines)
    posc = along(held, length, 0, (GROUP * length, length))
    posr = along(held, length, 1, (GROUP * length, length))
    causal = posr <= posc

    def one(seq, carry):
        for dc, dy, rows in blocks_of(slots):
            xseq[rows, :] = (xa, xb)[dc][pl.ds(block_rows(core, seq, dc, dy, slots), slots), :]
        low = turn(dot(xseq[...], wqkv[...]), cosines[...], sines[...]).astype(BF)
        qkv[seq] = low
        one_q, two_q, k, v = heads_of(low)
        q = jnp.concatenate([one_q, two_q], axis=0)
        allowed = causal & (posr < lens[seq])
        mixed = dot(probabilities(q, k, allowed).astype(BF), v)
        out = jnp.concatenate([mixed[:length], mixed[length:]], axis=1).astype(BF)
        for dc, dy, rows in blocks_of(slots):
            att[dc, pl.ds(block_rows(core, seq, dc, dy, slots), slots), :] = out[rows]
        return carry

    lax.fori_loop(0, 4, one, 0, unroll=True)


def project_kernel(att, full, wout, mine, theirs):
    fetch_out(full, wout)
    theirs[...] = dot(att[1], wout[...]).astype(BF)
    mine[...] = dot(att[0], wout[...]).astype(BF)


def attention_back_kernel(
    meta, lens, spans,
    h_ga, h_gb, h_att, h_wout, h_wqkv, h_qkv, h_xa, h_xb, cos_table, sin_table,
    o_mine, o_theirs, o0, o1, o2, o3,
    ga, gb, att, wout, wqkv, qkv, xa, xb, mine, theirs, u0, u1, u2, u3, g_pre, gseq, cosines, sines, out_grad, sems,
):
    copies = Copies(sems)
    held = spans_of(spans, meta[5])
    first = [copies.start(h, v) for h, v in ((h_wout, wout), (h_qkv, qkv), (h_ga, ga), (h_gb, gb))]
    first += rotary_copies(copies, held, cos_table, cosines) + rotary_copies(copies, held, sin_table, sines)
    for c in first:
        c.wait()
    later = [copies.start(h, v) for h, v in ((h_xa, xa), (h_xb, xb), (h_att, att), (h_wqkv, wqkv))]
    core, ctx = meta[4], meta[5]
    slots = ga.shape[0] // 8
    length = gseq.shape[0]
    posc = along(held, length, 0, (GROUP * length, length))
    posr = along(held, length, 1, (GROUP * length, length))
    causal = posr <= posc

    def one(seq, carry):
        for dc, dy, rows in blocks_of(slots):
            gseq[rows, :] = (ga, gb)[dc][pl.ds(block_rows(core, seq, dc, dy, slots), slots), :]
        g_att = dot(gseq[...], wout[...], RIGHT_T).astype(BF)
        one_q, two_q, k, v = heads_of(qkv[seq])
        q = jnp.concatenate([one_q, two_q], axis=0)
        g = jnp.concatenate(heads_of(g_att), axis=0)
        allowed = causal & (posr < lens[seq])
        p = probabilities(q, k, allowed)
        g_p = dot(g, v, RIGHT_T)
        g_s = (p * (g_p - jnp.sum(p * g_p, axis=-1, keepdims=True))).astype(BF)
        g_q = dot(g_s, k) * scale
        g_k = dot(g_s, q, LEFT_T) * scale
        g_v = dot(p.astype(BF), g, LEFT_T)
        full = jnp.concatenate([g_q[:length], g_q[length:], g_k, g_v], axis=1)
        out = turn(full, cosines[...], -sines[...]).astype(BF)
        for dc, dy, rows in blocks_of(slots):
            g_pre[dc, pl.ds(block_rows(core, seq, dc, dy, slots), slots), :] = out[rows]
        return carry

    lax.fori_loop(0, 4, one, 0, unroll=True)
    for c in later:
        c.wait()
    gone = []
    out_grad[...] = (dot(att[0], ga[...], LEFT_T) + dot(att[1], gb[...], LEFT_T)).astype(BF)
    step = xa.shape[1] // 4
    block = u0.shape[1]
    count = out_grad.shape[1] // block
    low = out_grad.shape[0] // 4
    for s, u, o in ((3, u3, o3), (2, u2, o2), (1, u1, o1), (0, u0, o0)):
        at = pl.ds(pl.multiple_of(meta[s] * step, step), step)
        u[:step, :] = (dot(xa[:, at], g_pre[0], LEFT_T) + dot(xb[:, at], g_pre[1], LEFT_T)).astype(BF)
        at = pl.ds(pl.multiple_of(meta[s] * low, low), low)
        for k in range(count):
            u[step + k * low : step + (k + 1) * low, :] = out_grad[at, k * block : (k + 1) * block]
        gone.append(copies.start(u, o))
    theirs[...] = dot(g_pre[1], wqkv[...], RIGHT_T).astype(BF)
    gone.append(copies.start(theirs, o_theirs))
    mine[...] = dot(g_pre[0], wqkv[...], RIGHT_T).astype(BF)
    gone.append(copies.start(mine, o_mine))
    for c in gone:
        c.wait()


def mlp_kernel(
    meta,
    h_ma, h_mb, h_ea, h_eb, h_wgu, h0, h1, h2, h3, h4, h5,
    o_down_mine, o_down_theirs, o_mine, o_theirs, o_u,
    x, g, back, down, wgu, d0, d1, d2, d3, d4, d5, u, hidden, g_gu, wdown, sems,
):
    copies = Copies(sems)
    came = [copies.start(h_wgu, wgu), copies.start(h_mb, x.at[1])]
    pieces = (d0, d1, d2, d3, d4, d5)
    came += [copies.start(h, d) for h, d in zip((h0, h1, h2, h3, h4, h5), pieces)]
    came += [copies.start(h_eb, g.at[1])]
    later = [copies.start(h_ma, x.at[0]), copies.start(h_ea, g.at[0])]
    half = wgu.shape[1] // 2
    for c in came:
        c.wait()
    assemble(meta, pieces, wdown)
    out_copies = [
        pltpu.make_async_copy(v, o, sems.at[copies.used + k])
        for k, (v, o) in enumerate(
            ((back.at[1], o_theirs), (down.at[1], o_down_theirs), (back.at[0], o_mine), (down.at[0], o_down_mine))
        )
    ]
    copies.used += 4

    def one(i, carry):
        part = 1 - i

        @pl.when(i == 1)
        def _():
            for c in later:
                c.wait()

        gate_up = dot(x[part], wgu[...])
        gate, up = gate_up[:, :half], gate_up[:, half:]
        sig = 1.0 / (1.0 + jnp.exp(-gate))
        act = gate * sig
        hidden[part] = (act * up).astype(BF)
        g_hidden = dot(g[part], wdown[...], RIGHT_T)
        g_gu[part, :, :half] = (g_hidden * up * sig * (1.0 + gate * (1.0 - sig))).astype(BF)
        g_gu[part, :, half:] = (g_hidden * act).astype(BF)
        back[part] = dot(g_gu[part], wgu[...], RIGHT_T).astype(BF)
        down[part] = dot(hidden[part], wdown[...]).astype(BF)

        @pl.when(i == 0)
        def _():
            out_copies[0].start()
            out_copies[1].start()

        @pl.when(i == 1)
        def _():
            out_copies[2].start()
            out_copies[3].start()

        return carry

    lax.fori_loop(0, 2, one, 0)
    nz, _, wide = u.shape
    piece = x.shape[2] // nz
    step = hidden.shape[2] // nz
    base = copies.used

    def grads(z, carry):
        at = pl.ds(pl.multiple_of(z * piece, piece), piece)
        both = dot(x[0, :, at], g_gu[0], LEFT_T) + dot(x[1, :, at], g_gu[1], LEFT_T)
        u[z, :piece, :] = both.astype(BF)
        at = pl.ds(pl.multiple_of(z * step, step), step)
        both = (dot(hidden[0, :, at], g[0], LEFT_T) + dot(hidden[1, :, at], g[1], LEFT_T)).astype(BF)
        u[z, piece : piece + step, :] = both[:, :wide]
        rest = both.shape[1] - wide
        u[z, piece + step :, :rest] = both[: step // 2, wide:]
        u[z, piece + step :, rest:] = both[step // 2 :, wide:]
        pltpu.make_async_copy(u.at[z], o_u.at[z], sems.at[base + z]).start()
        return carry

    lax.fori_loop(0, nz, grads, 0)
    for c in out_copies:
        c.wait()
    for z in range(nz):
        pltpu.make_async_copy(u.at[z], o_u.at[z], sems.at[base + z]).wait()


def unpack_down_kernel(u, out):
    step, wide = out.shape[0], u.shape[1]
    rest = out.shape[1] - wide
    out[:, :wide] = u[:step, :].astype(F32)
    out[: step // 2, wide:] = u[step:, :rest].astype(F32)
    out[step // 2 :, wide:] = u[step:, rest:].astype(F32)


def sums_kernel(a, b, c, d, ab, cd):
    ab[...] = a[...] + b[...]
    cd[...] = c[...] + d[...]


def last_sum_kernel(a, b, c, qkv, out):
    total = (a[...].astype(F32) + b[...].astype(F32) + c[...].astype(F32)).astype(BF)
    blocks, rows, width = qkv.shape
    for j in range(blocks):
        qkv[j] = total[j * rows : (j + 1) * rows]
    low = out.shape[0]
    for k in range(out.shape[1] // width):
        at = blocks * rows + k * low
        out[:, k * width : (k + 1) * width] = total[at : at + low]


def norm_kernel(source, a, b, residual, xhat, inverse):
    r = source[...].astype(F32) + a[...].astype(F32) + b[...].astype(F32)
    inv = lax.rsqrt(jnp.mean(r * r, axis=-1, keepdims=True) + epsilon)
    residual[...] = r
    inverse[...] = inv
    xhat[...] = (r * inv).astype(BF)


def norm_back(g_res, source, inverse, a, b):
    scaled = a[...].astype(F32) + b[...].astype(F32)
    inv = inverse[...]
    unit = source[...].astype(F32) * inv
    back = inv * (scaled - unit * jnp.mean(scaled * unit, axis=-1, keepdims=True))
    return g_res[...].astype(F32) + back


def norm_back_kernel(g_res, source, inverse, a, b, out, low):
    g = norm_back(g_res, source, inverse, a, b)
    out[...] = g
    low[...] = g.astype(BF)


def norm_back_low_kernel(g_res, source, inverse, a, b, low):
    low[...] = norm_back(g_res, source, inverse, a, b).astype(BF)


def rotary_constants(total):
    frequency = rope_base ** (-2.0 * np.arange(HD // 2, dtype=np.float32) / HD).astype(np.float32)
    angles = np.arange(total, dtype=np.float32)[:, None] * frequency[None, :].astype(np.float32)
    c, s = np.cos(angles), np.sin(angles)
    flat, signed = np.concatenate([c, c], 1), np.concatenate([-s, s], 1)
    cosines = np.concatenate([flat] * (GROUP + 1) + [np.ones_like(flat)], 1)
    sines = np.concatenate([signed] * (GROUP + 1) + [np.zeros_like(flat)], 1)
    return jnp.asarray(cosines, F32), jnp.asarray(sines, F32)


def paired(*items):
    return sum(jnp.sum(w.astype(F32) * g, axis=1) for w, g in items)


def on_line(
    hidden_in, lengths, span_order, attn_gain, w_query, w_key, w_value, w_out,
    mlp_gain, w_gate, w_up, w_down, out_grad,
):
    lay = Line()
    _, slots, width = hidden_in.shape
    rows, nz = w_query.shape[0], lay.nz
    tokens, length, own = 16 * slots, 4 * slots, 2 * slots
    go = lengths[0] > 0
    meta = jnp.stack([k.astype(jnp.int32) for k in (*lay.order, lay.c & 1, lay.c)])
    gain, gain_m = attn_gain[None, :], mlp_gain[None, :]
    cos_table, sin_table = rotary_constants(length)

    def halves(x):
        return x.reshape(2, x.shape[0] // 2, width)

    wide = w_gate.shape[1] * 2 // KV
    cut = wide // 2
    tables = [pltpu.VMEM((length, WIDE), F32)] * 2

    def flat(x):
        return x.reshape(-1, width)

    d1 = send(w_down, lay.pair)
    d2 = send(w_down, lay.inner)
    q0 = lay.exchange(
        kernel_call(pack_attention_kernel, shaped(KV, rows, WIDE))((), w_query, w_key, w_value, gain)
    )
    theirs = send(lengths, lay.xflip)
    o0 = send(w_out, lay.place)
    gu_s = kernel_call(pack_mlp_kernel, shaped(KV, rows, wide))((), w_gate, w_up, gain_m)
    xhat, inverse, g_low = kernel_call(
        prepare_kernel, (shaped(own, width), shaped(own, 1, dtype=F32), shaped(own, width))
    )((meta, lengths, span_order), hidden_in.reshape(own, width), out_grad.reshape(own, width))
    q0, d1, d2, theirs, gu_s, xhat, g_low = fence(q0, d1, d2, theirs, gu_s, xhat, g_low)
    d3 = send(d2, lay.outward)
    d4 = send(d1, lay.inner)
    x1 = send(xhat, lay.first)
    attn_piece = jnp.concatenate([q0.reshape(KV * rows, WIDE), stacked_columns(o0, WIDE)], axis=0)
    d3, d4, x1, attn_piece = fence(d3, d4, x1, attn_piece)
    attn_full = lay.spread(attn_piece)

    def gather(xhat, x1, g_low, gu_s):
        gu0 = lay.exchange(gu_s)
        x01 = jnp.stack([xhat, x1])
        x2 = send(x01, lay.second)
        x2, gu0, x01, g_low = fence(x2, gu0, x01, g_low)
        x0123 = jnp.stack([x01, x2])
        x3 = send(x0123, lay.core)
        e1 = send(g_low, lay.first)
        x3, x0123, e1 = fence(x3, x0123, e1)
        e01 = jnp.stack([g_low, e1])
        return x0123, x3, gu0, e01

    xa, xb, gu0, e01 = unit_of_work(go, gather, xhat, x1, g_low, gu_s)
    attn_full, gu0 = fence(attn_full, gu0)
    wgu = lay.spread(gu0.reshape(KV * rows, wide))
    attn_full = attn_full.reshape(nz, -1, WIDE)
    seq_len = jnp.concatenate([lengths, theirs])

    def forward(meta, seq_len, span_order, xa, xb, attn_full, cos_table, sin_table, hidden_in, e01, d4):
        e2 = send(e01, lay.second)
        wqkv, qkv, att = kernel_call(
            attention_kernel,
            (shaped(width, WIDE), shaped(4, length, WIDE), shaped(2, tokens // 2, QW)),
            scratch=[pltpu.VMEM((length, width), BF)] + tables,
        )((meta, seq_len, span_order), flat(xa), flat(xb), attn_full, cos_table, sin_table)
        wqkv, qkv, att, e2 = fence(wqkv, qkv, att, e2)
        wout, mine, other = kernel_call(
            project_kernel, (shaped(QW, width), shaped(tokens // 2, width), shaped(tokens // 2, width))
        )((), att, attn_full)
        got = send(other, lay.core)
        r = halves(plus(mine, got))
        e0123 = jnp.stack([e01, e2])
        r, e0123 = fence(r, e0123)
        got = send(r[1], lay.second)
        e3 = send(e0123, lay.core)
        got, e3, r = fence(got, e3, r)
        r = halves(plus(r[0], got))
        got = send(r[1], lay.first)
        residual, xm0, inverse_m = kernel_call(
            norm_kernel, (shaped(own, width, dtype=F32), shaped(own, width), shaped(own, 1, dtype=F32))
        )((), hidden_in.reshape(own, width), r[0], got)
        m01 = jnp.stack([xm0, send(xm0, lay.first)])
        m01, d4 = fence(m01, d4)
        m2 = send(m01, lay.second)
        d5 = send(d4, lay.outward)
        m2, d5 = fence(m2, d5)
        ma = jnp.stack([m01, m2])
        mb = send(ma, lay.core)
        return wqkv, qkv, att, wout, residual, inverse_m, flat(ma), flat(mb), flat(e0123), flat(e3), d5

    wqkv, qkv, att, wout, residual, inverse_m, ma, mb, ea, eb, d5 = unit_of_work(
        go, forward, meta, seq_len, span_order, xa, xb, attn_full, cos_table, sin_table, hidden_in, e01, d4
    )
    half_rows = shaped(tokens // 2, width)
    low = w_down.shape[0]
    piece = KV * rows + low * width // wide
    outs = (half_rows, half_rows, half_rows, half_rows, shaped(nz, piece, wide))
    ins = (ma, mb, ea, eb, wgu, w_down, d1, d2, d3, d4, d5)
    down_mine, down_other, mine, other, u_mlp = moving_call(
        mlp_kernel,
        outs,
        scratch=[pltpu.VMEM((2, tokens // 2, width), BF)] * 4
        + vmem(*ins[4:], outs[4])
        + [pltpu.VMEM((2, tokens // 2, cut), BF), pltpu.VMEM((2, tokens // 2, wide), BF), pltpu.VMEM((cut, width), BF)],
        copies=len(ins) + 4 + nz,
    )((meta,), *ins)
    v_mlp = lay.gather_sum(u_mlp.reshape(nz * piece, wide))
    both = KV * rows + QW // nz * width // WIDE

    def backward(
        meta, seq_len, lengths, span_order, mine, other, down_mine, down_other, g_low, residual, inverse_m, att, wqkv, wout, qkv,
        xa, xb, cos_table, sin_table,
    ):
        got = send(other, lay.core)
        got, mine = fence(got, mine.astype(F32))
        r = halves((mine + got.astype(F32)).astype(BF))
        r = halves(plus(r[0], send(r[1], lay.second)))
        got = send(r[1], lay.first)
        got_down = send(down_other, lay.core)
        g_res2, h0 = kernel_call(
            norm_back_kernel, (shaped(own, width, dtype=F32), shaped(own, width))
        )((), g_low, residual, inverse_m, r[0], got)
        ga, gb = lay.plane_tokens(h0)
        d = halves(plus(down_mine, got_down))
        ga, gb, d = fence(ga, gb, d)
        got_down = send(d[1], lay.second)
        outs = [half_rows, half_rows] + [shaped(both, WIDE)] * nz
        ins = (ga, gb, att, wout, wqkv, qkv, flat(xa), flat(xb))
        mine, other, u0, u1, u2, u3 = moving_call(
            attention_back_kernel,
            outs,
            scratch=vmem(*ins, *outs)
            + [pltpu.VMEM((2, tokens // 2, WIDE), BF), pltpu.VMEM((length, width), BF)]
            + tables
            + [pltpu.VMEM((QW, width), BF)],
            copies=len(ins) + len(outs) + 16,
        )((meta, seq_len, span_order), *ins, cos_table, sin_table)
        got_down, mine, other, u0, u1, u2, u3 = fence(got_down, mine, other, u0, u1, u2, u3)
        d = halves(plus(d[0], got_down))
        return g_res2, mine, other, d[0], d[1], u3, u2, u1, u0

    g_res2, mine, other, da, db, u3, u2, u1, u0 = unit_of_work(
        go, backward, meta, seq_len, lengths, span_order, mine, other, down_mine, down_other, g_low, residual, inverse_m, att, wqkv,
        wout, qkv, xa, xb, cos_table, sin_table,
    )
    got = send(other, lay.core)
    got, mine = fence(got, mine)
    c5 = send(u3, lay.inward)
    r = halves(plus(mine, got))
    got = send(r[1], lay.second)
    v_gu = v_mlp[: KV * rows]
    c5, r, got, v_gu = fence(c5, r, got, v_gu)
    c4 = send(plus(u3, c5), lay.inner)
    c3 = send(u2, lay.inward)
    r = halves(plus(r[0], got))
    got = send(r[1], lay.first)
    got_down = send(db, lay.first)
    c4, c3, r, got, got_down = fence(c4, c3, r, got, got_down)
    c1, c2 = kernel_call(sums_kernel, (shaped(both, WIDE), shaped(both, WIDE)))((), u1, c4, u2, c3)
    c1 = send(c1, lay.pair)
    c2 = send(c2, lay.inner)
    v_gu = lay.exchange(v_gu.reshape(KV, rows, wide))
    grad_down = kernel_call(unpack_down_kernel, shaped(low, width, dtype=F32))((), v_mlp[KV * rows :])
    block_out = kernel_call(finish_kernel, shaped(own, width))(
        (meta, lengths, span_order), residual, da, got_down
    )
    grad_in = kernel_call(norm_back_low_kernel, shaped(own, width))(
        (), g_res2, hidden_in.reshape(own, width), inverse, r[0], got
    )
    c1, c2, v_gu, grad_down, block_out, grad_in = fence(c1, c2, v_gu, grad_down, block_out, grad_in)
    c0 = u0
    v_qkv, v_out = kernel_call(last_sum_kernel, (shaped(KV, rows, WIDE), shaped(*w_out.shape)))((), c0, c1, c2)
    grad_out = send(v_out, lay.back)

    def share(v_qkv, v_gu, w_gate, w_up, gain_m):
        v_qkv = lay.exchange(v_qkv)
        grad_gate, grad_up, total_m = kernel_call(
            unpack_mlp_kernel,
            (shaped(*w_gate.shape, dtype=F32), shaped(*w_up.shape, dtype=F32), shaped(1, rows, dtype=F32)),
        )((), v_gu, w_gate, w_up, gain_m)
        return v_qkv, grad_gate, grad_up, total_m

    v_qkv, grad_gate, grad_up, total_m = unit_of_work(go, share, v_qkv, v_gu, w_gate, w_up, gain_m)
    grad_out = grad_out.astype(F32)
    grad_query, grad_key, grad_value, total = kernel_call(
        unpack_attention_kernel,
        tuple(shaped(*w.shape, dtype=F32) for w in (w_query, w_key, w_value)) + (shaped(1, rows, dtype=F32),),
    )((), v_qkv, w_query, w_key, w_value, gain)
    return (
        block_out.reshape(hidden_in.shape), grad_in.reshape(hidden_in.shape), total[0], grad_query, grad_key, grad_value,
        grad_out, total_m[0], grad_gate, grad_up, grad_down,
    )


def anywhere(
    hidden_in, lengths, span_order, attn_gain, w_query, w_key, w_value, w_out,
    mlp_gain, w_gate, w_up, w_down, out_grad,
):
    lay = Layout()
    micro, slots, width = hidden_in.shape
    rows, nz = w_query.shape[0], lay.nz
    gain = attn_gain.astype(F32)[:, None]
    gain_m = mlp_gain.astype(F32)[:, None]
    pos = jnp.concatenate([positions_of(span_order, k, slots) for k in range(lay.ctx)])
    usable = (positions_of(span_order, lay.c, slots)[None, :] < lengths[:, None]).astype(F32)[..., None]
    cosines, sines = rope_tables(pos)
    length = slots * lay.ctx

    def tokens(x):
        return lax.all_gather(x, "ctx", axis=1, tiled=True).reshape(micro * length, width)

    def own(x):
        x = x.astype(BF).reshape(micro, length, width)
        return lax.psum_scatter(x, "ctx", scatter_dimension=1, tiled=True).astype(F32)

    spread, collect = lay.spread, lay.gather_sum
    wqkv = spread(lay.exchange(pack_attention(w_query, w_key, w_value, gain)).reshape(KV * rows, -1))
    wgu = spread(lay.exchange(pack_mlp(w_gate, w_up, gain_m, nz)).reshape(KV * rows, -1))
    wout = spread(send(w_out, lay.place))
    wdown = spread(w_down)
    source = hidden_in.astype(F32)
    unit, inverse = unit_rows(source)
    xs = tokens(unit.astype(BF))
    g_res = out_grad.astype(F32) * usable
    g_mlp = tokens(g_res.astype(BF))
    pre = mm(xs, wqkv).reshape(micro, length, -1)
    attended, kept = attend(pre, pos, lengths, cosines, sines)
    att = attended.reshape(micro * length, QW)
    residual = source + own(mm(att, wout))
    unit_m, inverse_m = unit_rows(residual)
    xm = tokens(unit_m.astype(BF))
    gate_up = mm(xm, wgu)
    hidden = swiglu(gate_up)
    block_out = (usable * (residual + own(mm(hidden, wdown)))).astype(BF)
    grad_down = collect(mm_lt(hidden, g_mlp)).astype(F32)
    g_gu = swiglu_back(gate_up, mm_rt(g_mlp, wdown))
    v_gu = lay.exchange(collect(mm_lt(xm, g_gu)).reshape(KV, rows, -1))
    u_gate, u_up = unpack_mlp(v_gu, nz)
    g_res2 = g_res + unit_back(own(mm_rt(g_gu, wgu)), unit_m, inverse_m)
    g_branch = tokens(g_res2.astype(BF))
    grad_out = send(collect(mm_lt(att, g_branch)), lay.back).astype(F32)
    g_att = mm_rt(g_branch, wout).astype(BF).reshape(micro, length, QW)
    g_pre = attend_back(g_att, kept, cosines, sines).reshape(micro * length, -1)
    v_qkv = lay.exchange(collect(mm_lt(xs, g_pre)).reshape(KV, rows, -1))
    u_q, u_k, u_v = unpack_attention(v_qkv)
    grad_in = (g_res2 + unit_back(own(mm_rt(g_pre, wqkv)), unit, inverse)).astype(BF)
    return (
        block_out, grad_in, paired((w_query, u_q), (w_key, u_k), (w_value, u_v)),
        u_q * gain, u_k * gain, u_v * gain, grad_out,
        paired((w_gate, u_gate), (w_up, u_up)), u_gate * gain_m, u_up * gain_m, grad_down,
    )


def solution(mesh):
    rows = P(AXES, None)
    tokens = P("fsdp", "ctx", None)
    line = mesh.shape["ctx"] == 4 and mesh.shape["fsdp"] == 8
    return jax.shard_map(
        on_line if line else anywhere,
        mesh=mesh,
        in_specs=(tokens, P("fsdp"), P(), P(AXES), rows, rows, rows, rows, P(AXES), rows, rows, rows, tokens),
        out_specs=(tokens, tokens, P(AXES), rows, rows, rows, rows, P(AXES), rows, rows, rows),
        check_vma=False,
    )
```

```python
import jax
import jax.numpy as jnp
import numpy as np
from jax import lax
from jax.experimental import pallas as pl
from jax.experimental.pallas import tpu as pltpu
from jax.sharding import PartitionSpec as P

H = 16
KV = 8
HD = 96
GROUP = H // KV
QW = GROUP * HD
AXES = ("fsdp", "ctx")

epsilon = 1e-05
rope_base = 100000.0
masked_score = -1e30
scale = HD ** (-0.5)
BF = jnp.bfloat16
F32 = jnp.float32


def mm(left, right):
    return jnp.dot(left, right, preferred_element_type=F32)


def mm_lt(left, right):
    return lax.dot_general(left, right, (((0,), (0,)), ((), ())), preferred_element_type=F32)


def mm_rt(left, right):
    return lax.dot_general(left, right, (((1,), (1,)), ((), ())), preferred_element_type=F32)


def plus(a, b):
    return a + b


def send(x, pairs):
    return lax.ppermute(x, AXES, pairs)


def unit_of_work(go, body, *args):
    def idle(*args):
        return jax.tree.map(lambda leaf: jnp.zeros(leaf.shape, leaf.dtype), jax.eval_shape(body, *args))

    return lax.cond(go, body, idle, *args)


def fence(*items):
    return lax.optimization_barrier(items)


class Layout:
    def __init__(self):
        self.ctx = lax.axis_size("ctx")
        self.fsdp = lax.axis_size("fsdp")
        self.tpf = KV // self.ctx
        self.nz = self.fsdp // self.tpf
        self.total = self.fsdp * self.ctx
        self.fast = self.ctx == 4 and self.tpf == 2 and self.nz == 4
        self.f = lax.axis_index("fsdp")
        self.c = lax.axis_index("ctx")
        self.z = self.f // self.tpf
        self.place = [(b, (b % self.nz) * KV + b // self.nz) for b in range(self.total)]
        self.back = [(d, s) for s, d in self.place]

    def exchange(self, x):
        if self.tpf == 1:
            return lax.all_to_all(x, "ctx", split_axis=0, concat_axis=0, tiled=True)
        groups = [[z * KV + i for i in range(KV)] for z in range(self.nz)]
        return lax.all_to_all(
            x, AXES, split_axis=0, concat_axis=0, tiled=True, axis_index_groups=groups
        )

    def lines(self):
        return [[z * KV + i for z in range(self.nz)] for i in range(KV)]

    def spread(self, x):
        if self.tpf == 1:
            return lax.all_gather(x, "fsdp", axis=0, tiled=True)
        return lax.all_gather(x, AXES, axis=0, tiled=True, axis_index_groups=self.lines())

    def gather_sum(self, x):
        x = x.astype(BF)
        if self.tpf == 1:
            return lax.psum_scatter(x, "fsdp", scatter_dimension=0, tiled=True)
        return lax.psum_scatter(
            x, AXES, scatter_dimension=0, tiled=True, axis_index_groups=self.lines()
        )


class Line(Layout):
    def __init__(self):
        super().__init__()
        total = self.total
        self.core = [(d, d ^ 1) for d in range(total)]
        self.first = [(d, d ^ (2 if d & 1 else 4)) for d in range(total)]
        self.second = [(d, d ^ (4 if d & 1 else 2)) for d in range(total)]
        self.xflip = [(d, d ^ 4) for d in range(total)]

        def planes(pairs):
            return [(s * KV + i, d * KV + i) for s, d in pairs for i in range(KV)]

        self.pair = planes([(0, 1), (1, 0), (2, 3), (3, 2)])
        self.inner = planes([(1, 2), (2, 1)])
        self.outward = planes([(1, 0), (2, 3)])
        self.inward = planes([(0, 1), (3, 2)])
        z = self.z
        low = z < 2
        self.order = [z, z ^ 1, jnp.where(low, 2, 1), jnp.where(low, 3, 0)]
        table = ((0, 1, 3, 3), (1, 0, 2, 2), (2, 2, 0, 1), (3, 3, 1, 0))
        self.slot = [
            jnp.where(z == 0, r[0], jnp.where(z == 1, r[1], jnp.where(z == 2, r[2], r[3])))
            for r in table
        ]

    def take_columns(self, x, blocks):
        width = x.shape[-1] // self.nz
        return jnp.concatenate(
            [lax.dynamic_slice_in_dim(x, k * width, width, axis=-1) for k in blocks], axis=-1
        )

    def take_rows(self, pieces):
        full = jnp.stack(pieces)
        return jnp.concatenate(
            [lax.dynamic_index_in_dim(full, k, axis=0, keepdims=False) for k in self.slot], axis=0
        )

    def to_pieces(self, x):
        full = x.reshape((self.nz, x.shape[0] // self.nz) + x.shape[1:])
        return [lax.dynamic_index_in_dim(full, k, axis=0, keepdims=False) for k in self.order]

    def all_tokens(self, x):
        x = jnp.stack([x, send(x, self.first)])
        x = jnp.stack([x, send(x, self.second)])
        x = jnp.stack([x, send(x, self.core)])
        return x.reshape(-1, x.shape[-1])

    def plane_tokens(self, x):
        x = jnp.stack([x, send(x, self.first)])
        x = jnp.stack([x, send(x, self.second)])
        other = send(x, self.core)
        return x.reshape(-1, x.shape[-1]), other.reshape(-1, x.shape[-1])

    def collect_tokens(self, x, slots):
        x = x.reshape(2, 2, 2, 2, slots, x.shape[-1])
        x = plus(x[0], send(x[1], self.core))
        x = plus(x[0], send(x[1], self.second))
        return x[0].astype(F32) + send(x[1], self.first).astype(F32)

    def to_seqs(self, x, slots):
        x = x.reshape(2, 2, 2, 2, slots, x.shape[-1])
        halves = []
        for dc in range(2):
            even = ((self.c & 1) ^ dc) == 0
            h = x[dc]
            halves.append(jnp.where(even, jnp.swapaxes(h, 0, 1), h))
        x = jnp.stack(halves, axis=0)
        x = jnp.transpose(x, (1, 3, 0, 2, 4, 5))
        return x.reshape(4, 4 * slots, x.shape[-1])

    def from_seqs(self, x, slots):
        x = x.reshape(2, 2, 2, 2, slots, x.shape[-1])
        x = jnp.transpose(x, (2, 0, 3, 1, 4, 5))
        halves = []
        for dc in range(2):
            even = ((self.c & 1) ^ dc) == 0
            h = x[dc]
            halves.append(jnp.where(even, jnp.swapaxes(h, 0, 1), h))
        return jnp.stack(halves, axis=0).reshape(16 * slots, x.shape[-1])


def positions_of(span_order, index, slots):
    span_len = slots // 2
    at = jnp.arange(slots, dtype=jnp.int32)
    pair = lax.dynamic_slice_in_dim(span_order, 2 * index, 2)
    return jnp.where(at < span_len, pair[0], pair[1]) * span_len + at % span_len


def rope_tables(pos):
    frequency = rope_base ** (-2.0 * jnp.arange(HD // 2, dtype=F32) / HD)
    angles = pos.astype(F32)[:, None] * frequency[None, :]
    return jnp.cos(angles), jnp.sin(angles)


def rotate(v, cosines, sines):
    half = HD // 2
    co, si = cosines[None, :, None, :], sines[None, :, None, :]
    one, two = v[..., :half], v[..., half:]
    return jnp.concatenate([one * co - two * si, two * co + one * si], axis=-1)


def unit_rows(x):
    inverse = lax.rsqrt(jnp.mean(x * x, axis=-1, keepdims=True) + epsilon)
    return x * inverse, inverse


def unit_back(scaled, unit, inverse):
    return inverse * (scaled - unit * jnp.mean(scaled * unit, axis=-1, keepdims=True))


def attend(pre, pos, seq_len, cosines, sines):
    seqs, length, _ = pre.shape
    q = rotate(pre[..., :QW].reshape(seqs, length, GROUP, HD), cosines, sines).astype(BF)
    k = rotate(pre[..., QW : QW + HD].reshape(seqs, length, 1, HD), cosines, sines)[:, :, 0].astype(BF)
    v = pre[..., QW + HD :].astype(BF)
    allowed = (pos[None, None, :] <= pos[None, :, None]) & (
        pos[None, None, :] < seq_len[:, None, None]
    )
    scores = jnp.einsum("sqgd,snd->sgqn", q, k, preferred_element_type=F32) * scale
    scores = jnp.where(allowed[:, None], scores, masked_score)
    top = jnp.max(scores, axis=-1, keepdims=True)
    expo = jnp.exp(scores - top)
    probs = expo / jnp.sum(expo, axis=-1, keepdims=True)
    low = probs.astype(BF)
    attended = jnp.einsum("sgqn,snd->sqgd", low, v, preferred_element_type=F32)
    return attended.astype(BF).reshape(seqs, length, QW), (q, k, v, probs, low)


def attend_back(g_att, kept, cosines, sines):
    q, k, v, probs, low = kept
    seqs, length, _ = g_att.shape
    g_att = g_att.reshape(seqs, length, GROUP, HD)
    g_probs = jnp.einsum("sqgd,snd->sgqn", g_att, v, preferred_element_type=F32)
    inner = jnp.sum(probs * g_probs, axis=-1, keepdims=True)
    g_scores = (probs * (g_probs - inner)).astype(BF)
    g_q = jnp.einsum("sgqn,snd->sqgd", g_scores, k, preferred_element_type=F32) * scale
    g_k = jnp.einsum("sgqn,sqgd->snd", g_scores, q, preferred_element_type=F32) * scale
    g_v = jnp.einsum("sgqn,sqgd->snd", low, g_att, preferred_element_type=F32)
    return jnp.concatenate(
        [
            rotate(g_q, cosines, -sines).astype(BF).reshape(seqs, length, QW),
            rotate(g_k[:, :, None], cosines, -sines).astype(BF)[:, :, 0],
            g_v.astype(BF),
        ],
        axis=-1,
    )


def swiglu(gate_up):
    half = gate_up.shape[-1] // 2
    gate, up = gate_up[:, :half], gate_up[:, half:]
    return (jax.nn.silu(gate) * up).astype(BF)


def swiglu_back(gate_up, g_hidden):
    half = gate_up.shape[-1] // 2
    gate, up = gate_up[:, :half], gate_up[:, half:]
    sig = jax.nn.sigmoid(gate)
    g_gate = (g_hidden * up * sig * (1.0 + gate * (1.0 - sig))).astype(BF)
    g_up = (g_hidden * gate * sig).astype(BF)
    return jnp.concatenate([g_gate, g_up], axis=-1)


def pack_attention(w_query, w_key, w_value, gain):
    rows = w_query.shape[0]
    parts = [
        (w.astype(F32) * gain).astype(BF).reshape(rows, KV, w.shape[1] // KV)
        for w in (w_query, w_key, w_value)
    ]
    return jnp.transpose(jnp.concatenate(parts, axis=2), (1, 0, 2))


def unpack_attention(u):
    u = jnp.transpose(u, (1, 0, 2)).astype(F32)
    rows = u.shape[0]
    return (
        u[..., :QW].reshape(rows, KV * QW),
        u[..., QW : QW + HD].reshape(rows, KV * HD),
        u[..., QW + HD :].reshape(rows, KV * HD),
    )


def pack_mlp(w_gate, w_up, gain, nz):
    rows = w_gate.shape[0]

    def columns(w):
        w = (w.astype(F32) * gain).astype(BF).reshape(rows, nz, KV, -1)
        return jnp.transpose(w, (2, 0, 1, 3)).reshape(KV, rows, -1)

    return jnp.concatenate([columns(w_gate), columns(w_up)], axis=2)


def unpack_mlp(u, nz):
    rows = u.shape[1]
    u = u.reshape(KV, rows, 2, nz, -1)
    u = jnp.transpose(u, (2, 1, 3, 0, 4)).reshape(2, rows, -1).astype(F32)
    return u[0], u[1]


SMEM = pl.BlockSpec(memory_space=pltpu.SMEM)
VMEM = pl.BlockSpec(memory_space=pltpu.VMEM)
WIDE = QW + 2 * HD
FREE = pl.CostEstimate(flops=0, bytes_accessed=0, transcendentals=0)
ROOM = pltpu.CompilerParams(vmem_limit_bytes=56 * 1024 * 1024)


def shaped(*shape, dtype=BF):
    return jax.ShapeDtypeStruct(shape, dtype)


def kernel_call(body, outs, scratch=()):
    def call(scalars, *arrays):
        return pl.pallas_call(
            body,
            out_shape=outs,
            in_specs=[SMEM] * len(scalars) + [VMEM] * len(arrays),
            out_specs=jax.tree.map(lambda _: VMEM, outs),
            scratch_shapes=list(scratch),
            compiler_params=ROOM,
            cost_estimate=FREE,
        )(*scalars, *arrays)

    return call


def moving_call(body, outs, scratch=(), copies=1):
    def call(scalars, *arrays):
        anywhere_spec = pl.BlockSpec(memory_space=pl.ANY)
        return pl.pallas_call(
            body,
            out_shape=outs,
            in_specs=[SMEM] * len(scalars) + [pl.BlockSpec(memory_space=pltpu.HBM)] * len(arrays),
            out_specs=jax.tree.map(lambda _: anywhere_spec, outs),
            scratch_shapes=list(scratch) + [pltpu.SemaphoreType.DMA((copies,))],
            compiler_params=ROOM,
            cost_estimate=FREE,
        )(*scalars, *arrays)

    return call


class Copies:
    def __init__(self, sems):
        self.sems = sems
        self.used = 0

    def start(self, source, target):
        copy = pltpu.make_async_copy(source, target, self.sems.at[self.used])
        self.used += 1
        copy.start()
        return copy


def vmem(*arrays):
    return [pltpu.VMEM(a.shape, a.dtype) for a in arrays]


def dot(a, b, dims=((1,), (0,))):
    return lax.dot_general(a, b, (dims, ((), ())), preferred_element_type=F32)


LEFT_T = ((0,), (0,))
RIGHT_T = ((1,), (1,))


def block_rows(core, seq, dc, dy, slots):
    dx, m = seq // 2, seq % 2
    even = (core ^ dc) == 0
    s1 = jnp.where(even, dx, dy)
    s2 = jnp.where(even, dy, dx)
    return pl.multiple_of(((s2 * 2 + s1) * 2 + m) * slots, slots)


def blocks_of(slots):
    for dc in range(2):
        for dy in range(2):
            b = dc * 2 + dy
            yield dc, dy, slice(b * slots, (b + 1) * slots)


def spans_of(spans, ctx):
    out = []
    for dc in range(2):
        for dy in range(2):
            other = ctx ^ (dy * 2 + dc)
            out += [spans[2 * other], spans[2 * other + 1]]
    return out


def along(held, length, axis, shape):
    at = lax.broadcasted_iota(jnp.int32, shape, axis) % length
    step = length // len(held)
    pos = at % step
    for i, span in enumerate(held):
        pos = pos + jnp.where(at // step == i, span * step, 0)
    return pos


def rotary_rows(held, table, out):
    step = out.shape[0] // len(held)
    for i, span in enumerate(held):
        out[i * step : (i + 1) * step, :] = table[pl.ds(pl.multiple_of(span * step, step), step), :]


def rotary_copies(copies, held, table, out):
    step = out.shape[0] // len(held)
    return [
        copies.start(table.at[pl.ds(pl.multiple_of(span * step, step), step)], out.at[pl.ds(i * step, step)])
        for i, span in enumerate(held)
    ]


def turn(x, cosines, sines):
    half, width = HD // 2, x.shape[1]
    lane = lax.broadcasted_iota(jnp.int32, x.shape, 1) % HD
    partner = jnp.where(lane < half, pltpu.roll(x, width - half, 1), pltpu.roll(x, half, 1))
    return x * cosines + partner * sines


def probabilities(q, k, allowed):
    scores = jnp.where(allowed, dot(q, k, RIGHT_T) * scale, masked_score)
    expo = jnp.exp(scores - jnp.max(scores, axis=-1, keepdims=True))
    return expo / jnp.sum(expo, axis=-1, keepdims=True)


def heads_of(x):
    return [x[:, h * HD : (h + 1) * HD] for h in range(x.shape[1] // HD)]


def assemble(meta, pieces, out):
    p0, p1, p2, p3, p4, p5 = pieces
    step = p0.shape[0]
    for s, parts in enumerate(((p0,), (p1,), (p2, p3), (p4, p5))):
        piece = parts[0][...]
        if len(parts) > 1:
            piece = piece + parts[1][...]
        out[pl.ds(pl.multiple_of(meta[s] * step, step), step), :] = piece


def fetch_qkv(full, out):
    step = full.shape[2]
    for z in range(full.shape[0]):
        out[z * step : (z + 1) * step, :] = full[z, :step, :]


def fetch_out(full, out):
    nz, total, step = full.shape
    count = out.shape[1] // step
    rows = (total - step) // count
    for z in range(nz):
        for k in range(count):
            out[z * rows : (z + 1) * rows, k * step : (k + 1) * step] = full[
                z, step + k * rows : step + (k + 1) * rows, :
            ]


def stacked_columns(x, cut):
    return jnp.concatenate([x[:, k : k + cut] for k in range(0, x.shape[1], cut)], axis=0)


def column(row):
    n = row.shape[1]
    same = lax.broadcasted_iota(jnp.int32, (n, n), 0) == lax.broadcasted_iota(jnp.int32, (n, n), 1)
    return jnp.sum(jnp.where(same, row, 0.0), axis=1, keepdims=True)


def row_of(col):
    n = col.shape[0]
    same = lax.broadcasted_iota(jnp.int32, (n, n), 0) == lax.broadcasted_iota(jnp.int32, (n, n), 1)
    return jnp.sum(jnp.where(same, col, 0.0), axis=0, keepdims=True)


def pack_attention_kernel(wq, wk, wv, gain, out):
    g = column(gain[...].astype(F32))
    q, k, v = ((w[...].astype(F32) * g).astype(BF) for w in (wq, wk, wv))
    for j in range(KV):
        out[j] = jnp.concatenate(
            [q[:, j * QW : (j + 1) * QW], k[:, j * HD : (j + 1) * HD], v[:, j * HD : (j + 1) * HD]], axis=1
        )


def pack_mlp_kernel(wg, wu, gain, out):
    g = column(gain[...].astype(F32))
    half = out.shape[2] // 2
    blocks = 4
    hid = half // blocks
    for h, w in enumerate((wg, wu)):
        x = (w[...].astype(F32) * g).astype(BF)
        for z in range(blocks):
            for j in range(KV):
                out[j, :, h * half + z * hid : h * half + (z + 1) * hid] = x[
                    :, (z * KV + j) * hid : (z * KV + j + 1) * hid
                ]


def unpack_attention_kernel(u, wq, wk, wv, gain, gq, gk, gv, total):
    g = column(gain[...].astype(F32))
    acc = jnp.zeros(g.shape, F32)
    for w, out, lo, n in ((wq, gq, 0, QW), (wk, gk, QW, HD), (wv, gv, QW + HD, HD)):
        part = jnp.concatenate([u[j, :, lo : lo + n] for j in range(KV)], axis=1).astype(F32)
        out[...] = part * g
        acc += jnp.sum(part * w[...].astype(F32), axis=1, keepdims=True)
    total[...] = row_of(acc)


def unpack_mlp_kernel(u, wg, wu, gain, gg, gu, total):
    g = column(gain[...].astype(F32))
    acc = jnp.zeros(g.shape, F32)
    half = wg.shape[1] // KV
    blocks = 4
    hid = half // blocks
    for j in range(KV):
        x = u[j].astype(F32)
        for h, (w, out) in enumerate(((wg, gg), (wu, gu))):
            for z in range(blocks):
                at = slice((z * KV + j) * hid, (z * KV + j + 1) * hid)
                part = x[:, h * half + z * hid : h * half + (z + 1) * hid]
                out[:, at] = part * g
                acc += jnp.sum(part * w[:, at].astype(F32), axis=1, keepdims=True)
    total[...] = row_of(acc)


def usable_rows(lens, spans, ctx, shape):
    at = lax.broadcasted_iota(jnp.int32, shape, 0)
    slots = shape[0] // 2
    slot, step = at % slots, slots // 2
    pos = jnp.where(slot < step, spans[2 * ctx], spans[2 * ctx + 1]) * step + slot % step
    length = jnp.where(at < slots, lens[0], lens[1])
    return (pos < length).astype(F32)


def prepare_kernel(meta, lens, spans, x, g, xhat, inverse, g_low):
    v = x[...].astype(F32)
    inv = lax.rsqrt(jnp.mean(v * v, axis=-1, keepdims=True) + epsilon)
    inverse[...] = inv
    xhat[...] = (v * inv).astype(BF)
    g_low[...] = (g[...].astype(F32) * usable_rows(lens, spans, meta[5], inverse.shape)).astype(BF)


def finish_kernel(meta, lens, spans, residual, a, b, out):
    total = residual[...] + a[...].astype(F32) + b[...].astype(F32)
    out[...] = (total * usable_rows(lens, spans, meta[5], (total.shape[0], 1))).astype(BF)


def attention_kernel(
    meta, lens, spans, xa, xb, full, cos_table, sin_table, wqkv, qkv, att, xseq, cosines, sines
):
    core, ctx = meta[4], meta[5]
    slots = xa.shape[0] // 8
    length = xseq.shape[0]
    fetch_qkv(full, wqkv)
    held = spans_of(spans, ctx)
    rotary_rows(held, cos_table, cosines)
    rotary_rows(held, sin_table, sines)
    posc = along(held, length, 0, (GROUP * length, length))
    posr = along(held, length, 1, (GROUP * length, length))
    causal = posr <= posc

    def one(seq, carry):
        for dc, dy, rows in blocks_of(slots):
            xseq[rows, :] = (xa, xb)[dc][pl.ds(block_rows(core, seq, dc, dy, slots), slots), :]
        low = turn(dot(xseq[...], wqkv[...]), cosines[...], sines[...]).astype(BF)
        qkv[seq] = low
        one_q, two_q, k, v = heads_of(low)
        q = jnp.concatenate([one_q, two_q], axis=0)
        allowed = causal & (posr < lens[seq])
        mixed = dot(probabilities(q, k, allowed).astype(BF), v)
        out = jnp.concatenate([mixed[:length], mixed[length:]], axis=1).astype(BF)
        for dc, dy, rows in blocks_of(slots):
            att[dc, pl.ds(block_rows(core, seq, dc, dy, slots), slots), :] = out[rows]
        return carry

    lax.fori_loop(0, 4, one, 0, unroll=True)


def project_kernel(att, full, wout, mine, theirs):
    fetch_out(full, wout)
    theirs[...] = dot(att[1], wout[...]).astype(BF)
    mine[...] = dot(att[0], wout[...]).astype(BF)


def attention_back_kernel(
    meta, lens, spans,
    h_ga, h_gb, h_att, h_wout, h_wqkv, h_qkv, h_xa, h_xb, cos_table, sin_table,
    o_mine, o_theirs, o0, o1, o2, o3,
    ga, gb, att, wout, wqkv, qkv, xa, xb, mine, theirs, u0, u1, u2, u3, g_pre, gseq, cosines, sines, out_grad, sems,
):
    copies = Copies(sems)
    held = spans_of(spans, meta[5])
    first = [copies.start(h, v) for h, v in ((h_wout, wout), (h_qkv, qkv), (h_ga, ga), (h_gb, gb))]
    first += rotary_copies(copies, held, cos_table, cosines) + rotary_copies(copies, held, sin_table, sines)
    for c in first:
        c.wait()
    later = [copies.start(h, v) for h, v in ((h_xa, xa), (h_xb, xb), (h_att, att), (h_wqkv, wqkv))]
    core, ctx = meta[4], meta[5]
    slots = ga.shape[0] // 8
    length = gseq.shape[0]
    posc = along(held, length, 0, (GROUP * length, length))
    posr = along(held, length, 1, (GROUP * length, length))
    causal = posr <= posc

    def one(seq, carry):
        for dc, dy, rows in blocks_of(slots):
            gseq[rows, :] = (ga, gb)[dc][pl.ds(block_rows(core, seq, dc, dy, slots), slots), :]
        g_att = dot(gseq[...], wout[...], RIGHT_T).astype(BF)
        one_q, two_q, k, v = heads_of(qkv[seq])
        q = jnp.concatenate([one_q, two_q], axis=0)
        g = jnp.concatenate(heads_of(g_att), axis=0)
        allowed = causal & (posr < lens[seq])
        p = probabilities(q, k, allowed)
        g_p = dot(g, v, RIGHT_T)
        g_s = (p * (g_p - jnp.sum(p * g_p, axis=-1, keepdims=True))).astype(BF)
        g_q = dot(g_s, k) * scale
        g_k = dot(g_s, q, LEFT_T) * scale
        g_v = dot(p.astype(BF), g, LEFT_T)
        full = jnp.concatenate([g_q[:length], g_q[length:], g_k, g_v], axis=1)
        out = turn(full, cosines[...], -sines[...]).astype(BF)
        for dc, dy, rows in blocks_of(slots):
            g_pre[dc, pl.ds(block_rows(core, seq, dc, dy, slots), slots), :] = out[rows]
        return carry

    lax.fori_loop(0, 4, one, 0, unroll=True)
    for c in later:
        c.wait()
    gone = []
    out_grad[...] = (dot(att[0], ga[...], LEFT_T) + dot(att[1], gb[...], LEFT_T)).astype(BF)
    step = xa.shape[1] // 4
    block = u0.shape[1]
    count = out_grad.shape[1] // block
    low = out_grad.shape[0] // 4
    for s, u, o in ((3, u3, o3), (2, u2, o2), (1, u1, o1), (0, u0, o0)):
        at = pl.ds(pl.multiple_of(meta[s] * step, step), step)
        u[:step, :] = (dot(xa[:, at], g_pre[0], LEFT_T) + dot(xb[:, at], g_pre[1], LEFT_T)).astype(BF)
        at = pl.ds(pl.multiple_of(meta[s] * low, low), low)
        for k in range(count):
            u[step + k * low : step + (k + 1) * low, :] = out_grad[at, k * block : (k + 1) * block]
        gone.append(copies.start(u, o))
    theirs[...] = dot(g_pre[1], wqkv[...], RIGHT_T).astype(BF)
    gone.append(copies.start(theirs, o_theirs))
    mine[...] = dot(g_pre[0], wqkv[...], RIGHT_T).astype(BF)
    gone.append(copies.start(mine, o_mine))
    for c in gone:
        c.wait()


def mlp_kernel(
    meta,
    h_ma, h_mb, h_ea, h_eb, h_wgu, h0, h1, h2, h3, h4, h5,
    o_down_mine, o_down_theirs, o_mine, o_theirs, o_u,
    x, g, back, down, wgu, d0, d1, d2, d3, d4, d5, u, hidden, g_gu, wdown, sems,
):
    copies = Copies(sems)
    came = [copies.start(h_wgu, wgu), copies.start(h_mb, x.at[1])]
    pieces = (d0, d1, d2, d3, d4, d5)
    came += [copies.start(h, d) for h, d in zip((h0, h1, h2, h3, h4, h5), pieces)]
    came += [copies.start(h_eb, g.at[1])]
    later = [copies.start(h_ma, x.at[0]), copies.start(h_ea, g.at[0])]
    half = wgu.shape[1] // 2
    for c in came:
        c.wait()
    assemble(meta, pieces, wdown)
    out_copies = [
        pltpu.make_async_copy(v, o, sems.at[copies.used + k])
        for k, (v, o) in enumerate(
            ((back.at[1], o_theirs), (down.at[1], o_down_theirs), (back.at[0], o_mine), (down.at[0], o_down_mine))
        )
    ]
    copies.used += 4

    def one(i, carry):
        part = 1 - i

        @pl.when(i == 1)
        def _():
            for c in later:
                c.wait()

        gate_up = dot(x[part], wgu[...])
        gate, up = gate_up[:, :half], gate_up[:, half:]
        sig = 1.0 / (1.0 + jnp.exp(-gate))
        act = gate * sig
        hidden[part] = (act * up).astype(BF)
        g_hidden = dot(g[part], wdown[...], RIGHT_T)
        g_gu[part, :, :half] = (g_hidden * up * sig * (1.0 + gate * (1.0 - sig))).astype(BF)
        g_gu[part, :, half:] = (g_hidden * act).astype(BF)
        back[part] = dot(g_gu[part], wgu[...], RIGHT_T).astype(BF)
        down[part] = dot(hidden[part], wdown[...]).astype(BF)

        @pl.when(i == 0)
        def _():
            out_copies[0].start()
            out_copies[1].start()

        @pl.when(i == 1)
        def _():
            out_copies[2].start()
            out_copies[3].start()

        return carry

    lax.fori_loop(0, 2, one, 0)
    nz, _, wide = u.shape
    piece = x.shape[2] // nz
    step = hidden.shape[2] // nz
    base = copies.used

    def grads(z, carry):
        at = pl.ds(pl.multiple_of(z * piece, piece), piece)
        both = dot(x[0, :, at], g_gu[0], LEFT_T) + dot(x[1, :, at], g_gu[1], LEFT_T)
        u[z, :piece, :] = both.astype(BF)
        at = pl.ds(pl.multiple_of(z * step, step), step)
        both = (dot(hidden[0, :, at], g[0], LEFT_T) + dot(hidden[1, :, at], g[1], LEFT_T)).astype(BF)
        u[z, piece : piece + step, :] = both[:, :wide]
        rest = both.shape[1] - wide
        u[z, piece + step :, :rest] = both[: step // 2, wide:]
        u[z, piece + step :, rest:] = both[step // 2 :, wide:]
        pltpu.make_async_copy(u.at[z], o_u.at[z], sems.at[base + z]).start()
        return carry

    lax.fori_loop(0, nz, grads, 0)
    for c in out_copies:
        c.wait()
    for z in range(nz):
        pltpu.make_async_copy(u.at[z], o_u.at[z], sems.at[base + z]).wait()


def unpack_down_kernel(u, out):
    step, wide = out.shape[0], u.shape[1]
    rest = out.shape[1] - wide
    out[:, :wide] = u[:step, :].astype(F32)
    out[: step // 2, wide:] = u[step:, :rest].astype(F32)
    out[step // 2 :, wide:] = u[step:, rest:].astype(F32)


def sums_kernel(a, b, c, d, ab, cd):
    ab[...] = a[...] + b[...]
    cd[...] = c[...] + d[...]


def last_sum_kernel(a, b, c, qkv, out):
    total = (a[...].astype(F32) + b[...].astype(F32) + c[...].astype(F32)).astype(BF)
    blocks, rows, width = qkv.shape
    for j in range(blocks):
        qkv[j] = total[j * rows : (j + 1) * rows]
    low = out.shape[0]
    for k in range(out.shape[1] // width):
        at = blocks * rows + k * low
        out[:, k * width : (k + 1) * width] = total[at : at + low]


def norm_kernel(source, a, b, residual, xhat, inverse):
    r = source[...].astype(F32) + a[...].astype(F32) + b[...].astype(F32)
    inv = lax.rsqrt(jnp.mean(r * r, axis=-1, keepdims=True) + epsilon)
    residual[...] = r
    inverse[...] = inv
    xhat[...] = (r * inv).astype(BF)


def norm_back(g_res, source, inverse, a, b):
    scaled = a[...].astype(F32) + b[...].astype(F32)
    inv = inverse[...]
    unit = source[...].astype(F32) * inv
    back = inv * (scaled - unit * jnp.mean(scaled * unit, axis=-1, keepdims=True))
    return g_res[...].astype(F32) + back


def norm_back_kernel(g_res, source, inverse, a, b, out, low):
    g = norm_back(g_res, source, inverse, a, b)
    out[...] = g
    low[...] = g.astype(BF)


def norm_back_low_kernel(g_res, source, inverse, a, b, low):
    low[...] = norm_back(g_res, source, inverse, a, b).astype(BF)


def rotary_constants(total):
    frequency = rope_base ** (-2.0 * np.arange(HD // 2, dtype=np.float32) / HD).astype(np.float32)
    angles = np.arange(total, dtype=np.float32)[:, None] * frequency[None, :].astype(np.float32)
    c, s = np.cos(angles), np.sin(angles)
    flat, signed = np.concatenate([c, c], 1), np.concatenate([-s, s], 1)
    cosines = np.concatenate([flat] * (GROUP + 1) + [np.ones_like(flat)], 1)
    sines = np.concatenate([signed] * (GROUP + 1) + [np.zeros_like(flat)], 1)
    return jnp.asarray(cosines, F32), jnp.asarray(sines, F32)


def paired(*items):
    return sum(jnp.sum(w.astype(F32) * g, axis=1) for w, g in items)


def on_line(
    hidden_in, lengths, span_order, attn_gain, w_query, w_key, w_value, w_out,
    mlp_gain, w_gate, w_up, w_down, out_grad,
):
    lay = Line()
    _, slots, width = hidden_in.shape
    rows, nz = w_query.shape[0], lay.nz
    tokens, length, own = 16 * slots, 4 * slots, 2 * slots
    go = lengths[0] > 0
    meta = jnp.stack([k.astype(jnp.int32) for k in (*lay.order, lay.c & 1, lay.c)])
    gain, gain_m = attn_gain[None, :], mlp_gain[None, :]
    cos_table, sin_table = rotary_constants(length)

    def halves(x):
        return x.reshape(2, x.shape[0] // 2, width)

    wide = w_gate.shape[1] * 2 // KV
    cut = wide // 2
    tables = [pltpu.VMEM((length, WIDE), F32)] * 2

    def flat(x):
        return x.reshape(-1, width)

    d1 = send(w_down, lay.pair)
    d2 = send(w_down, lay.inner)
    q0 = lay.exchange(
        kernel_call(pack_attention_kernel, shaped(KV, rows, WIDE))((), w_query, w_key, w_value, gain)
    )
    theirs = send(lengths, lay.xflip)
    o0 = send(w_out, lay.place)
    gu_s = kernel_call(pack_mlp_kernel, shaped(KV, rows, wide))((), w_gate, w_up, gain_m)
    xhat, inverse, g_low = kernel_call(
        prepare_kernel, (shaped(own, width), shaped(own, 1, dtype=F32), shaped(own, width))
    )((meta, lengths, span_order), hidden_in.reshape(own, width), out_grad.reshape(own, width))
    q0, d1, d2, theirs, gu_s, xhat, g_low = fence(q0, d1, d2, theirs, gu_s, xhat, g_low)
    d3 = send(d2, lay.outward)
    d4 = send(d1, lay.inner)
    x1 = send(xhat, lay.first)
    attn_piece = jnp.concatenate([q0.reshape(KV * rows, WIDE), stacked_columns(o0, WIDE)], axis=0)
    d3, d4, x1, attn_piece = fence(d3, d4, x1, attn_piece)
    attn_full = lay.spread(attn_piece)

    def gather(xhat, x1, g_low, gu_s):
        gu0 = lay.exchange(gu_s)
        x01 = jnp.stack([xhat, x1])
        x2 = send(x01, lay.second)
        x2, gu0, x01, g_low = fence(x2, gu0, x01, g_low)
        x0123 = jnp.stack([x01, x2])
        x3 = send(x0123, lay.core)
        e1 = send(g_low, lay.first)
        x3, x0123, e1 = fence(x3, x0123, e1)
        e01 = jnp.stack([g_low, e1])
        return x0123, x3, gu0, e01

    xa, xb, gu0, e01 = unit_of_work(go, gather, xhat, x1, g_low, gu_s)
    attn_full, gu0 = fence(attn_full, gu0)
    wgu = lay.spread(gu0.reshape(KV * rows, wide))
    d5 = send(d4, lay.outward)
    attn_full = attn_full.reshape(nz, -1, WIDE)
    seq_len = jnp.concatenate([lengths, theirs])

    def forward(meta, seq_len, span_order, xa, xb, attn_full, cos_table, sin_table, hidden_in, e01):
        e2 = send(e01, lay.second)
        wqkv, qkv, att = kernel_call(
            attention_kernel,
            (shaped(width, WIDE), shaped(4, length, WIDE), shaped(2, tokens // 2, QW)),
            scratch=[pltpu.VMEM((length, width), BF)] + tables,
        )((meta, seq_len, span_order), flat(xa), flat(xb), attn_full, cos_table, sin_table)
        wout, mine, other = kernel_call(
            project_kernel, (shaped(QW, width), shaped(tokens // 2, width), shaped(tokens // 2, width))
        )((), att, attn_full)
        wqkv, qkv, att, wout, mine, other, e2 = fence(wqkv, qkv, att, wout, mine, other, e2)
        got = send(other, lay.core)
        r = halves(plus(mine, got))
        e0123 = jnp.stack([e01, e2])
        r, e0123 = fence(r, e0123)
        got = send(r[1], lay.second)
        e3 = send(e0123, lay.core)
        got, e3, r = fence(got, e3, r)
        r = halves(plus(r[0], got))
        got = send(r[1], lay.first)
        residual, xm0, inverse_m = kernel_call(
            norm_kernel, (shaped(own, width, dtype=F32), shaped(own, width), shaped(own, 1, dtype=F32))
        )((), hidden_in.reshape(own, width), r[0], got)
        m01 = jnp.stack([xm0, send(xm0, lay.first)])
        m2 = send(m01, lay.second)
        ma = jnp.stack([m01, m2])
        mb = send(ma, lay.core)
        return wqkv, qkv, att, wout, residual, inverse_m, flat(ma), flat(mb), flat(e0123), flat(e3)

    wqkv, qkv, att, wout, residual, inverse_m, ma, mb, ea, eb = unit_of_work(
        go, forward, meta, seq_len, span_order, xa, xb, attn_full, cos_table, sin_table, hidden_in, e01
    )
    half_rows = shaped(tokens // 2, width)
    low = w_down.shape[0]
    piece = KV * rows + low * width // wide
    outs = (half_rows, half_rows, half_rows, half_rows, shaped(nz, piece, wide))
    ins = (ma, mb, ea, eb, wgu, w_down, d1, d2, d3, d4, d5)
    down_mine, down_other, mine, other, u_mlp = moving_call(
        mlp_kernel,
        outs,
        scratch=[pltpu.VMEM((2, tokens // 2, width), BF)] * 4
        + vmem(*ins[4:], outs[4])
        + [pltpu.VMEM((2, tokens // 2, cut), BF), pltpu.VMEM((2, tokens // 2, wide), BF), pltpu.VMEM((cut, width), BF)],
        copies=len(ins) + 4 + nz,
    )((meta,), *ins)
    v_mlp = lay.gather_sum(u_mlp.reshape(nz * piece, wide))
    both = KV * rows + QW // nz * width // WIDE

    def backward(
        meta, seq_len, lengths, span_order, mine, other, down_mine, down_other, g_low, residual, inverse_m, att, wqkv, wout, qkv,
        xa, xb, cos_table, sin_table,
    ):
        got = send(other, lay.core)
        got, mine = fence(got, mine.astype(F32))
        r = halves((mine + got.astype(F32)).astype(BF))
        r = halves(plus(r[0], send(r[1], lay.second)))
        got = send(r[1], lay.first)
        got_down = send(down_other, lay.core)
        g_res2, h0 = kernel_call(
            norm_back_kernel, (shaped(own, width, dtype=F32), shaped(own, width))
        )((), g_low, residual, inverse_m, r[0], got)
        ga, gb = lay.plane_tokens(h0)
        d = halves(plus(down_mine, got_down))
        ga, gb, d = fence(ga, gb, d)
        got_down = send(d[1], lay.second)
        outs = [half_rows, half_rows] + [shaped(both, WIDE)] * nz
        ins = (ga, gb, att, wout, wqkv, qkv, flat(xa), flat(xb))
        mine, other, u0, u1, u2, u3 = moving_call(
            attention_back_kernel,
            outs,
            scratch=vmem(*ins, *outs)
            + [pltpu.VMEM((2, tokens // 2, WIDE), BF), pltpu.VMEM((length, width), BF)]
            + tables
            + [pltpu.VMEM((QW, width), BF)],
            copies=len(ins) + len(outs) + 16,
        )((meta, seq_len, span_order), *ins, cos_table, sin_table)
        got_down, mine, other, u0, u1, u2, u3 = fence(got_down, mine, other, u0, u1, u2, u3)
        d = halves(plus(d[0], got_down))
        return g_res2, mine, other, d[0], d[1], u3, u2, u1, u0

    g_res2, mine, other, da, db, u3, u2, u1, u0 = unit_of_work(
        go, backward, meta, seq_len, lengths, span_order, mine, other, down_mine, down_other, g_low, residual, inverse_m, att, wqkv,
        wout, qkv, xa, xb, cos_table, sin_table,
    )
    got = send(other, lay.core)
    got, mine = fence(got, mine)
    c5 = send(u3, lay.inward)
    r = halves(plus(mine, got))
    got = send(r[1], lay.second)
    v_gu = v_mlp[: KV * rows]
    c5, r, got, v_gu = fence(c5, r, got, v_gu)
    c4 = send(plus(u3, c5), lay.inner)
    c3 = send(u2, lay.inward)
    r = halves(plus(r[0], got))
    got = send(r[1], lay.first)
    got_down = send(db, lay.first)
    c4, c3, r, got, got_down = fence(c4, c3, r, got, got_down)
    c1, c2 = kernel_call(sums_kernel, (shaped(both, WIDE), shaped(both, WIDE)))((), u1, c4, u2, c3)
    c1 = send(c1, lay.pair)
    c2 = send(c2, lay.inner)
    v_gu = lay.exchange(v_gu.reshape(KV, rows, wide))
    grad_down = kernel_call(unpack_down_kernel, shaped(low, width, dtype=F32))((), v_mlp[KV * rows :])
    block_out = kernel_call(finish_kernel, shaped(own, width))(
        (meta, lengths, span_order), residual, da, got_down
    )
    grad_in = kernel_call(norm_back_low_kernel, shaped(own, width))(
        (), g_res2, hidden_in.reshape(own, width), inverse, r[0], got
    )
    c1, c2, v_gu, grad_down, block_out, grad_in = fence(c1, c2, v_gu, grad_down, block_out, grad_in)
    c0 = u0
    v_qkv, v_out = kernel_call(last_sum_kernel, (shaped(KV, rows, WIDE), shaped(*w_out.shape)))((), c0, c1, c2)
    grad_out = send(v_out, lay.back)

    def share(v_qkv, v_gu, w_gate, w_up, gain_m):
        v_qkv = lay.exchange(v_qkv)
        grad_gate, grad_up, total_m = kernel_call(
            unpack_mlp_kernel,
            (shaped(*w_gate.shape, dtype=F32), shaped(*w_up.shape, dtype=F32), shaped(1, rows, dtype=F32)),
        )((), v_gu, w_gate, w_up, gain_m)
        return v_qkv, grad_gate, grad_up, total_m

    v_qkv, grad_gate, grad_up, total_m = unit_of_work(go, share, v_qkv, v_gu, w_gate, w_up, gain_m)
    grad_out = grad_out.astype(F32)
    grad_query, grad_key, grad_value, total = kernel_call(
        unpack_attention_kernel,
        tuple(shaped(*w.shape, dtype=F32) for w in (w_query, w_key, w_value)) + (shaped(1, rows, dtype=F32),),
    )((), v_qkv, w_query, w_key, w_value, gain)
    return (
        block_out.reshape(hidden_in.shape), grad_in.reshape(hidden_in.shape), total[0], grad_query, grad_key, grad_value,
        grad_out, total_m[0], grad_gate, grad_up, grad_down,
    )


def anywhere(
    hidden_in, lengths, span_order, attn_gain, w_query, w_key, w_value, w_out,
    mlp_gain, w_gate, w_up, w_down, out_grad,
):
    lay = Layout()
    micro, slots, width = hidden_in.shape
    rows, nz = w_query.shape[0], lay.nz
    gain = attn_gain.astype(F32)[:, None]
    gain_m = mlp_gain.astype(F32)[:, None]
    pos = jnp.concatenate([positions_of(span_order, k, slots) for k in range(lay.ctx)])
    usable = (positions_of(span_order, lay.c, slots)[None, :] < lengths[:, None]).astype(F32)[..., None]
    cosines, sines = rope_tables(pos)
    length = slots * lay.ctx

    def tokens(x):
        return lax.all_gather(x, "ctx", axis=1, tiled=True).reshape(micro * length, width)

    def own(x):
        x = x.astype(BF).reshape(micro, length, width)
        return lax.psum_scatter(x, "ctx", scatter_dimension=1, tiled=True).astype(F32)

    spread, collect = lay.spread, lay.gather_sum
    wqkv = spread(lay.exchange(pack_attention(w_query, w_key, w_value, gain)).reshape(KV * rows, -1))
    wgu = spread(lay.exchange(pack_mlp(w_gate, w_up, gain_m, nz)).reshape(KV * rows, -1))
    wout = spread(send(w_out, lay.place))
    wdown = spread(w_down)
    source = hidden_in.astype(F32)
    unit, inverse = unit_rows(source)
    xs = tokens(unit.astype(BF))
    g_res = out_grad.astype(F32) * usable
    g_mlp = tokens(g_res.astype(BF))
    pre = mm(xs, wqkv).reshape(micro, length, -1)
    attended, kept = attend(pre, pos, lengths, cosines, sines)
    att = attended.reshape(micro * length, QW)
    residual = source + own(mm(att, wout))
    unit_m, inverse_m = unit_rows(residual)
    xm = tokens(unit_m.astype(BF))
    gate_up = mm(xm, wgu)
    hidden = swiglu(gate_up)
    block_out = (usable * (residual + own(mm(hidden, wdown)))).astype(BF)
    grad_down = collect(mm_lt(hidden, g_mlp)).astype(F32)
    g_gu = swiglu_back(gate_up, mm_rt(g_mlp, wdown))
    v_gu = lay.exchange(collect(mm_lt(xm, g_gu)).reshape(KV, rows, -1))
    u_gate, u_up = unpack_mlp(v_gu, nz)
    g_res2 = g_res + unit_back(own(mm_rt(g_gu, wgu)), unit_m, inverse_m)
    g_branch = tokens(g_res2.astype(BF))
    grad_out = send(collect(mm_lt(att, g_branch)), lay.back).astype(F32)
    g_att = mm_rt(g_branch, wout).astype(BF).reshape(micro, length, QW)
    g_pre = attend_back(g_att, kept, cosines, sines).reshape(micro * length, -1)
    v_qkv = lay.exchange(collect(mm_lt(xs, g_pre)).reshape(KV, rows, -1))
    u_q, u_k, u_v = unpack_attention(v_qkv)
    grad_in = (g_res2 + unit_back(own(mm_rt(g_pre, wqkv)), unit, inverse)).astype(BF)
    return (
        block_out, grad_in, paired((w_query, u_q), (w_key, u_k), (w_value, u_v)),
        u_q * gain, u_k * gain, u_v * gain, grad_out,
        paired((w_gate, u_gate), (w_up, u_up)), u_gate * gain_m, u_up * gain_m, grad_down,
    )


def solution(mesh):
    rows = P(AXES, None)
    tokens = P("fsdp", "ctx", None)
    line = mesh.shape["ctx"] == 4 and mesh.shape["fsdp"] == 8
    return jax.shard_map(
        on_line if line else anywhere,
        mesh=mesh,
        in_specs=(tokens, P("fsdp"), P(), P(AXES), rows, rows, rows, rows, P(AXES), rows, rows, rows, tokens),
        out_specs=(tokens, tokens, P(AXES), rows, rows, rows, rows, P(AXES), rows, rows, rows),
        check_vma=False,
    )
```

```python
import jax
import jax.numpy as jnp
import numpy as np
from jax import lax
from jax.experimental import pallas as pl
from jax.experimental.pallas import tpu as pltpu
from jax.sharding import PartitionSpec as P

H = 16
KV = 8
HD = 96
GROUP = H // KV
QW = GROUP * HD
AXES = ("fsdp", "ctx")

epsilon = 1e-05
rope_base = 100000.0
masked_score = -1e30
scale = HD ** (-0.5)
BF = jnp.bfloat16
F32 = jnp.float32


def mm(left, right):
    return jnp.dot(left, right, preferred_element_type=F32)


def mm_lt(left, right):
    return lax.dot_general(left, right, (((0,), (0,)), ((), ())), preferred_element_type=F32)


def mm_rt(left, right):
    return lax.dot_general(left, right, (((1,), (1,)), ((), ())), preferred_element_type=F32)


def plus(a, b):
    return a + b


def send(x, pairs):
    return lax.ppermute(x, AXES, pairs)


def unit_of_work(go, body, *args):
    def idle(*args):
        return jax.tree.map(lambda leaf: jnp.zeros(leaf.shape, leaf.dtype), jax.eval_shape(body, *args))

    return lax.cond(go, body, idle, *args)


def fence(*items):
    return lax.optimization_barrier(items)


class Layout:
    def __init__(self):
        self.ctx = lax.axis_size("ctx")
        self.fsdp = lax.axis_size("fsdp")
        self.tpf = KV // self.ctx
        self.nz = self.fsdp // self.tpf
        self.total = self.fsdp * self.ctx
        self.fast = self.ctx == 4 and self.tpf == 2 and self.nz == 4
        self.f = lax.axis_index("fsdp")
        self.c = lax.axis_index("ctx")
        self.z = self.f // self.tpf
        self.place = [(b, (b % self.nz) * KV + b // self.nz) for b in range(self.total)]
        self.back = [(d, s) for s, d in self.place]

    def exchange(self, x):
        if self.tpf == 1:
            return lax.all_to_all(x, "ctx", split_axis=0, concat_axis=0, tiled=True)
        groups = [[z * KV + i for i in range(KV)] for z in range(self.nz)]
        return lax.all_to_all(
            x, AXES, split_axis=0, concat_axis=0, tiled=True, axis_index_groups=groups
        )

    def lines(self):
        return [[z * KV + i for z in range(self.nz)] for i in range(KV)]

    def spread(self, x):
        if self.tpf == 1:
            return lax.all_gather(x, "fsdp", axis=0, tiled=True)
        return lax.all_gather(x, AXES, axis=0, tiled=True, axis_index_groups=self.lines())

    def gather_sum(self, x):
        x = x.astype(BF)
        if self.tpf == 1:
            return lax.psum_scatter(x, "fsdp", scatter_dimension=0, tiled=True)
        return lax.psum_scatter(
            x, AXES, scatter_dimension=0, tiled=True, axis_index_groups=self.lines()
        )


class Line(Layout):
    def __init__(self):
        super().__init__()
        total = self.total
        self.core = [(d, d ^ 1) for d in range(total)]
        self.first = [(d, d ^ (2 if d & 1 else 4)) for d in range(total)]
        self.second = [(d, d ^ (4 if d & 1 else 2)) for d in range(total)]
        self.xflip = [(d, d ^ 4) for d in range(total)]

        def planes(pairs):
            return [(s * KV + i, d * KV + i) for s, d in pairs for i in range(KV)]

        self.pair = planes([(0, 1), (1, 0), (2, 3), (3, 2)])
        self.inner = planes([(1, 2), (2, 1)])
        self.outward = planes([(1, 0), (2, 3)])
        self.inward = planes([(0, 1), (3, 2)])
        z = self.z
        low = z < 2
        self.order = [z, z ^ 1, jnp.where(low, 2, 1), jnp.where(low, 3, 0)]
        table = ((0, 1, 3, 3), (1, 0, 2, 2), (2, 2, 0, 1), (3, 3, 1, 0))
        self.slot = [
            jnp.where(z == 0, r[0], jnp.where(z == 1, r[1], jnp.where(z == 2, r[2], r[3])))
            for r in table
        ]

    def take_columns(self, x, blocks):
        width = x.shape[-1] // self.nz
        return jnp.concatenate(
            [lax.dynamic_slice_in_dim(x, k * width, width, axis=-1) for k in blocks], axis=-1
        )

    def take_rows(self, pieces):
        full = jnp.stack(pieces)
        return jnp.concatenate(
            [lax.dynamic_index_in_dim(full, k, axis=0, keepdims=False) for k in self.slot], axis=0
        )

    def to_pieces(self, x):
        full = x.reshape((self.nz, x.shape[0] // self.nz) + x.shape[1:])
        return [lax.dynamic_index_in_dim(full, k, axis=0, keepdims=False) for k in self.order]

    def all_tokens(self, x):
        x = jnp.stack([x, send(x, self.first)])
        x = jnp.stack([x, send(x, self.second)])
        x = jnp.stack([x, send(x, self.core)])
        return x.reshape(-1, x.shape[-1])

    def plane_tokens(self, x):
        x = jnp.stack([x, send(x, self.first)])
        x = jnp.stack([x, send(x, self.second)])
        other = send(x, self.core)
        return x.reshape(-1, x.shape[-1]), other.reshape(-1, x.shape[-1])

    def collect_tokens(self, x, slots):
        x = x.reshape(2, 2, 2, 2, slots, x.shape[-1])
        x = plus(x[0], send(x[1], self.core))
        x = plus(x[0], send(x[1], self.second))
        return x[0].astype(F32) + send(x[1], self.first).astype(F32)

    def to_seqs(self, x, slots):
        x = x.reshape(2, 2, 2, 2, slots, x.shape[-1])
        halves = []
        for dc in range(2):
            even = ((self.c & 1) ^ dc) == 0
            h = x[dc]
            halves.append(jnp.where(even, jnp.swapaxes(h, 0, 1), h))
        x = jnp.stack(halves, axis=0)
        x = jnp.transpose(x, (1, 3, 0, 2, 4, 5))
        return x.reshape(4, 4 * slots, x.shape[-1])

    def from_seqs(self, x, slots):
        x = x.reshape(2, 2, 2, 2, slots, x.shape[-1])
        x = jnp.transpose(x, (2, 0, 3, 1, 4, 5))
        halves = []
        for dc in range(2):
            even = ((self.c & 1) ^ dc) == 0
            h = x[dc]
            halves.append(jnp.where(even, jnp.swapaxes(h, 0, 1), h))
        return jnp.stack(halves, axis=0).reshape(16 * slots, x.shape[-1])


def positions_of(span_order, index, slots):
    span_len = slots // 2
    at = jnp.arange(slots, dtype=jnp.int32)
    pair = lax.dynamic_slice_in_dim(span_order, 2 * index, 2)
    return jnp.where(at < span_len, pair[0], pair[1]) * span_len + at % span_len


def rope_tables(pos):
    frequency = rope_base ** (-2.0 * jnp.arange(HD // 2, dtype=F32) / HD)
    angles = pos.astype(F32)[:, None] * frequency[None, :]
    return jnp.cos(angles), jnp.sin(angles)


def rotate(v, cosines, sines):
    half = HD // 2
    co, si = cosines[None, :, None, :], sines[None, :, None, :]
    one, two = v[..., :half], v[..., half:]
    return jnp.concatenate([one * co - two * si, two * co + one * si], axis=-1)


def unit_rows(x):
    inverse = lax.rsqrt(jnp.mean(x * x, axis=-1, keepdims=True) + epsilon)
    return x * inverse, inverse


def unit_back(scaled, unit, inverse):
    return inverse * (scaled - unit * jnp.mean(scaled * unit, axis=-1, keepdims=True))


def attend(pre, pos, seq_len, cosines, sines):
    seqs, length, _ = pre.shape
    q = rotate(pre[..., :QW].reshape(seqs, length, GROUP, HD), cosines, sines).astype(BF)
    k = rotate(pre[..., QW : QW + HD].reshape(seqs, length, 1, HD), cosines, sines)[:, :, 0].astype(BF)
    v = pre[..., QW + HD :].astype(BF)
    allowed = (pos[None, None, :] <= pos[None, :, None]) & (
        pos[None, None, :] < seq_len[:, None, None]
    )
    scores = jnp.einsum("sqgd,snd->sgqn", q, k, preferred_element_type=F32) * scale
    scores = jnp.where(allowed[:, None], scores, masked_score)
    top = jnp.max(scores, axis=-1, keepdims=True)
    expo = jnp.exp(scores - top)
    probs = expo / jnp.sum(expo, axis=-1, keepdims=True)
    low = probs.astype(BF)
    attended = jnp.einsum("sgqn,snd->sqgd", low, v, preferred_element_type=F32)
    return attended.astype(BF).reshape(seqs, length, QW), (q, k, v, probs, low)


def attend_back(g_att, kept, cosines, sines):
    q, k, v, probs, low = kept
    seqs, length, _ = g_att.shape
    g_att = g_att.reshape(seqs, length, GROUP, HD)
    g_probs = jnp.einsum("sqgd,snd->sgqn", g_att, v, preferred_element_type=F32)
    inner = jnp.sum(probs * g_probs, axis=-1, keepdims=True)
    g_scores = (probs * (g_probs - inner)).astype(BF)
    g_q = jnp.einsum("sgqn,snd->sqgd", g_scores, k, preferred_element_type=F32) * scale
    g_k = jnp.einsum("sgqn,sqgd->snd", g_scores, q, preferred_element_type=F32) * scale
    g_v = jnp.einsum("sgqn,sqgd->snd", low, g_att, preferred_element_type=F32)
    return jnp.concatenate(
        [
            rotate(g_q, cosines, -sines).astype(BF).reshape(seqs, length, QW),
            rotate(g_k[:, :, None], cosines, -sines).astype(BF)[:, :, 0],
            g_v.astype(BF),
        ],
        axis=-1,
    )


def swiglu(gate_up):
    half = gate_up.shape[-1] // 2
    gate, up = gate_up[:, :half], gate_up[:, half:]
    return (jax.nn.silu(gate) * up).astype(BF)


def swiglu_back(gate_up, g_hidden):
    half = gate_up.shape[-1] // 2
    gate, up = gate_up[:, :half], gate_up[:, half:]
    sig = jax.nn.sigmoid(gate)
    g_gate = (g_hidden * up * sig * (1.0 + gate * (1.0 - sig))).astype(BF)
    g_up = (g_hidden * gate * sig).astype(BF)
    return jnp.concatenate([g_gate, g_up], axis=-1)


def pack_attention(w_query, w_key, w_value, gain):
    rows = w_query.shape[0]
    parts = [
        (w.astype(F32) * gain).astype(BF).reshape(rows, KV, w.shape[1] // KV)
        for w in (w_query, w_key, w_value)
    ]
    return jnp.transpose(jnp.concatenate(parts, axis=2), (1, 0, 2))


def unpack_attention(u):
    u = jnp.transpose(u, (1, 0, 2)).astype(F32)
    rows = u.shape[0]
    return (
        u[..., :QW].reshape(rows, KV * QW),
        u[..., QW : QW + HD].reshape(rows, KV * HD),
        u[..., QW + HD :].reshape(rows, KV * HD),
    )


def pack_mlp(w_gate, w_up, gain, nz):
    rows = w_gate.shape[0]

    def columns(w):
        w = (w.astype(F32) * gain).astype(BF).reshape(rows, nz, KV, -1)
        return jnp.transpose(w, (2, 0, 1, 3)).reshape(KV, rows, -1)

    return jnp.concatenate([columns(w_gate), columns(w_up)], axis=2)


def unpack_mlp(u, nz):
    rows = u.shape[1]
    u = u.reshape(KV, rows, 2, nz, -1)
    u = jnp.transpose(u, (2, 1, 3, 0, 4)).reshape(2, rows, -1).astype(F32)
    return u[0], u[1]


SMEM = pl.BlockSpec(memory_space=pltpu.SMEM)
VMEM = pl.BlockSpec(memory_space=pltpu.VMEM)
WIDE = QW + 2 * HD
FREE = pl.CostEstimate(flops=0, bytes_accessed=0, transcendentals=0)
ROOM = pltpu.CompilerParams(vmem_limit_bytes=56 * 1024 * 1024)


def shaped(*shape, dtype=BF):
    return jax.ShapeDtypeStruct(shape, dtype)


def kernel_call(body, outs, scratch=()):
    def call(scalars, *arrays):
        return pl.pallas_call(
            body,
            out_shape=outs,
            in_specs=[SMEM] * len(scalars) + [VMEM] * len(arrays),
            out_specs=jax.tree.map(lambda _: VMEM, outs),
            scratch_shapes=list(scratch),
            compiler_params=ROOM,
            cost_estimate=FREE,
        )(*scalars, *arrays)

    return call


def moving_call(body, outs, scratch=(), copies=1):
    def call(scalars, *arrays):
        anywhere_spec = pl.BlockSpec(memory_space=pl.ANY)
        return pl.pallas_call(
            body,
            out_shape=outs,
            in_specs=[SMEM] * len(scalars) + [pl.BlockSpec(memory_space=pltpu.HBM)] * len(arrays),
            out_specs=jax.tree.map(lambda _: anywhere_spec, outs),
            scratch_shapes=list(scratch) + [pltpu.SemaphoreType.DMA((copies,))],
            compiler_params=ROOM,
            cost_estimate=FREE,
        )(*scalars, *arrays)

    return call


class Copies:
    def __init__(self, sems):
        self.sems = sems
        self.used = 0

    def start(self, source, target):
        copy = pltpu.make_async_copy(source, target, self.sems.at[self.used])
        self.used += 1
        copy.start()
        return copy


def vmem(*arrays):
    return [pltpu.VMEM(a.shape, a.dtype) for a in arrays]


def dot(a, b, dims=((1,), (0,))):
    return lax.dot_general(a, b, (dims, ((), ())), preferred_element_type=F32)


LEFT_T = ((0,), (0,))
RIGHT_T = ((1,), (1,))


def block_rows(core, seq, dc, dy, slots):
    dx, m = seq // 2, seq % 2
    even = (core ^ dc) == 0
    s1 = jnp.where(even, dx, dy)
    s2 = jnp.where(even, dy, dx)
    return pl.multiple_of(((s2 * 2 + s1) * 2 + m) * slots, slots)


def blocks_of(slots):
    for dc in range(2):
        for dy in range(2):
            b = dc * 2 + dy
            yield dc, dy, slice(b * slots, (b + 1) * slots)


def spans_of(spans, ctx):
    out = []
    for dc in range(2):
        for dy in range(2):
            other = ctx ^ (dy * 2 + dc)
            out += [spans[2 * other], spans[2 * other + 1]]
    return out


def along(held, length, axis, shape):
    at = lax.broadcasted_iota(jnp.int32, shape, axis) % length
    step = length // len(held)
    pos = at % step
    for i, span in enumerate(held):
        pos = pos + jnp.where(at // step == i, span * step, 0)
    return pos


def rotary_rows(held, table, out):
    step = out.shape[0] // len(held)
    for i, span in enumerate(held):
        out[i * step : (i + 1) * step, :] = table[pl.ds(pl.multiple_of(span * step, step), step), :]


def rotary_copies(copies, held, table, out):
    step = out.shape[0] // len(held)
    return [
        copies.start(table.at[pl.ds(pl.multiple_of(span * step, step), step)], out.at[pl.ds(i * step, step)])
        for i, span in enumerate(held)
    ]


def turn(x, cosines, sines):
    half, width = HD // 2, x.shape[1]
    lane = lax.broadcasted_iota(jnp.int32, x.shape, 1) % HD
    partner = jnp.where(lane < half, pltpu.roll(x, width - half, 1), pltpu.roll(x, half, 1))
    return x * cosines + partner * sines


def probabilities(q, k, allowed):
    scores = jnp.where(allowed, dot(q, k, RIGHT_T) * scale, masked_score)
    expo = jnp.exp(scores - jnp.max(scores, axis=-1, keepdims=True))
    return expo / jnp.sum(expo, axis=-1, keepdims=True)


def heads_of(x):
    return [x[:, h * HD : (h + 1) * HD] for h in range(x.shape[1] // HD)]


def assemble(meta, pieces, out):
    p0, p1, p2, p3, p4, p5 = pieces
    step = p0.shape[0]
    for s, parts in enumerate(((p0,), (p1,), (p2, p3), (p4, p5))):
        piece = parts[0][...]
        if len(parts) > 1:
            piece = piece + parts[1][...]
        out[pl.ds(pl.multiple_of(meta[s] * step, step), step), :] = piece


def fetch_qkv(full, out):
    step = full.shape[2]
    for z in range(full.shape[0]):
        out[z * step : (z + 1) * step, :] = full[z, :step, :]


def fetch_out(full, out):
    nz, total, step = full.shape
    count = out.shape[1] // step
    rows = (total - step) // count
    for z in range(nz):
        for k in range(count):
            out[z * rows : (z + 1) * rows, k * step : (k + 1) * step] = full[
                z, step + k * rows : step + (k + 1) * rows, :
            ]


def stacked_columns(x, cut):
    return jnp.concatenate([x[:, k : k + cut] for k in range(0, x.shape[1], cut)], axis=0)


def column(row):
    n = row.shape[1]
    same = lax.broadcasted_iota(jnp.int32, (n, n), 0) == lax.broadcasted_iota(jnp.int32, (n, n), 1)
    return jnp.sum(jnp.where(same, row, 0.0), axis=1, keepdims=True)


def row_of(col):
    n = col.shape[0]
    same = lax.broadcasted_iota(jnp.int32, (n, n), 0) == lax.broadcasted_iota(jnp.int32, (n, n), 1)
    return jnp.sum(jnp.where(same, col, 0.0), axis=0, keepdims=True)


def pack_attention_kernel(wq, wk, wv, gain, out):
    g = column(gain[...].astype(F32))
    q, k, v = ((w[...].astype(F32) * g).astype(BF) for w in (wq, wk, wv))
    for j in range(KV):
        out[j] = jnp.concatenate(
            [q[:, j * QW : (j + 1) * QW], k[:, j * HD : (j + 1) * HD], v[:, j * HD : (j + 1) * HD]], axis=1
        )


def pack_mlp_kernel(wg, wu, gain, out):
    g = column(gain[...].astype(F32))
    half = out.shape[2] // 2
    blocks = 4
    hid = half // blocks
    for h, w in enumerate((wg, wu)):
        x = (w[...].astype(F32) * g).astype(BF)
        for z in range(blocks):
            for j in range(KV):
                out[j, :, h * half + z * hid : h * half + (z + 1) * hid] = x[
                    :, (z * KV + j) * hid : (z * KV + j + 1) * hid
                ]


def unpack_attention_kernel(u, wq, wk, wv, gain, gq, gk, gv, total):
    g = column(gain[...].astype(F32))
    acc = jnp.zeros(g.shape, F32)
    for w, out, lo, n in ((wq, gq, 0, QW), (wk, gk, QW, HD), (wv, gv, QW + HD, HD)):
        part = jnp.concatenate([u[j, :, lo : lo + n] for j in range(KV)], axis=1).astype(F32)
        out[...] = part * g
        acc += jnp.sum(part * w[...].astype(F32), axis=1, keepdims=True)
    total[...] = row_of(acc)


def unpack_mlp_kernel(u, wg, wu, gain, gg, gu, total):
    g = column(gain[...].astype(F32))
    acc = jnp.zeros(g.shape, F32)
    half = wg.shape[1] // KV
    blocks = 4
    hid = half // blocks
    for j in range(KV):
        x = u[j].astype(F32)
        for h, (w, out) in enumerate(((wg, gg), (wu, gu))):
            for z in range(blocks):
                at = slice((z * KV + j) * hid, (z * KV + j + 1) * hid)
                part = x[:, h * half + z * hid : h * half + (z + 1) * hid]
                out[:, at] = part * g
                acc += jnp.sum(part * w[:, at].astype(F32), axis=1, keepdims=True)
    total[...] = row_of(acc)


def usable_rows(lens, spans, ctx, shape):
    at = lax.broadcasted_iota(jnp.int32, shape, 0)
    slots = shape[0] // 2
    slot, step = at % slots, slots // 2
    pos = jnp.where(slot < step, spans[2 * ctx], spans[2 * ctx + 1]) * step + slot % step
    length = jnp.where(at < slots, lens[0], lens[1])
    return (pos < length).astype(F32)


def prepare_kernel(meta, lens, spans, x, g, xhat, inverse, g_low):
    v = x[...].astype(F32)
    inv = lax.rsqrt(jnp.mean(v * v, axis=-1, keepdims=True) + epsilon)
    inverse[...] = inv
    xhat[...] = (v * inv).astype(BF)
    g_low[...] = (g[...].astype(F32) * usable_rows(lens, spans, meta[5], inverse.shape)).astype(BF)


def finish_kernel(meta, lens, spans, residual, a, b, out):
    total = residual[...] + a[...].astype(F32) + b[...].astype(F32)
    out[...] = (total * usable_rows(lens, spans, meta[5], (total.shape[0], 1))).astype(BF)


def attention_kernel(
    meta, lens, spans, xa, xb, full, cos_table, sin_table, wqkv, qkv, att, xseq, cosines, sines
):
    core, ctx = meta[4], meta[5]
    slots = xa.shape[0] // 8
    length = xseq.shape[0]
    fetch_qkv(full, wqkv)
    held = spans_of(spans, ctx)
    rotary_rows(held, cos_table, cosines)
    rotary_rows(held, sin_table, sines)
    posc = along(held, length, 0, (GROUP * length, length))
    posr = along(held, length, 1, (GROUP * length, length))
    causal = posr <= posc

    def one(seq, carry):
        for dc, dy, rows in blocks_of(slots):
            xseq[rows, :] = (xa, xb)[dc][pl.ds(block_rows(core, seq, dc, dy, slots), slots), :]
        low = turn(dot(xseq[...], wqkv[...]), cosines[...], sines[...]).astype(BF)
        qkv[seq] = low
        one_q, two_q, k, v = heads_of(low)
        q = jnp.concatenate([one_q, two_q], axis=0)
        allowed = causal & (posr < lens[seq])
        mixed = dot(probabilities(q, k, allowed).astype(BF), v)
        out = jnp.concatenate([mixed[:length], mixed[length:]], axis=1).astype(BF)
        for dc, dy, rows in blocks_of(slots):
            att[dc, pl.ds(block_rows(core, seq, dc, dy, slots), slots), :] = out[rows]
        return carry

    lax.fori_loop(0, 4, one, 0, unroll=True)


def project_kernel(att, full, wout, theirs):
    fetch_out(full, wout)
    theirs[...] = dot(att[1], wout[...]).astype(BF)


def project_own_kernel(att, wout, mine):
    mine[...] = dot(att[0], wout[...]).astype(BF)


def attention_back_kernel(
    meta, lens, spans,
    h_ga, h_gb, h_att, h_wout, h_wqkv, h_qkv, h_xa, h_xb, cos_table, sin_table,
    o_mine, o_theirs, o0, o1, o2, o3,
    ga, gb, att, wout, wqkv, qkv, xa, xb, mine, theirs, u0, u1, u2, u3, g_pre, gseq, cosines, sines, out_grad, sems,
):
    copies = Copies(sems)
    held = spans_of(spans, meta[5])
    first = [copies.start(h, v) for h, v in ((h_wout, wout), (h_qkv, qkv), (h_ga, ga), (h_gb, gb))]
    first += rotary_copies(copies, held, cos_table, cosines) + rotary_copies(copies, held, sin_table, sines)
    for c in first:
        c.wait()
    later = [copies.start(h, v) for h, v in ((h_xa, xa), (h_xb, xb), (h_att, att), (h_wqkv, wqkv))]
    core, ctx = meta[4], meta[5]
    slots = ga.shape[0] // 8
    length = gseq.shape[0]
    posc = along(held, length, 0, (GROUP * length, length))
    posr = along(held, length, 1, (GROUP * length, length))
    causal = posr <= posc

    def one(seq, carry):
        for dc, dy, rows in blocks_of(slots):
            gseq[rows, :] = (ga, gb)[dc][pl.ds(block_rows(core, seq, dc, dy, slots), slots), :]
        g_att = dot(gseq[...], wout[...], RIGHT_T).astype(BF)
        one_q, two_q, k, v = heads_of(qkv[seq])
        q = jnp.concatenate([one_q, two_q], axis=0)
        g = jnp.concatenate(heads_of(g_att), axis=0)
        allowed = causal & (posr < lens[seq])
        p = probabilities(q, k, allowed)
        g_p = dot(g, v, RIGHT_T)
        g_s = (p * (g_p - jnp.sum(p * g_p, axis=-1, keepdims=True))).astype(BF)
        g_q = dot(g_s, k) * scale
        g_k = dot(g_s, q, LEFT_T) * scale
        g_v = dot(p.astype(BF), g, LEFT_T)
        full = jnp.concatenate([g_q[:length], g_q[length:], g_k, g_v], axis=1)
        out = turn(full, cosines[...], -sines[...]).astype(BF)
        for dc, dy, rows in blocks_of(slots):
            g_pre[dc, pl.ds(block_rows(core, seq, dc, dy, slots), slots), :] = out[rows]
        return carry

    lax.fori_loop(0, 4, one, 0, unroll=True)
    for c in later:
        c.wait()
    gone = []
    out_grad[...] = (dot(att[0], ga[...], LEFT_T) + dot(att[1], gb[...], LEFT_T)).astype(BF)
    step = xa.shape[1] // 4
    block = u0.shape[1]
    count = out_grad.shape[1] // block
    low = out_grad.shape[0] // 4
    for s, u, o in ((3, u3, o3), (2, u2, o2), (1, u1, o1), (0, u0, o0)):
        at = pl.ds(pl.multiple_of(meta[s] * step, step), step)
        u[:step, :] = (dot(xa[:, at], g_pre[0], LEFT_T) + dot(xb[:, at], g_pre[1], LEFT_T)).astype(BF)
        at = pl.ds(pl.multiple_of(meta[s] * low, low), low)
        for k in range(count):
            u[step + k * low : step + (k + 1) * low, :] = out_grad[at, k * block : (k + 1) * block]
        gone.append(copies.start(u, o))
    theirs[...] = dot(g_pre[1], wqkv[...], RIGHT_T).astype(BF)
    gone.append(copies.start(theirs, o_theirs))
    mine[...] = dot(g_pre[0], wqkv[...], RIGHT_T).astype(BF)
    gone.append(copies.start(mine, o_mine))
    for c in gone:
        c.wait()


def mlp_kernel(
    meta,
    h_ma, h_mb, h_ea, h_eb, h_wgu, h0, h1, h2, h3, h4, h5,
    o_down_mine, o_down_theirs, o_mine, o_theirs, o_u,
    x, g, back, down, wgu, d0, d1, d2, d3, d4, d5, u, hidden, g_gu, wdown, sems,
):
    copies = Copies(sems)
    came = [copies.start(h_wgu, wgu), copies.start(h_mb, x.at[1])]
    pieces = (d0, d1, d2, d3, d4, d5)
    came += [copies.start(h, d) for h, d in zip((h0, h1, h2, h3, h4, h5), pieces)]
    came += [copies.start(h_eb, g.at[1])]
    later = [copies.start(h_ma, x.at[0]), copies.start(h_ea, g.at[0])]
    half = wgu.shape[1] // 2
    for c in came:
        c.wait()
    assemble(meta, pieces, wdown)
    out_copies = [
        pltpu.make_async_copy(v, o, sems.at[copies.used + k])
        for k, (v, o) in enumerate(
            ((back.at[1], o_theirs), (down.at[1], o_down_theirs), (back.at[0], o_mine), (down.at[0], o_down_mine))
        )
    ]
    copies.used += 4

    def one(i, carry):
        part = 1 - i

        @pl.when(i == 1)
        def _():
            for c in later:
                c.wait()

        gate_up = dot(x[part], wgu[...])
        gate, up = gate_up[:, :half], gate_up[:, half:]
        sig = 1.0 / (1.0 + jnp.exp(-gate))
        act = gate * sig
        hidden[part] = (act * up).astype(BF)
        g_hidden = dot(g[part], wdown[...], RIGHT_T)
        g_gu[part, :, :half] = (g_hidden * up * sig * (1.0 + gate * (1.0 - sig))).astype(BF)
        g_gu[part, :, half:] = (g_hidden * act).astype(BF)
        back[part] = dot(g_gu[part], wgu[...], RIGHT_T).astype(BF)
        down[part] = dot(hidden[part], wdown[...]).astype(BF)

        @pl.when(i == 0)
        def _():
            out_copies[0].start()
            out_copies[1].start()

        @pl.when(i == 1)
        def _():
            out_copies[2].start()
            out_copies[3].start()

        return carry

    lax.fori_loop(0, 2, one, 0)
    nz, _, wide = u.shape
    piece = x.shape[2] // nz
    step = hidden.shape[2] // nz
    base = copies.used

    def grads(z, carry):
        at = pl.ds(pl.multiple_of(z * piece, piece), piece)
        both = dot(x[0, :, at], g_gu[0], LEFT_T) + dot(x[1, :, at], g_gu[1], LEFT_T)
        u[z, :piece, :] = both.astype(BF)
        at = pl.ds(pl.multiple_of(z * step, step), step)
        both = (dot(hidden[0, :, at], g[0], LEFT_T) + dot(hidden[1, :, at], g[1], LEFT_T)).astype(BF)
        u[z, piece : piece + step, :] = both[:, :wide]
        rest = both.shape[1] - wide
        u[z, piece + step :, :rest] = both[: step // 2, wide:]
        u[z, piece + step :, rest:] = both[step // 2 :, wide:]
        pltpu.make_async_copy(u.at[z], o_u.at[z], sems.at[base + z]).start()
        return carry

    lax.fori_loop(0, nz, grads, 0)
    for c in out_copies:
        c.wait()
    for z in range(nz):
        pltpu.make_async_copy(u.at[z], o_u.at[z], sems.at[base + z]).wait()


def unpack_down_kernel(u, out):
    step, wide = out.shape[0], u.shape[1]
    rest = out.shape[1] - wide
    out[:, :wide] = u[:step, :].astype(F32)
    out[: step // 2, wide:] = u[step:, :rest].astype(F32)
    out[step // 2 :, wide:] = u[step:, rest:].astype(F32)


def sums_kernel(a, b, c, d, ab, cd):
    ab[...] = a[...] + b[...]
    cd[...] = c[...] + d[...]


def last_sum_kernel(a, b, c, qkv, out):
    total = (a[...].astype(F32) + b[...].astype(F32) + c[...].astype(F32)).astype(BF)
    blocks, rows, width = qkv.shape
    for j in range(blocks):
        qkv[j] = total[j * rows : (j + 1) * rows]
    low = out.shape[0]
    for k in range(out.shape[1] // width):
        at = blocks * rows + k * low
        out[:, k * width : (k + 1) * width] = total[at : at + low]


def norm_kernel(source, a, b, residual, xhat, inverse):
    r = source[...].astype(F32) + a[...].astype(F32) + b[...].astype(F32)
    inv = lax.rsqrt(jnp.mean(r * r, axis=-1, keepdims=True) + epsilon)
    residual[...] = r
    inverse[...] = inv
    xhat[...] = (r * inv).astype(BF)


def norm_back(g_res, source, inverse, a, b):
    scaled = a[...].astype(F32) + b[...].astype(F32)
    inv = inverse[...]
    unit = source[...].astype(F32) * inv
    back = inv * (scaled - unit * jnp.mean(scaled * unit, axis=-1, keepdims=True))
    return g_res[...].astype(F32) + back


def norm_back_kernel(g_res, source, inverse, a, b, out, low):
    g = norm_back(g_res, source, inverse, a, b)
    out[...] = g
    low[...] = g.astype(BF)


def norm_back_low_kernel(g_res, source, inverse, a, b, low):
    low[...] = norm_back(g_res, source, inverse, a, b).astype(BF)


def rotary_constants(total):
    frequency = rope_base ** (-2.0 * np.arange(HD // 2, dtype=np.float32) / HD).astype(np.float32)
    angles = np.arange(total, dtype=np.float32)[:, None] * frequency[None, :].astype(np.float32)
    c, s = np.cos(angles), np.sin(angles)
    flat, signed = np.concatenate([c, c], 1), np.concatenate([-s, s], 1)
    cosines = np.concatenate([flat] * (GROUP + 1) + [np.ones_like(flat)], 1)
    sines = np.concatenate([signed] * (GROUP + 1) + [np.zeros_like(flat)], 1)
    return jnp.asarray(cosines, F32), jnp.asarray(sines, F32)


def paired(*items):
    return sum(jnp.sum(w.astype(F32) * g, axis=1) for w, g in items)


def on_line(
    hidden_in, lengths, span_order, attn_gain, w_query, w_key, w_value, w_out,
    mlp_gain, w_gate, w_up, w_down, out_grad,
):
    lay = Line()
    _, slots, width = hidden_in.shape
    rows, nz = w_query.shape[0], lay.nz
    tokens, length, own = 16 * slots, 4 * slots, 2 * slots
    go = lengths[0] > 0
    meta = jnp.stack([k.astype(jnp.int32) for k in (*lay.order, lay.c & 1, lay.c)])
    gain, gain_m = attn_gain[None, :], mlp_gain[None, :]
    cos_table, sin_table = rotary_constants(length)

    def halves(x):
        return x.reshape(2, x.shape[0] // 2, width)

    wide = w_gate.shape[1] * 2 // KV
    cut = wide // 2
    tables = [pltpu.VMEM((length, WIDE), F32)] * 2

    def flat(x):
        return x.reshape(-1, width)

    d1 = send(w_down, lay.pair)
    d2 = send(w_down, lay.inner)
    q0 = lay.exchange(
        kernel_call(pack_attention_kernel, shaped(KV, rows, WIDE))((), w_query, w_key, w_value, gain)
    )
    theirs = send(lengths, lay.xflip)
    o0 = send(w_out, lay.place)
    gu_s = kernel_call(pack_mlp_kernel, shaped(KV, rows, wide))((), w_gate, w_up, gain_m)
    xhat, inverse, g_low = kernel_call(
        prepare_kernel, (shaped(own, width), shaped(own, 1, dtype=F32), shaped(own, width))
    )((meta, lengths, span_order), hidden_in.reshape(own, width), out_grad.reshape(own, width))
    q0, d1, d2, theirs, gu_s, xhat, g_low = fence(q0, d1, d2, theirs, gu_s, xhat, g_low)
    d3 = send(d2, lay.outward)
    d4 = send(d1, lay.inner)
    x1 = send(xhat, lay.first)
    attn_piece = jnp.concatenate([q0.reshape(KV * rows, WIDE), stacked_columns(o0, WIDE)], axis=0)
    d3, d4, x1, attn_piece = fence(d3, d4, x1, attn_piece)
    attn_full = lay.spread(attn_piece)

    def gather(xhat, x1, g_low, gu_s):
        gu0 = lay.exchange(gu_s)
        x01 = jnp.stack([xhat, x1])
        x2 = send(x01, lay.second)
        x2, gu0, x01, g_low = fence(x2, gu0, x01, g_low)
        x0123 = jnp.stack([x01, x2])
        x3 = send(x0123, lay.core)
        e1 = send(g_low, lay.first)
        x3, x0123, e1 = fence(x3, x0123, e1)
        e01 = jnp.stack([g_low, e1])
        return x0123, x3, gu0, e01

    xa, xb, gu0, e01 = unit_of_work(go, gather, xhat, x1, g_low, gu_s)
    attn_full, gu0 = fence(attn_full, gu0)
    wgu = lay.spread(gu0.reshape(KV * rows, wide))
    d5 = send(d4, lay.outward)
    attn_full = attn_full.reshape(nz, -1, WIDE)
    seq_len = jnp.concatenate([lengths, theirs])

    def forward(meta, seq_len, span_order, xa, xb, attn_full, cos_table, sin_table, hidden_in, e01):
        e2 = send(e01, lay.second)
        wqkv, qkv, att = kernel_call(
            attention_kernel,
            (shaped(width, WIDE), shaped(4, length, WIDE), shaped(2, tokens // 2, QW)),
            scratch=[pltpu.VMEM((length, width), BF)] + tables,
        )((meta, seq_len, span_order), flat(xa), flat(xb), attn_full, cos_table, sin_table)
        wout, other = kernel_call(project_kernel, (shaped(QW, width), shaped(tokens // 2, width)))((), att, attn_full)
        wqkv, qkv, att, wout, other, e2 = fence(wqkv, qkv, att, wout, other, e2)
        got = send(other, lay.core)
        mine = kernel_call(project_own_kernel, shaped(tokens // 2, width))((), att, wout)
        got, mine = fence(got, mine)
        r = halves(plus(mine, got))
        e0123 = jnp.stack([e01, e2])
        r, e0123 = fence(r, e0123)
        got = send(r[1], lay.second)
        e3 = send(e0123, lay.core)
        got, e3, r = fence(got, e3, r)
        r = halves(plus(r[0], got))
        got = send(r[1], lay.first)
        residual, xm0, inverse_m = kernel_call(
            norm_kernel, (shaped(own, width, dtype=F32), shaped(own, width), shaped(own, 1, dtype=F32))
        )((), hidden_in.reshape(own, width), r[0], got)
        m01 = jnp.stack([xm0, send(xm0, lay.first)])
        m2 = send(m01, lay.second)
        ma = jnp.stack([m01, m2])
        mb = send(ma, lay.core)
        return wqkv, qkv, att, wout, residual, inverse_m, flat(ma), flat(mb), flat(e0123), flat(e3)

    wqkv, qkv, att, wout, residual, inverse_m, ma, mb, ea, eb = unit_of_work(
        go, forward, meta, seq_len, span_order, xa, xb, attn_full, cos_table, sin_table, hidden_in, e01
    )
    half_rows = shaped(tokens // 2, width)
    low = w_down.shape[0]
    piece = KV * rows + low * width // wide
    outs = (half_rows, half_rows, half_rows, half_rows, shaped(nz, piece, wide))
    ins = (ma, mb, ea, eb, wgu, w_down, d1, d2, d3, d4, d5)
    down_mine, down_other, mine, other, u_mlp = moving_call(
        mlp_kernel,
        outs,
        scratch=[pltpu.VMEM((2, tokens // 2, width), BF)] * 4
        + vmem(*ins[4:], outs[4])
        + [pltpu.VMEM((2, tokens // 2, cut), BF), pltpu.VMEM((2, tokens // 2, wide), BF), pltpu.VMEM((cut, width), BF)],
        copies=len(ins) + 4 + nz,
    )((meta,), *ins)
    v_mlp = lay.gather_sum(u_mlp.reshape(nz * piece, wide))
    both = KV * rows + QW // nz * width // WIDE

    def backward(
        meta, seq_len, lengths, span_order, mine, other, down_mine, down_other, g_low, residual, inverse_m, att, wqkv, wout, qkv,
        xa, xb, cos_table, sin_table,
    ):
        got = send(other, lay.core)
        got, mine = fence(got, mine.astype(F32))
        r = halves((mine + got.astype(F32)).astype(BF))
        r = halves(plus(r[0], send(r[1], lay.second)))
        got = send(r[1], lay.first)
        got_down = send(down_other, lay.core)
        g_res2, h0 = kernel_call(
            norm_back_kernel, (shaped(own, width, dtype=F32), shaped(own, width))
        )((), g_low, residual, inverse_m, r[0], got)
        ga, gb = lay.plane_tokens(h0)
        d = halves(plus(down_mine, got_down))
        ga, gb, d = fence(ga, gb, d)
        got_down = send(d[1], lay.second)
        outs = [half_rows, half_rows] + [shaped(both, WIDE)] * nz
        ins = (ga, gb, att, wout, wqkv, qkv, flat(xa), flat(xb))
        mine, other, u0, u1, u2, u3 = moving_call(
            attention_back_kernel,
            outs,
            scratch=vmem(*ins, *outs)
            + [pltpu.VMEM((2, tokens // 2, WIDE), BF), pltpu.VMEM((length, width), BF)]
            + tables
            + [pltpu.VMEM((QW, width), BF)],
            copies=len(ins) + len(outs) + 16,
        )((meta, seq_len, span_order), *ins, cos_table, sin_table)
        got_down, mine, other, u0, u1, u2, u3 = fence(got_down, mine, other, u0, u1, u2, u3)
        d = halves(plus(d[0], got_down))
        return g_res2, mine, other, d[0], d[1], u3, u2, u1, u0

    g_res2, mine, other, da, db, u3, u2, u1, u0 = unit_of_work(
        go, backward, meta, seq_len, lengths, span_order, mine, other, down_mine, down_other, g_low, residual, inverse_m, att, wqkv,
        wout, qkv, xa, xb, cos_table, sin_table,
    )
    got = send(other, lay.core)
    got, mine = fence(got, mine)
    c5 = send(u3, lay.inward)
    r = halves(plus(mine, got))
    got = send(r[1], lay.second)
    v_gu = v_mlp[: KV * rows]
    c5, r, got, v_gu = fence(c5, r, got, v_gu)
    c4 = send(plus(u3, c5), lay.inner)
    c3 = send(u2, lay.inward)
    r = halves(plus(r[0], got))
    got = send(r[1], lay.first)
    got_down = send(db, lay.first)
    c4, c3, r, got, got_down = fence(c4, c3, r, got, got_down)
    c1, c2 = kernel_call(sums_kernel, (shaped(both, WIDE), shaped(both, WIDE)))((), u1, c4, u2, c3)
    c1 = send(c1, lay.pair)
    c2 = send(c2, lay.inner)
    v_gu = lay.exchange(v_gu.reshape(KV, rows, wide))
    grad_down = kernel_call(unpack_down_kernel, shaped(low, width, dtype=F32))((), v_mlp[KV * rows :])
    block_out = kernel_call(finish_kernel, shaped(own, width))(
        (meta, lengths, span_order), residual, da, got_down
    )
    grad_in = kernel_call(norm_back_low_kernel, shaped(own, width))(
        (), g_res2, hidden_in.reshape(own, width), inverse, r[0], got
    )
    c1, c2, v_gu, grad_down, block_out, grad_in = fence(c1, c2, v_gu, grad_down, block_out, grad_in)
    c0 = u0
    v_qkv, v_out = kernel_call(last_sum_kernel, (shaped(KV, rows, WIDE), shaped(*w_out.shape)))((), c0, c1, c2)
    grad_out = send(v_out, lay.back)

    def share(v_qkv, v_gu, w_gate, w_up, gain_m):
        v_qkv = lay.exchange(v_qkv)
        grad_gate, grad_up, total_m = kernel_call(
            unpack_mlp_kernel,
            (shaped(*w_gate.shape, dtype=F32), shaped(*w_up.shape, dtype=F32), shaped(1, rows, dtype=F32)),
        )((), v_gu, w_gate, w_up, gain_m)
        return v_qkv, grad_gate, grad_up, total_m

    v_qkv, grad_gate, grad_up, total_m = unit_of_work(go, share, v_qkv, v_gu, w_gate, w_up, gain_m)
    grad_out = grad_out.astype(F32)
    grad_query, grad_key, grad_value, total = kernel_call(
        unpack_attention_kernel,
        tuple(shaped(*w.shape, dtype=F32) for w in (w_query, w_key, w_value)) + (shaped(1, rows, dtype=F32),),
    )((), v_qkv, w_query, w_key, w_value, gain)
    return (
        block_out.reshape(hidden_in.shape), grad_in.reshape(hidden_in.shape), total[0], grad_query, grad_key, grad_value,
        grad_out, total_m[0], grad_gate, grad_up, grad_down,
    )


def anywhere(
    hidden_in, lengths, span_order, attn_gain, w_query, w_key, w_value, w_out,
    mlp_gain, w_gate, w_up, w_down, out_grad,
):
    lay = Layout()
    micro, slots, width = hidden_in.shape
    rows, nz = w_query.shape[0], lay.nz
    gain = attn_gain.astype(F32)[:, None]
    gain_m = mlp_gain.astype(F32)[:, None]
    pos = jnp.concatenate([positions_of(span_order, k, slots) for k in range(lay.ctx)])
    usable = (positions_of(span_order, lay.c, slots)[None, :] < lengths[:, None]).astype(F32)[..., None]
    cosines, sines = rope_tables(pos)
    length = slots * lay.ctx

    def tokens(x):
        return lax.all_gather(x, "ctx", axis=1, tiled=True).reshape(micro * length, width)

    def own(x):
        x = x.astype(BF).reshape(micro, length, width)
        return lax.psum_scatter(x, "ctx", scatter_dimension=1, tiled=True).astype(F32)

    spread, collect = lay.spread, lay.gather_sum
    wqkv = spread(lay.exchange(pack_attention(w_query, w_key, w_value, gain)).reshape(KV * rows, -1))
    wgu = spread(lay.exchange(pack_mlp(w_gate, w_up, gain_m, nz)).reshape(KV * rows, -1))
    wout = spread(send(w_out, lay.place))
    wdown = spread(w_down)
    source = hidden_in.astype(F32)
    unit, inverse = unit_rows(source)
    xs = tokens(unit.astype(BF))
    g_res = out_grad.astype(F32) * usable
    g_mlp = tokens(g_res.astype(BF))
    pre = mm(xs, wqkv).reshape(micro, length, -1)
    attended, kept = attend(pre, pos, lengths, cosines, sines)
    att = attended.reshape(micro * length, QW)
    residual = source + own(mm(att, wout))
    unit_m, inverse_m = unit_rows(residual)
    xm = tokens(unit_m.astype(BF))
    gate_up = mm(xm, wgu)
    hidden = swiglu(gate_up)
    block_out = (usable * (residual + own(mm(hidden, wdown)))).astype(BF)
    grad_down = collect(mm_lt(hidden, g_mlp)).astype(F32)
    g_gu = swiglu_back(gate_up, mm_rt(g_mlp, wdown))
    v_gu = lay.exchange(collect(mm_lt(xm, g_gu)).reshape(KV, rows, -1))
    u_gate, u_up = unpack_mlp(v_gu, nz)
    g_res2 = g_res + unit_back(own(mm_rt(g_gu, wgu)), unit_m, inverse_m)
    g_branch = tokens(g_res2.astype(BF))
    grad_out = send(collect(mm_lt(att, g_branch)), lay.back).astype(F32)
    g_att = mm_rt(g_branch, wout).astype(BF).reshape(micro, length, QW)
    g_pre = attend_back(g_att, kept, cosines, sines).reshape(micro * length, -1)
    v_qkv = lay.exchange(collect(mm_lt(xs, g_pre)).reshape(KV, rows, -1))
    u_q, u_k, u_v = unpack_attention(v_qkv)
    grad_in = (g_res2 + unit_back(own(mm_rt(g_pre, wqkv)), unit, inverse)).astype(BF)
    return (
        block_out, grad_in, paired((w_query, u_q), (w_key, u_k), (w_value, u_v)),
        u_q * gain, u_k * gain, u_v * gain, grad_out,
        paired((w_gate, u_gate), (w_up, u_up)), u_gate * gain_m, u_up * gain_m, grad_down,
    )


def solution(mesh):
    rows = P(AXES, None)
    tokens = P("fsdp", "ctx", None)
    line = mesh.shape["ctx"] == 4 and mesh.shape["fsdp"] == 8
    return jax.shard_map(
        on_line if line else anywhere,
        mesh=mesh,
        in_specs=(tokens, P("fsdp"), P(), P(AXES), rows, rows, rows, rows, P(AXES), rows, rows, rows, tokens),
        out_specs=(tokens, tokens, P(AXES), rows, rows, rows, rows, P(AXES), rows, rows, rows),
        check_vma=False,
    )
```
